256 devices in a mesh: freq: 128 (over z, x, y_lo, core), tile: 2 (over y_hi).
Axes of the slice: x: 4, y: 4 (y_hi: 2, y_lo: 2; y = y_hi * 2 + y_lo), z: 8, core: 2. Of those that a mesh axis runs over, the one named last changes fastest.
Arguments:
- source_field: float32 [2, 128, 128, 1024], P(None, 'freq', 'tile'), may hold values from -6 to 6
- receiver_field: float32 [2, 128, 128, 1024], P(None, 'freq', 'tile'), may hold values from -6 to 6
- omegas: float32 [128], P('freq'), may hold values from 30 to 380
- velocity: float32 [256, 128, 1024], P('freq', 'tile'), may hold values from 1500 to 4500
- epsilon: float32 [256, 128, 1024], P('freq', 'tile'), may hold values from 0 to 0.3
- delta: float32 [256, 128, 1024], P('freq', 'tile'), may hold values from -0.1 to 0.2
- owner_map: int32 [256], replicated, may hold values from 0 to 255, each once
- stencil_reach: int32 [2], replicated, may hold values from 1 to 3, as said below
- source_rows: int32 [4], replicated, may hold values from 0 to 127
- source_cols: int32 [4], replicated, may hold values from 0 to 1023
Outputs:
- source_next: float32 [2, 128, 128, 1024], P(None, 'freq', 'tile')
- receiver_next: float32 [2, 128, 128, 1024], P(None, 'freq', 'tile')
- image: float32 [2, 128, 1024], P(None, 'tile')
The draws below stay inside these ranges and needn't reach their ends.
Inputs may be any that keep to these rules, and one draw needn't show every extreme that they name: `stencil_reach`: some step has half-width 3.
All inputs are finite; a program needn't handle non-finite values.
Results may differ from the reference program's by a relative error of at most 0.0002.
Values sent between devices are 32-bit elements; how exact they have to be, the bound alone decides.
A program may use at most 64 MiB of HBM per device.

```python
import math
import jax
import jax.numpy as jnp
from jax import lax

NY = 1024
STEPS = 2
HMAX = 3
SOURCES = 4
NX = 128
FREQS = 128
DEPTHS = 256


def draw_stencil_reach(key, part):
    key = jax.random.fold_in(key, 7)
    first_key, second_key = jax.random.split(key)
    widths = jax.random.randint(first_key, (STEPS,), 1, HMAX + 1)
    widest = jax.random.randint(second_key, (), 0, STEPS)
    return jnp.where(jnp.arange(STEPS) == widest, HMAX, widths).astype(jnp.int32)


def set_ends(entries, key, smallest, high):
    index_at = [jax.random.randint(jax.random.fold_in(key, axis), (), 0, length) for axis, length in enumerate(entries.shape)]
    longest = entries.shape.index(max(entries.shape))
    beside = index_at[:longest] + [(index_at[longest] + 1) % entries.shape[longest]] + index_at[longest + 1:]
    return entries.at[tuple(index_at)].set(smallest).at[tuple(beside)].set(high)


def block_scale(key, extent, pieces, least, largest):
    loudness, own = 1.0, jax.random.fold_in(key, 6)
    for position, parts in pieces:
        heights = jnp.exp(jax.random.uniform(jax.random.fold_in(own, position), (parts,), jnp.float32, least / len(pieces), largest / len(pieces)))
        loudness = loudness * jnp.repeat(heights, extent[position] // parts).reshape([-1 if axis == position else 1 for axis in range(len(extent))])
    return loudness


def normal_values(rng, dims, scale, bound, pieces=(), held_as=jnp.bfloat16):
    factor_of = block_scale(rng, dims, pieces, -0.22, 0.18) if pieces else 1.0
    result = jax.random.normal(rng, dims, jnp.float32) * scale * factor_of
    return jnp.minimum(jnp.maximum(result, -bound), bound).astype(held_as)


def setup_inputs(seed: int = 0) -> dict:
    key_list = jax.random.split(jax.random.key(seed), 11)
    return {
        "source_field": normal_values(key_list[0], (2, FREQS, NX, NY), 1.0, 6.0, ((1, 128), (2, 2)), jnp.float32),
        "receiver_field": normal_values(key_list[1], (2, FREQS, NX, NY), 1.0, 6.0, ((1, 128), (2, 2)), jnp.float32),
        "omegas": jnp.clip(jnp.exp(math.log(380.0) - 2.5389739 * jax.random.uniform(key_list[2], (FREQS,), jnp.float32) ** block_scale(key_list[2], (FREQS,), ((0, 128),), -0.2, 0.2)), 30.0, 380.0),
        "velocity": jnp.clip(1500.0 + 3000.0 * jax.random.uniform(key_list[3], (DEPTHS, NX, NY), jnp.float32) ** block_scale(key_list[3], (DEPTHS, NX, NY), ((0, 128), (1, 2)), -0.2, 0.2), 1500.0, 4500.0),
        "epsilon": jnp.clip(0.3 * jax.random.uniform(key_list[4], (DEPTHS, NX, NY), jnp.float32) ** block_scale(key_list[4], (DEPTHS, NX, NY), ((0, 128), (1, 2)), -0.2, 0.2), 0.0, 0.3),
        "delta": jnp.clip(-0.1 + 0.3 * jax.random.uniform(key_list[5], (DEPTHS, NX, NY), jnp.float32) ** block_scale(key_list[5], (DEPTHS, NX, NY), ((0, 128), (1, 2)), -0.2, 0.2), -0.1, 0.2),
        "owner_map": jax.random.permutation(key_list[6], DEPTHS).astype(jnp.int32),
        "stencil_reach": draw_stencil_reach(jax.random.fold_in(key_list[10], 71), 0),
        "source_rows": set_ends(jax.random.randint(key_list[8], (SOURCES,), 0, NX), jax.random.fold_in(key_list[8], 1), 0, NX - 1).astype(jnp.int32),
        "source_cols": set_ends(jax.random.randint(key_list[9], (SOURCES,), 0, NY), jax.random.fold_in(key_list[9], 1), 0, NY - 1).astype(jnp.int32),
    }


depth_step = 10.0
lateral_step = 10.0
source_delay = 0.05
source_amplitude = 16.0
image_gain = 16.0
taper_width = 4.0

def offset_groups(half_width):
    offsets_range = range(-half_width, half_width + 1)
    radii = sorted(set((down_shift * down_shift + side_shift * side_shift for down_shift in offsets_range for side_shift in offsets_range)))
    return [(radius, [(down_shift, side_shift) for down_shift in offsets_range for side_shift in offsets_range if down_shift * down_shift + side_shift * side_shift == radius]) for radius in radii]

def step_weights(reach_now, groups):
    tapers = jnp.array([math.exp(-radius / taper_width) for radius, members in groups], jnp.float32)
    counts = jnp.array([len(members) for radius, members in groups], jnp.float32)
    needed = jnp.array([max((max(abs(down_shift), abs(side_shift)) for down_shift, side_shift in members)) for radius, members in groups], jnp.int32)
    live_mask = (needed <= reach_now).astype(jnp.float32)
    normalizer = jnp.sum(tapers * counts * live_mask)
    return tapers * live_mask / normalizer

def inject(fields, omegas, source_spots):
    delay_phase = omegas * source_delay
    pulse_real = (source_amplitude * jnp.cos(delay_phase))[:, None, None] * source_spots[None]
    pulse_imag = (-source_amplitude * jnp.sin(delay_phase))[:, None, None] * source_spots[None]
    return jnp.concatenate([fields[0:1] + pulse_real[None], fields[1:2] + pulse_imag[None], fields[2:4]], axis=0)

def extrapolate(padded, omegas, planes, weights, groups):
    row_count = padded.shape[2] - 2 * HMAX
    col_count = padded.shape[3] - 2 * HMAX
    velocity_now, epsilon_now, delta_now = (planes[0], planes[1], planes[2])
    stretch = 1.0 / (1.0 + 2.0 * delta_now)
    slowness = 1.0 / velocity_now
    vert_wave = omegas[:, None, None] * (depth_step * slowness)[None]
    curvature = omegas[:, None, None] * (lateral_step * lateral_step / (2.0 * depth_step) * slowness * stretch)[None]
    eta_ratio = ((epsilon_now - delta_now) * stretch)[None]
    summed = jnp.zeros((4, padded.shape[1], row_count, col_count), jnp.float32)
    for group_index, (radius, members) in enumerate(groups):
        gathered = None
        for down_shift, side_shift in members:
            piece = padded[:, :, HMAX + down_shift:HMAX + down_shift + row_count, HMAX + side_shift:HMAX + side_shift + col_count]
            gathered = piece if gathered is None else gathered + piece
        phase_angle = vert_wave + curvature * radius * (1.0 - eta_ratio * (radius / 8.0))
        weight_real = weights[group_index] * jnp.cos(phase_angle)
        weight_imag = weights[group_index] * jnp.sin(phase_angle)
        summed = summed + jnp.stack([weight_real * gathered[0] - weight_imag * gathered[1], weight_real * gathered[1] + weight_imag * gathered[0], weight_real * gathered[2] + weight_imag * gathered[3], weight_real * gathered[3] - weight_imag * gathered[2]])
    return summed

def correlate(fields):
    return lax.optimization_barrier(jnp.sum(fields[0] * fields[2] + fields[1] * fields[3], axis=0))

def reference(source_field, receiver_field, omegas, velocity, epsilon, delta, owner_map, stencil_reach, source_rows, source_cols):
    groups = offset_groups(HMAX)
    row_hit = (source_rows[None, :] == jnp.arange(NX, dtype=jnp.int32)[:, None]).astype(jnp.float32)
    col_hit = (source_cols[:, None] == jnp.arange(NY, dtype=jnp.int32)[None, :]).astype(jnp.float32)
    source_spots = jnp.dot(row_hit, col_hit, precision=lax.Precision.HIGHEST, preferred_element_type=jnp.float32)
    plane_list = [jnp.stack([velocity[owner_map[depth_index]], epsilon[owner_map[depth_index]], delta[owner_map[depth_index]]]) for depth_index in range(STEPS)]
    weight_list = [step_weights(stencil_reach[depth_index], groups) for depth_index in range(STEPS)]

    def one_freq(image_sum, freq_item):
        source_now, receiver_now, omega_now = freq_item
        fields = jnp.concatenate([source_now[:, None], receiver_now[:, None]], axis=0)
        fields = inject(fields, omega_now[None], source_spots)
        image_terms = []
        for depth_index in range(STEPS):
            padded = jnp.pad(fields, ((0, 0), (0, 0), (HMAX, HMAX), (HMAX, HMAX)))
            fields = extrapolate(padded, omega_now[None], plane_list[depth_index], weight_list[depth_index], groups)
            image_terms.append(correlate(fields))
        return (image_sum + jnp.stack(image_terms), fields[:, 0])
    start = jnp.zeros((STEPS, NX, NY), jnp.float32)
    image_sum, finals = lax.scan(one_freq, start, (jnp.moveaxis(source_field, 1, 0), jnp.moveaxis(receiver_field, 1, 0), omegas))
    source_next = jnp.moveaxis(finals[:, 0:2], 0, 1)
    receiver_next = jnp.moveaxis(finals[:, 2:4], 0, 1)
    image = image_sum * (image_gain / math.sqrt(FREQS))
    return (source_next, receiver_next, image)
```

```python
import math

import jax
import jax.numpy as jnp
import numpy as np
from jax import lax
from jax.experimental import pallas as pl
from jax.experimental.pallas import tpu as pltpu
from jax.sharding import PartitionSpec as P

STEPS = 2
HMAX = 3
ROWS = 64
TALL = ROWS + 2 * HMAX
LANES = 128
GAIN = 16.0 / math.sqrt(128.0)
MESH = pl.DeviceIdType.MESH
F32 = jnp.float32


def _minimax(fn, high, degree, weight):
    count = 2000
    nodes = high / 2 + high / 2 * np.cos(np.pi * (np.arange(count) + 0.5) / count)
    target, scale = fn(nodes), weight(nodes)
    table = np.vander(nodes, degree + 1, increasing=True)
    bias = np.ones(count)
    best, least = None, np.inf
    for _ in range(60):
        coefs = np.linalg.lstsq(table * (bias * scale)[:, None], target * bias * scale, rcond=None)[0]
        error = np.abs((table @ coefs - target) * scale)
        if error.max() < least:
            best, least = coefs, error.max()
        bias = bias * (error / error.max() + 1e-3) ** 0.3
        bias = bias / bias.max()
    return tuple(float(np.float32(c)) for c in best)


REACH_SQ = 1.6 * 1.6
SIN = _minimax(lambda u: np.sin(np.sqrt(u)) / np.sqrt(u), REACH_SQ, 4, np.sqrt)
COS = _minimax(lambda u: np.cos(np.sqrt(u)), REACH_SQ, 4, np.ones_like)

GROUPS = sorted({a * a + b * b for a in range(4) for b in range(4)})
COUNTS = [
    sum(1 for a in range(-3, 4) for b in range(-3, 4) if a * a + b * b == r) for r in GROUPS
]
NEEDED = [
    max(max(a, b) for a in range(4) for b in range(4) if a * a + b * b == r) for r in GROUPS
]
TAPERS = [float(np.float32(math.exp(-r / 4.0))) for r in GROUPS]


def at(unit, count=1):
    return pl.ds(pl.multiple_of(unit * 8, 8), count * 8)


def horner(u, coefs):
    value = coefs[-1] * u + coefs[-2]
    for c in coefs[-3::-1]:
        value = value * u + c
    return value


def cis(x):
    u = x * x
    return horner(u, COS), x * horner(u, SIN)


def mul(a, b):
    return a[0] * b[0] - a[1] * b[1], a[0] * b[1] + a[1] * b[0]


def square(a):
    twice = a[1] + a[1]
    return 1.0 - a[1] * twice, a[0] * twice


def coords():
    f = lax.axis_index("freq")
    return f // 16, (f // 4) % 4, (f // 2) % 2, f % 2


def device(z, x, y, c):
    return {"freq": ((z * 4 + x) * 2 + y) * 2 + c}


def xy_peers():
    z, x, y, c = coords()
    out = []
    for k in range(1, 8):
        px, py = (x + k // 2) % 4, (y + k % 2) % 2
        out.append((device(z, px, py, c), px * 2 + py))
    return x * 2 + y, out


def z_peers():
    z, x, y, c = coords()
    return z, [(device((z + k) % 8, x, y, c), (z + k) % 8) for k in range(1, 8)]


def core_peer():
    z, x, y, c = coords()
    return device(z, x, y, 1 - c)


def all_peers():
    return [core_peer()] + [d for d, _ in xy_peers()[1]] + [d for d, _ in z_peers()[1]]


class Stream:
    SEMS = 30

    def __init__(self, src, res, base, units, order, bufs, sends, recvs):
        self.src, self.res, self.base, self.units = src, res, base, units
        self.core_in, self.half, self.in1, self.sum1, self.in2, self.out1 = bufs
        self.sends, self.recvs = sends, recvs
        self.groups = [xy_peers() if o == "xy" else z_peers() for o in order]
        self.core = coords()[3]
        self.started = []

    @staticmethod
    def scratch(units):
        def block(n):
            return pltpu.VMEM((n * 8, LANES), F32)

        return [
            block(units // 2),
            block(units // 2),
            block(7 * units // 16),
            block(units // 16),
            block(7 * units // 128),
            block(units // 16),
        ]

    def copy(self, slot, src, dst, to):
        made = pltpu.make_async_remote_copy(
            src_ref=src,
            dst_ref=dst,
            send_sem=self.sends.at[slot],
            recv_sem=self.recvs.at[slot],
            device_id=to,
            device_id_type=MESH,
        )
        made.start()
        self.started.append(made)
        return made

    def core_out(self):
        n = self.units // 2
        other = self.base + (1 - self.core) * n
        self.flying = [self.copy(0, self.src.at[at(other, n)], self.core_in, core_peer())]

    def land(self):
        for made in self.flying:
            made.wait_recv()

    def core_sum(self):
        n = self.units // 2
        mine = self.base + self.core * n

        def body(i, _):
            self.half[at(i * 4, 4)] = self.src[at(mine + i * 4, 4)] + self.core_in[at(i * 4, 4)]
            return 0

        lax.fori_loop(0, n // 4, body, 0)

    def scatter1(self):
        n = self.units // 16
        self.flying = [
            self.copy(1 + k, self.half.at[at(j * n, n)], self.in1.at[at(k * n, n)], to)
            for k, (to, j) in enumerate(self.groups[0][1])
        ]

    def sum1_(self):
        n = self.units // 16
        me = self.groups[0][0]

        def body(i, _):
            total = self.half[at(me * n + i)]
            for k in range(7):
                total = total + self.in1[at(k * n + i)]
            self.sum1[at(i)] = total
            return 0

        lax.fori_loop(0, n, body, 0)

    def scatter2(self):
        n = self.units // 128
        self.flying = [
            self.copy(8 + k, self.sum1.at[at(j * n, n)], self.in2.at[at(k * n, n)], to)
            for k, (to, j) in enumerate(self.groups[1][1])
        ]

    def sum2_(self):
        n = self.units // 128
        me = self.groups[1][0]
        for i in range(n):
            total = self.sum1[at(me * n + i)]
            for k in range(7):
                total = total + self.in2[at(k * n + i)]
            self.out1[at(me * n + i)] = total

    def gather2(self):
        n = self.units // 128
        me = self.groups[1][0]
        self.flying = [
            self.copy(15 + k, self.out1.at[at(me * n, n)], self.out1.at[at(me * n, n)], to)
            for k, (to, j) in enumerate(self.groups[1][1])
        ]

    def gather1(self):
        n = self.units // 16
        place = self.base + self.core * (self.units // 2) + self.groups[0][0] * n
        self.flying = [
            self.copy(22 + k, self.out1, self.res.at[at(place, n)], to)
            for k, (to, j) in enumerate(self.groups[0][1])
        ]

        def body(i, _):
            self.res[at(place + i)] = self.out1[at(i)]
            return 0

        lax.fori_loop(0, n, body, 0)

    def core_back(self):
        n = self.units // 2
        mine = self.base + self.core * n
        self.flying = [
            self.copy(29, self.res.at[at(mine, n)], self.res.at[at(mine, n)], core_peer())
        ]

    def finish(self):
        for made in self.started:
            made.wait_send()


def reduce_all(streams):
    for s in streams:
        s.core_out()
    for s in streams:
        s.land()
        s.core_sum()
        s.scatter1()
    for s in streams:
        s.land()
        s.sum1_()
        s.scatter2()
    for s in streams:
        s.land()
        s.sum2_()
        s.gather2()
    for s in streams:
        s.land()
        s.gather1()
    for s in streams:
        s.land()
        s.core_back()


def spread(field, pairs):
    def body(i, _):
        lane = lax.broadcasted_iota(jnp.int32, (8, LANES), 1)
        block = lax.broadcasted_iota(jnp.int32, (8, LANES), 0)
        for c in range(4):
            here = field[at(i * 4 + c)]
            above = jnp.where(block < 7, pltpu.roll(here, 7, 0), 0.0)
            below = jnp.where(block > 0, pltpu.roll(here, 1, 0), 0.0)
            for b in range(1, 4):
                plus = pltpu.roll(jnp.where(lane < b, above, here), LANES - b, 1)
                minus = pltpu.roll(jnp.where(lane >= LANES - b, below, here), b, 1)
                pairs[b - 1][at(i * 4 + c)] = plus + minus
        return 0

    return body


def weights_of(planes, step, x, omega):
    t, s = x // 8, x % 8

    def row(array):
        start = (step * 3 + array) * 512 + t * 64 + s
        return planes[pl.ds(start, 8, stride=8)]

    turn = cis((0.5 * omega) * row(0))
    turn = square(turn)
    q, a = omega * row(1), omega * row(2)
    z = cis(q)
    u = a * a
    w1 = (1.0 + u * (-0.5 + u * (1.0 / 24.0)), a * (u * (1.0 / 6.0) - 1.0))
    w2 = square(w1)
    w4 = square(w2)
    w8 = square(w4)
    w16 = square(w8)
    w32 = square(w16)
    w64 = square(w32)
    w128 = square(w64)
    g = {}
    g[1] = mul(z, w1)
    g[2] = mul(square(g[1]), w2)
    g[4] = mul(square(g[2]), w8)
    g[8] = mul(square(g[4]), w32)
    g[5] = mul(mul(g[4], w8), g[1])
    g[9] = mul(mul(g[8], w16), g[1])
    w34 = mul(w32, w2)
    g[10] = mul(square(g[5]), mul(w34, w16))
    g[13] = mul(mul(g[9], g[4]), mul(w64, w8))
    g[18] = mul(square(g[9]), mul(w34, w128))
    return turn, g


def one_row(field, pairs, planes, coef, step, x, omega):
    rows = [field] + list(pairs)

    def gathered(r, c):
        total = None
        for a in range(4):
            for b in range(4):
                if a * a + b * b != r:
                    continue
                for shift in sorted({a, -a}):
                    piece = rows[b][at((x + HMAX + shift) * 4 + c)]
                    total = piece if total is None else total + piece
        return total

    turn, g = weights_of(planes, step, x, omega)
    first = coef[at(step * 10)]
    acc = [first * gathered(0, c) for c in range(4)]
    for index, r in enumerate(GROUPS):
        if r == 0:
            continue
        scale = coef[at(step * 10 + index)]
        wr, wi = g[r][0] * scale, g[r][1] * scale
        sr, si, rr, ri = [gathered(r, c) for c in range(4)]
        acc[0] = acc[0] + (wr * sr - wi * si)
        acc[1] = acc[1] + (wr * si + wi * sr)
        acc[2] = acc[2] + (wr * rr + wi * ri)
        acc[3] = acc[3] + (wr * ri - wi * rr)
    tr, ti = turn
    return (
        tr * acc[0] - ti * acc[1],
        tr * acc[1] + ti * acc[0],
        tr * acc[2] + ti * acc[3],
        tr * acc[3] - ti * acc[2],
    )


PLANE_UNITS = STEPS * 3 * ROWS
IMAGE_UNITS = STEPS * ROWS


def kernel(
    omegas, owner, reach, srows, scols, source, receiver, velocity, epsilon, delta,
    source_out, receiver_out, image_out,
    raw_fields, raw_model, cand, planes, field0, field1, field2, pair1, pair2, pair3, coef, images,
    image_sum, image_nat, load_sems, halo_sends, halo_recvs, a_sends, a_recvs, b_sends, b_recvs,
    i_sends, i_recvs, *stream_bufs,
):
    tile = lax.axis_index("tile")
    index = lax.axis_index("freq")
    neighbour = {"tile": 1 - tile}
    omega = omegas[0]
    pairs = (pair1, pair2, pair3)

    loads = []
    for i, array in enumerate((velocity, epsilon, delta)):
        loads.append(pltpu.make_async_copy(array, raw_model.at[i], load_sems.at[i]))
    for i, array in enumerate((source, receiver)):
        loads.append(pltpu.make_async_copy(array, raw_fields.at[i], load_sems.at[3 + i]))
    for made in loads:
        made.start()

    barrier = pltpu.get_barrier_semaphore()
    greeted = all_peers() + [neighbour]
    for peer in greeted:
        pl.semaphore_signal(barrier, inc=1, device_id=peer, device_id_type=MESH)

    for made in loads[:3]:
        made.wait()
    picks = []
    for step in range(STEPS):
        for slot in range(2):
            hit = owner[step] == index * 2 + slot
            picks.append(jnp.full((8, LANES), jnp.where(hit, 1.0, 0.0), F32))

    def candidate(t, _):
        for k in range(8):
            place = (pl.ds(pl.multiple_of(t * 8, 8), 8), pl.ds(k * LANES, LANES))
            forms = []
            for slot in range(2):
                v = raw_model[(0, slot) + place]
                e = raw_model[(1, slot) + place]
                d = raw_model[(2, slot) + place]
                wide = 1.0 + 2.0 * d
                both = 1.0 / (v * wide)
                slowness = both * wide
                stretch = both * v
                curve = 5.0 * slowness * stretch
                forms.append((10.0 * slowness, curve, curve * ((e - d) * stretch * 0.125)))
            for step in range(STEPS):
                for n in range(3):
                    value = picks[step * 2] * forms[0][n] + picks[step * 2 + 1] * forms[1][n]
                    cand[at((step * 3 + n) * 64 + t * 8 + k)] = value
        return 0

    lax.fori_loop(0, 8, candidate, 0)
    pl.semaphore_wait(barrier, len(greeted))

    a_bufs, b_bufs, i_bufs = stream_bufs[0:6], stream_bufs[6:12], stream_bufs[12:18]
    a = Stream(cand, planes, 0, 256, ("xy", "z"), a_bufs, a_sends, a_recvs)
    b = Stream(cand, planes, 256, 128, ("z", "xy"), b_bufs, b_sends, b_recvs)
    for s in (a, b):
        s.core_out()

    for made in loads[3:]:
        made.wait()
    zero = jnp.zeros((8, LANES), F32)
    for field in (field0, field1):
        for i in range(HMAX * 4):
            field[at(67 * 4 * tile + i)] = zero
    delay = jnp.full((8, LANES), omega * 0.05, F32)
    pulse = (16.0 * jnp.cos(delay), -16.0 * jnp.sin(delay))

    def arrange(t, _):
        for c in range(4):
            for k in range(8):
                place = (pl.ds(pl.multiple_of(t * 8, 8), 8), pl.ds(k * LANES, LANES))
                value = raw_fields[(c // 2, c % 2, 0) + place]
                if c < 2:
                    row = lax.broadcasted_iota(jnp.int32, (8, LANES), 0) + (tile * ROWS + t * 8)
                    col = lax.broadcasted_iota(jnp.int32, (8, LANES), 1) + k * LANES
                    for s in range(4):
                        hit = (row == srows[s]) & (col == scols[s])
                        value = value + jnp.where(hit, pulse[c], 0.0)
                field0[pl.ds((t * 8 + HMAX) * 32 + c * 8 + k, 8, stride=32)] = value
        return 0

    def weights():
        for step in range(STEPS):
            live = [jnp.where(reach[step] >= n, t, 0.0) for n, t in zip(NEEDED, TAPERS)]
            total = live[0] * COUNTS[0]
            for n, w in zip(COUNTS[1:], live[1:]):
                total = total + w * n
            inverse = 1.0 / jnp.full((8, LANES), total, F32)
            for i, w in enumerate(live):
                coef[at(step * 10 + i)] = inverse * w

    def halo(field, slot):
        made = pltpu.make_async_remote_copy(
            src_ref=field.at[at((64 - 61 * tile) * 4, HMAX * 4)],
            dst_ref=field.at[at(67 * tile * 4, HMAX * 4)],
            send_sem=halo_sends.at[slot],
            recv_sem=halo_recvs.at[slot],
            device_id=neighbour,
            device_id_type=MESH,
        )
        made.start()
        return made

    for s in (a, b):
        s.land()
        s.core_sum()
        s.scatter1()
    lax.fori_loop(0, 8, arrange, 0)
    halo0 = halo(field0, 0)
    for s in (a, b):
        s.land()
        s.sum1_()
        s.scatter2()
    weights()
    lax.fori_loop(HMAX, HMAX + ROWS, spread(field0, pairs), 0)
    for s in (a, b):
        s.land()
        s.sum2_()
        s.gather2()
    halo0.wait()
    lax.fori_loop(0, HMAX, spread(field0, pairs), 0)
    lax.fori_loop(HMAX + ROWS, TALL, spread(field0, pairs), 0)
    for s in (a, b):
        s.land()
        s.gather1()
    for s in (a, b):
        s.land()
        s.core_back()
    for s in (a, b):
        s.land()

    def row_at(i):
        return (1 - tile) * (ROWS - 1) + (2 * tile - 1) * i

    def first_step(i, _):
        x = row_at(i)
        out = one_row(field0, pairs, planes, coef, 0, x, omega)
        for c in range(4):
            field1[at((x + HMAX) * 4 + c)] = out[c]
        images[at(x)] = out[0] * out[2] + out[1] * out[3]
        return 0

    lax.fori_loop(0, HMAX, first_step, 0)
    halo1 = halo(field1, 1)
    lax.fori_loop(HMAX, ROWS, first_step, 0)

    lax.fori_loop(HMAX, HMAX + ROWS, spread(field1, pairs), 0)
    halo1.wait()
    lax.fori_loop(0, HMAX, spread(field1, pairs), 0)
    lax.fori_loop(HMAX + ROWS, TALL, spread(field1, pairs), 0)

    def second_step(x, _):
        out = one_row(field1, pairs, planes, coef, 1, x, omega)
        for c in range(4):
            field2[at(x * 4 + c)] = out[c]
        images[at(ROWS + x)] = out[0] * out[2] + out[1] * out[3]
        return 0

    lax.fori_loop(0, ROWS, second_step, 0)

    i = Stream(images, image_sum, 0, IMAGE_UNITS, ("xy", "z"), i_bufs, i_sends, i_recvs)
    i.core_out()

    def restore(t, _):
        for c in range(4):
            for k in range(8):
                place = (pl.ds(pl.multiple_of(t * 8, 8), 8), pl.ds(k * LANES, LANES))
                raw_fields[(c // 2, c % 2, 0) + place] = field2[
                    pl.ds(t * 256 + c * 8 + k, 8, stride=32)
                ]
        return 0

    i.land()
    i.core_sum()
    i.scatter1()
    lax.fori_loop(0, 8, restore, 0)
    stores = [
        pltpu.make_async_copy(raw_fields.at[0], source_out, load_sems.at[3]),
        pltpu.make_async_copy(raw_fields.at[1], receiver_out, load_sems.at[4]),
    ]
    for made in stores:
        made.start()
    i.land()
    i.sum1_()
    i.scatter2()
    i.land()
    i.sum2_()
    i.gather2()
    i.land()
    i.gather1()
    i.land()
    i.core_back()
    i.land()

    def picture(t, _):
        for step in range(STEPS):
            for k in range(8):
                place = (pl.ds(pl.multiple_of(t * 8, 8), 8), pl.ds(k * LANES, LANES))
                value = image_sum[pl.ds(step * 512 + t * 64 + k, 8, stride=8)]
                image_nat[(step,) + place] = value * GAIN
        return 0

    lax.fori_loop(0, 8, picture, 0)
    last = pltpu.make_async_copy(image_nat, image_out, load_sems.at[0])
    last.start()
    for made in stores + [last]:
        made.wait()
    for s in (a, b, i):
        s.finish()


def per_device(*args):
    source, receiver, omegas, velocity, epsilon, delta, owner, reach, srows, scols = args
    smem = pl.BlockSpec(memory_space=pltpu.SMEM)
    hbm = pl.BlockSpec(memory_space=pl.ANY)

    def block(n):
        return pltpu.VMEM((n * 8, LANES), F32)

    sems = [pltpu.SemaphoreType.DMA((Stream.SEMS,))] * 6
    return pl.pallas_call(
        kernel,
        out_shape=(
            jax.ShapeDtypeStruct(source.shape, F32),
            jax.ShapeDtypeStruct(receiver.shape, F32),
            jax.ShapeDtypeStruct((STEPS, ROWS, 1024), F32),
        ),
        in_specs=[smem] * 5 + [hbm] * 5,
        out_specs=(hbm, hbm, hbm),
        scratch_shapes=[
            pltpu.VMEM((2, 2, 1, ROWS, 1024), F32),
            pltpu.VMEM((3, 2, ROWS, 1024), F32),
            block(PLANE_UNITS),
            block(PLANE_UNITS),
            block(TALL * 4),
            block(TALL * 4),
            block(ROWS * 4),
            block(TALL * 4),
            block(TALL * 4),
            block(TALL * 4),
            block(20),
            block(IMAGE_UNITS),
            block(IMAGE_UNITS),
            pltpu.VMEM((STEPS, ROWS, 1024), F32),
            pltpu.SemaphoreType.DMA((5,)),
            pltpu.SemaphoreType.DMA((2,)),
            pltpu.SemaphoreType.DMA((2,)),
        ]
        + sems
        + Stream.scratch(256)
        + Stream.scratch(128)
        + Stream.scratch(IMAGE_UNITS),
        compiler_params=pltpu.CompilerParams(
            collective_id=0, has_side_effects=True, vmem_limit_bytes=48 << 20
        ),
        name="migrate",
    )(omegas, owner, reach, srows, scols, source, receiver, velocity, epsilon, delta)


def solution(mesh):
    in_specs = (
        P(None, "freq", "tile", None),
        P(None, "freq", "tile", None),
        P("freq"),
        P("freq", "tile", None),
        P("freq", "tile", None),
        P("freq", "tile", None),
        P(),
        P(),
        P(),
        P(),
    )
    out_specs = (
        P(None, "freq", "tile", None),
        P(None, "freq", "tile", None),
        P(None, "tile", None),
    )
    return jax.shard_map(
        per_device, mesh=mesh, in_specs=in_specs, out_specs=out_specs, check_vma=False
    )
```

```python
import math

import jax
import jax.numpy as jnp
import numpy as np
from jax import lax
from jax.experimental import pallas as pl
from jax.experimental.pallas import tpu as pltpu
from jax.sharding import PartitionSpec as P

STEPS = 2
HMAX = 3
ROWS = 64
TALL = ROWS + 2 * HMAX
LANES = 128
GAIN = 16.0 / math.sqrt(128.0)
MESH = pl.DeviceIdType.MESH
F32 = jnp.float32


def _minimax(fn, high, degree, weight):
    count = 2000
    nodes = high / 2 + high / 2 * np.cos(np.pi * (np.arange(count) + 0.5) / count)
    target, scale = fn(nodes), weight(nodes)
    table = np.vander(nodes, degree + 1, increasing=True)
    bias = np.ones(count)
    best, least = None, np.inf
    for _ in range(60):
        coefs = np.linalg.lstsq(table * (bias * scale)[:, None], target * bias * scale, rcond=None)[0]
        error = np.abs((table @ coefs - target) * scale)
        if error.max() < least:
            best, least = coefs, error.max()
        bias = bias * (error / error.max() + 1e-3) ** 0.3
        bias = bias / bias.max()
    return tuple(float(np.float32(c)) for c in best)


REACH_SQ = 1.6 * 1.6
SIN = _minimax(lambda u: np.sin(np.sqrt(u)) / np.sqrt(u), REACH_SQ, 4, np.sqrt)
COS = _minimax(lambda u: np.cos(np.sqrt(u)), REACH_SQ, 4, np.ones_like)

GROUPS = sorted({a * a + b * b for a in range(4) for b in range(4)})
COUNTS = [
    sum(1 for a in range(-3, 4) for b in range(-3, 4) if a * a + b * b == r) for r in GROUPS
]
NEEDED = [
    max(max(a, b) for a in range(4) for b in range(4) if a * a + b * b == r) for r in GROUPS
]
TAPERS = [float(np.float32(math.exp(-r / 4.0))) for r in GROUPS]


def at(unit, count=1):
    return pl.ds(pl.multiple_of(unit * 8, 8), count * 8)


def horner(u, coefs):
    value = coefs[-1] * u + coefs[-2]
    for c in coefs[-3::-1]:
        value = value * u + c
    return value


def cis(x):
    u = x * x
    return horner(u, COS), x * horner(u, SIN)


def mul(a, b):
    return a[0] * b[0] - a[1] * b[1], a[0] * b[1] + a[1] * b[0]


def square(a):
    twice = a[1] + a[1]
    return 1.0 - a[1] * twice, a[0] * twice


def coords():
    f = lax.axis_index("freq")
    return f // 16, (f // 4) % 4, (f // 2) % 2, f % 2


def device(z, x, y, c):
    return {"freq": ((z * 4 + x) * 2 + y) * 2 + c}


def xy_peers():
    z, x, y, c = coords()
    out = []
    for k in range(1, 8):
        px, py = (x + k // 2) % 4, (y + k % 2) % 2
        out.append((device(z, px, py, c), px * 2 + py))
    return x * 2 + y, out


def z_peers():
    z, x, y, c = coords()
    return z, [(device((z + k) % 8, x, y, c), (z + k) % 8) for k in range(1, 8)]


def flat_peers():
    z, x, y, c = coords()
    out = []
    for k in range(1, 16):
        px, py, pc = (x + k // 4) % 4, (y + k // 2 % 2) % 2, (c + k % 2) % 2
        out.append((device(z, px, py, pc), px * 4 + py * 2 + pc))
    return x * 4 + y * 2 + c, out


def core_peer():
    z, x, y, c = coords()
    return device(z, x, y, 1 - c)


def all_peers():
    return [d for d, _ in flat_peers()[1]] + [d for d, _ in z_peers()[1]]


class Stream:
    SEMS = 30

    def __init__(self, src, res, base, units, order, bufs, sends, recvs):
        self.src, self.res, self.base, self.units = src, res, base, units
        self.core_in, self.half, self.in1, self.sum1, self.in2, self.out1 = bufs
        self.sends, self.recvs = sends, recvs
        self.groups = [xy_peers() if o == "xy" else z_peers() for o in order]
        self.core = coords()[3]
        self.started = []

    @staticmethod
    def scratch(units):
        def block(n):
            return pltpu.VMEM((n * 8, LANES), F32)

        return [
            block(units // 2),
            block(units // 2),
            block(7 * units // 16),
            block(units // 16),
            block(7 * units // 128),
            block(units // 16),
        ]

    def copy(self, slot, src, dst, to):
        made = pltpu.make_async_remote_copy(
            src_ref=src,
            dst_ref=dst,
            send_sem=self.sends.at[slot],
            recv_sem=self.recvs.at[slot],
            device_id=to,
            device_id_type=MESH,
        )
        made.start()
        self.started.append(made)
        return made

    def core_out(self):
        n = self.units // 2
        other = self.base + (1 - self.core) * n
        self.flying = [self.copy(0, self.src.at[at(other, n)], self.core_in, core_peer())]

    def land(self):
        for made in self.flying:
            made.wait_recv()

    def core_sum(self):
        n = self.units // 2
        mine = self.base + self.core * n

        def body(i, _):
            self.half[at(i * 4, 4)] = self.src[at(mine + i * 4, 4)] + self.core_in[at(i * 4, 4)]
            return 0

        lax.fori_loop(0, n // 4, body, 0)

    def scatter1(self):
        n = self.units // 16
        self.flying = [
            self.copy(1 + k, self.half.at[at(j * n, n)], self.in1.at[at(k * n, n)], to)
            for k, (to, j) in enumerate(self.groups[0][1])
        ]

    def sum1_(self):
        n = self.units // 16
        me = self.groups[0][0]

        def body(i, _):
            total = self.half[at(me * n + i)]
            for k in range(7):
                total = total + self.in1[at(k * n + i)]
            self.sum1[at(i)] = total
            return 0

        lax.fori_loop(0, n, body, 0)

    def scatter2(self):
        n = self.units // 128
        self.flying = [
            self.copy(8 + k, self.sum1.at[at(j * n, n)], self.in2.at[at(k * n, n)], to)
            for k, (to, j) in enumerate(self.groups[1][1])
        ]

    def sum2_(self):
        n = self.units // 128
        me = self.groups[1][0]
        for i in range(n):
            total = self.sum1[at(me * n + i)]
            for k in range(7):
                total = total + self.in2[at(k * n + i)]
            self.out1[at(me * n + i)] = total

    def gather2(self):
        n = self.units // 128
        me = self.groups[1][0]
        self.flying = [
            self.copy(15 + k, self.out1.at[at(me * n, n)], self.out1.at[at(me * n, n)], to)
            for k, (to, j) in enumerate(self.groups[1][1])
        ]

    def gather1(self):
        n = self.units // 16
        place = self.base + self.core * (self.units // 2) + self.groups[0][0] * n
        self.flying = [
            self.copy(22 + k, self.out1, self.res.at[at(place, n)], to)
            for k, (to, j) in enumerate(self.groups[0][1])
        ]

        def body(i, _):
            self.res[at(place + i)] = self.out1[at(i)]
            return 0

        lax.fori_loop(0, n, body, 0)

    def core_back(self):
        n = self.units // 2
        mine = self.base + self.core * n
        self.flying = [
            self.copy(29, self.res.at[at(mine, n)], self.res.at[at(mine, n)], core_peer())
        ]

    def finish(self):
        for made in self.started:
            made.wait_send()


class Relay:
    SEMS = 23

    def __init__(self, src, res, base, units, bufs, sends, recvs):
        self.src, self.res, self.base, self.units = src, res, base, units
        self.core_in, self.half, self.shares, self.stack, self.total = bufs
        self.sends, self.recvs = sends, recvs
        self.z, self.ring = z_peers()
        self.me, self.group = xy_peers()
        self.core = coords()[3]
        self.started = []

    @staticmethod
    def scratch(units):
        def block(n):
            return pltpu.VMEM((n * 8, LANES), F32)

        share = units // 16
        return [block(units // 2), block(units // 2), block(7 * share), block(8 * share), block(share)]

    copy = Stream.copy
    land = Stream.land
    finish = Stream.finish
    core_out = Stream.core_out
    core_sum = Stream.core_sum

    def scatter1(self):
        n = self.units // 16
        self.flying = [
            self.copy(1 + k, self.half.at[at(j * n, n)], self.shares.at[at(k * n, n)], to)
            for k, (to, j) in enumerate(self.ring)
        ]

    def exchange(self):
        n = self.units // 16
        total = self.half[at(self.z * n, n)]
        for k in range(7):
            total = total + self.shares[at(k * n, n)]
        mine = at(self.me * n, n)
        self.stack[mine] = total
        self.flying = [
            self.copy(8 + k, self.stack.at[mine], self.stack.at[mine], to)
            for k, (to, j) in enumerate(self.group)
        ]

    def gather(self):
        n = self.units // 16
        place = self.base + self.core * (self.units // 2) + self.z * n
        total = self.stack[at(0, n)]
        for k in range(1, 8):
            total = total + self.stack[at(k * n, n)]
        self.total[...] = total
        self.res[at(place, n)] = total
        self.flying = [
            self.copy(15 + k, self.total, self.res.at[at(place, n)], to)
            for k, (to, j) in enumerate(self.ring)
        ]

    def core_back(self):
        n = self.units // 2
        mine = at(self.base + self.core * n, n)
        self.flying = [self.copy(22, self.res.at[mine], self.res.at[mine], core_peer())]


class Picture:
    SEMS = 37
    SHARE = ROWS // 16

    def __init__(self, src, res, base, bufs, sends, recvs):
        self.src, self.res, self.base = src, res, base
        self.shares, self.stack, self.total = bufs
        self.sends, self.recvs = sends, recvs
        self.me, self.group = flat_peers()
        self.z, self.ring = z_peers()
        self.started = []

    @staticmethod
    def scratch():
        n = Picture.SHARE * 8
        return [
            pltpu.VMEM((15 * n, LANES), F32),
            pltpu.VMEM((8 * n, LANES), F32),
            pltpu.VMEM((n, LANES), F32),
        ]

    copy = Stream.copy
    land = Stream.land
    finish = Stream.finish

    def scatter(self):
        n = self.SHARE
        self.flying = [
            self.copy(k, self.src.at[at(self.base + j * n, n)], self.shares.at[at(k * n, n)], to)
            for k, (to, j) in enumerate(self.group)
        ]

    def exchange(self):
        n = self.SHARE
        for i in range(n):
            total = self.src[at(self.base + self.me * n + i)]
            for k in range(15):
                total = total + self.shares[at(k * n + i)]
            self.stack[at(self.z * n + i)] = total
        mine = at(self.z * n, n)
        self.flying = [
            self.copy(15 + k, self.stack.at[mine], self.stack.at[mine], to)
            for k, (to, j) in enumerate(self.ring)
        ]

    def gather(self):
        n = self.SHARE
        place = self.base + self.me * n
        for i in range(n):
            total = self.stack[at(i)]
            for k in range(1, 8):
                total = total + self.stack[at(k * n + i)]
            total = total * GAIN
            self.total[at(i)] = total
            self.res[at(place + i)] = total
        self.flying = [
            self.copy(22 + k, self.total, self.res.at[at(place, n)], to)
            for k, (to, j) in enumerate(self.group)
        ]


def spread(here):
    lane = lax.broadcasted_iota(jnp.int32, (8, LANES), 1)
    block = lax.broadcasted_iota(jnp.int32, (8, LANES), 0)
    above = jnp.where(block < 7, pltpu.roll(here, 7, 0), 0.0)
    below = jnp.where(block > 0, pltpu.roll(here, 1, 0), 0.0)
    out = []
    for b in range(1, 4):
        plus = pltpu.roll(jnp.where(lane < b, above, here), LANES - b, 1)
        minus = pltpu.roll(jnp.where(lane >= LANES - b, below, here), b, 1)
        out.append(plus + minus)
    return out


def spread_rows(field, pairs, first, count):
    def body(i, _):
        for c in range(4):
            for pair, value in zip(pairs, spread(field[c, at(first + i)])):
                pair[c, at(first + i)] = value
        return 0

    lax.fori_loop(0, count, body, 0, unroll=4 if count % 4 == 0 else 1)


def weights_of(planes, step, x, omega):
    t, s = x // 8, x % 8

    def row(array):
        start = (step * 3 + array) * 512 + t * 64 + s
        both = [planes[pl.ds(start + i, 8, stride=8)] for i in range(2)]
        return jnp.concatenate(both, axis=0)

    turn = cis((0.5 * omega) * row(0))
    turn = square(turn)
    q, a = omega * row(1), omega * row(2)
    z = cis(q)
    u = a * a
    w1 = (1.0 + u * (-0.5 + u * (1.0 / 24.0)), a * (u * (1.0 / 6.0) - 1.0))
    w2 = square(w1)
    w4 = square(w2)
    w8 = square(w4)
    w16 = square(w8)
    w32 = square(w16)
    w64 = square(w32)
    w128 = square(w64)
    g = {}
    g[1] = mul(z, w1)
    g[2] = mul(square(g[1]), w2)
    g[4] = mul(square(g[2]), w8)
    g[8] = mul(square(g[4]), w32)
    g[5] = mul(mul(g[4], w8), g[1])
    g[9] = mul(mul(g[8], w16), g[1])
    w34 = mul(w32, w2)
    g[10] = mul(square(g[5]), mul(w34, w16))
    g[13] = mul(mul(g[9], g[4]), mul(w64, w8))
    g[18] = mul(square(g[9]), mul(w34, w128))
    return turn, g


def two_rows(field, pairs, planes, coef, step, x, omega):
    rows = [field] + list(pairs)

    def gathered(r, c):
        total = None
        for a in range(4):
            for b in range(4):
                if a * a + b * b != r:
                    continue
                for shift in sorted({a, -a}):
                    piece = rows[b][c, at(x + HMAX + shift, 2)]
                    total = piece if total is None else total + piece
        return total

    turn, g = weights_of(planes, step, x, omega)
    first = coef[at(step * 20, 2)]
    acc = [first * gathered(0, c) for c in range(4)]
    for index, r in enumerate(GROUPS):
        if r == 0:
            continue
        scale = coef[at(step * 20 + index * 2, 2)]
        wr, wi = g[r][0] * scale, g[r][1] * scale
        sr, si, rr, ri = [gathered(r, c) for c in range(4)]
        acc[0] = acc[0] + (wr * sr - wi * si)
        acc[1] = acc[1] + (wr * si + wi * sr)
        acc[2] = acc[2] + (wr * rr + wi * ri)
        acc[3] = acc[3] + (wr * ri - wi * rr)
    tr, ti = turn
    return (
        tr * acc[0] - ti * acc[1],
        tr * acc[1] + ti * acc[0],
        tr * acc[2] + ti * acc[3],
        tr * acc[3] - ti * acc[2],
    )


PLANE_UNITS = STEPS * 3 * ROWS
IMAGE_UNITS = STEPS * ROWS


def kernel(
    omegas_in, owner_in, reach_in, srows_in, scols_in, source, receiver, velocity, epsilon, delta,
    source_out, receiver_out, image_out,
    omegas, owner, reach, srows, scols,
    raw_fields, raw_model, cand, planes, field0, field1, field2, pair1, pair2, pair3, next1, next2,
    next3, coef, images, image_sum, image_nat, load_sems, halo_sends, halo_recvs, *rest,
):
    sems, bufs = rest[:12], rest[12:]
    tile = lax.axis_index("tile")
    index = lax.axis_index("freq")
    neighbour = {"tile": 1 - tile}
    pairs, nexts = (pair1, pair2, pair3), (next1, next2, next3)

    loads = []
    for i, array in enumerate((velocity, epsilon, delta)):
        loads.append(pltpu.make_async_copy(array, raw_model.at[i], load_sems.at[i]))
    for i, array in enumerate((source, receiver)):
        loads.append(pltpu.make_async_copy(array, raw_fields.at[i], load_sems.at[3 + i]))
    smalls = ((omegas_in, omegas), (owner_in, owner), (reach_in, reach), (srows_in, srows), (scols_in, scols))
    for i, (array, place) in enumerate(smalls):
        loads.append(pltpu.make_async_copy(array, place, load_sems.at[5 + i]))
    for made in loads:
        made.start()

    barrier = pltpu.get_barrier_semaphore()
    greeted = all_peers() + [neighbour]
    for peer in greeted:
        pl.semaphore_signal(barrier, inc=1, device_id=peer, device_id_type=MESH)

    for made in loads[:3] + loads[5:]:
        made.wait()
    omega = omegas[0]
    picks = []
    for step in range(STEPS):
        for slot in range(2):
            hit = owner[step] == index * 2 + slot
            picks.append(jnp.full((8, LANES), jnp.where(hit, 1.0, 0.0), F32))

    def candidate(t, _):
        for k in range(8):
            place = (pl.ds(pl.multiple_of(t * 8, 8), 8), pl.ds(k * LANES, LANES))
            forms = []
            for slot in range(2):
                v = raw_model[(0, slot) + place]
                e = raw_model[(1, slot) + place]
                d = raw_model[(2, slot) + place]
                wide = 1.0 + 2.0 * d
                both = 1.0 / (v * wide)
                slowness = both * wide
                stretch = both * v
                curve = 5.0 * slowness * stretch
                forms.append((10.0 * slowness, curve, curve * ((e - d) * stretch * 0.125)))
            for step in range(STEPS):
                for n in range(3):
                    value = picks[step * 2] * forms[0][n] + picks[step * 2 + 1] * forms[1][n]
                    cand[at((step * 3 + n) * 64 + t * 8 + k)] = value
        return 0

    lax.fori_loop(0, 8, candidate, 0)
    pl.semaphore_wait(barrier, len(greeted))

    a0 = Stream(cand, planes, 0, 128, ("xy", "z"), bufs[0:6], sems[0], sems[1])
    a1 = Stream(cand, planes, 192, 128, ("xy", "z"), bufs[6:12], sems[2], sems[3])
    b0 = Relay(cand, planes, 128, 64, bufs[12:17], sems[4], sems[5])
    b1 = Relay(cand, planes, 320, 64, bufs[17:22], sems[6], sems[7])
    p0 = Picture(images, image_sum, 0, bufs[22:25], sems[8], sems[9])
    p1 = Picture(images, image_sum, ROWS, bufs[25:28], sems[10], sems[11])
    for s in (a0, b0, a1, b1):
        s.core_out()

    for made in loads[3:5]:
        made.wait()
    zero = jnp.zeros((8, LANES), F32)
    for field in (field0, field1) + pairs + nexts:
        for i in range(HMAX):
            for c in range(4):
                field[c, at(67 * tile + i)] = zero
    delay = jnp.full((8, LANES), omega * 0.05, F32)
    pulse = (16.0 * jnp.cos(delay), -16.0 * jnp.sin(delay))

    def arrange(t, _):
        for c in range(4):
            for k in range(8):
                place = (pl.ds(pl.multiple_of(t * 8, 8), 8), pl.ds(k * LANES, LANES))
                value = raw_fields[(c // 2, c % 2, 0) + place]
                if c < 2:
                    row = lax.broadcasted_iota(jnp.int32, (8, LANES), 0) + (tile * ROWS + t * 8)
                    col = lax.broadcasted_iota(jnp.int32, (8, LANES), 1) + k * LANES
                    for s in range(4):
                        hit = (row == srows[s]) & (col == scols[s])
                        value = value + jnp.where(hit, pulse[c], 0.0)
                field0[c, pl.ds((t * 8 + HMAX) * 8 + k, 8, stride=8)] = value
        return 0

    def weights():
        for step in range(STEPS):
            live = [jnp.where(reach[step] >= n, t, 0.0) for n, t in zip(NEEDED, TAPERS)]
            total = live[0] * COUNTS[0]
            for n, w in zip(COUNTS[1:], live[1:]):
                total = total + w * n
            inverse = 1.0 / jnp.full((8, LANES), total, F32)
            for i, w in enumerate(live):
                coef[at(step * 20 + i * 2)] = inverse * w
                coef[at(step * 20 + i * 2 + 1)] = inverse * w

    def halo(field, slot):
        made = pltpu.make_async_remote_copy(
            src_ref=field.at[:, at(64 - 61 * tile, HMAX)],
            dst_ref=field.at[:, at(67 * tile, HMAX)],
            send_sem=halo_sends.at[slot],
            recv_sem=halo_recvs.at[slot],
            device_id=neighbour,
            device_id_type=MESH,
        )
        made.start()
        return made

    for s in (a0, b0):
        s.land()
        s.core_sum()
        s.scatter1()
    lax.fori_loop(0, 8, arrange, 0)
    halo0 = halo(field0, 0)
    a0.land()
    a0.sum1_()
    a0.scatter2()
    b0.land()
    b0.exchange()
    for s in (a1, b1):
        s.land()
        s.core_sum()
        s.scatter1()
    weights()
    spread_rows(field0, pairs, HMAX, ROWS)
    halo0.wait()
    spread_rows(field0, pairs, 67 * (1 - tile), HMAX)
    a0.land()
    a0.sum2_()
    a0.gather2()
    b0.land()
    b0.gather()
    a1.land()
    a1.sum1_()
    a1.scatter2()
    b1.land()
    b1.exchange()
    a0.land()
    a0.gather1()
    b0.land()
    b0.core_back()
    a1.land()
    a1.sum2_()
    a1.gather2()
    b1.land()
    b1.gather()
    a0.land()
    a0.core_back()
    b0.land()
    a0.land()
    a1.land()
    a1.gather1()
    b1.land()
    b1.core_back()

    def first_step(i, _):
        x = (1 - tile) * (ROWS - 2) + (2 * tile - 1) * (i * 2)
        out = two_rows(field0, pairs, planes, coef, 0, x, omega)
        for c in range(4):
            field1[c, at(x + HMAX, 2)] = out[c]
            for h in range(2):
                for pair, value in zip(nexts, spread(out[c][h * 8 : h * 8 + 8])):
                    pair[c, at(x + HMAX + h)] = value
        images[at(x, 2)] = out[0] * out[2] + out[1] * out[3]
        return 0

    lax.fori_loop(0, 2, first_step, 0)
    halo1 = halo(field1, 1)
    lax.fori_loop(2, 20, first_step, 0)
    a1.land()
    a1.core_back()
    lax.fori_loop(20, ROWS // 2, first_step, 0)
    p0.scatter()
    halo1.wait()
    spread_rows(field1, nexts, 67 * (1 - tile), HMAX)
    a1.land()
    b1.land()

    def second_step(i, _):
        x = i * 2
        out = two_rows(field1, nexts, planes, coef, 1, x, omega)
        for c in range(4):
            field2[c, at(x, 2)] = out[c]
        images[at(ROWS + x, 2)] = out[0] * out[2] + out[1] * out[3]
        return 0

    lax.fori_loop(0, 28, second_step, 0)
    p0.land()
    p0.exchange()
    lax.fori_loop(28, ROWS // 2, second_step, 0)
    p1.scatter()

    def restore(t, _):
        for c in range(4):
            for k in range(8):
                place = (pl.ds(pl.multiple_of(t * 8, 8), 8), pl.ds(k * LANES, LANES))
                raw_fields[(c // 2, c % 2, 0) + place] = field2[
                    c, pl.ds(t * 64 + k, 8, stride=8)
                ]
        return 0

    lax.fori_loop(0, 8, restore, 0)
    stores = [
        pltpu.make_async_copy(raw_fields.at[0], source_out, load_sems.at[3]),
        pltpu.make_async_copy(raw_fields.at[1], receiver_out, load_sems.at[4]),
    ]
    for made in stores:
        made.start()
    p0.land()
    p0.gather()
    p1.land()
    p1.exchange()
    p1.land()
    p1.gather()
    p0.land()
    p1.land()

    def picture(t, _):
        for step in range(STEPS):
            for k in range(8):
                place = (pl.ds(pl.multiple_of(t * 8, 8), 8), pl.ds(k * LANES, LANES))
                value = image_sum[pl.ds(step * 512 + t * 64 + k, 8, stride=8)]
                image_nat[(step,) + place] = value
        return 0

    lax.fori_loop(0, 8, picture, 0)
    last = pltpu.make_async_copy(image_nat, image_out, load_sems.at[0])
    last.start()
    for made in stores + [last]:
        made.wait()
    for s in (a0, b0, a1, b1, p0, p1):
        s.finish()


def hand_over(*refs):
    between, sems = refs[6:9], refs[9]
    loads = [pltpu.make_async_copy(refs[i], between[i], sems.at[i]) for i in range(3)]
    stores = [pltpu.make_async_copy(between[i], refs[3 + i], sems.at[3 + i]) for i in range(3)]
    for made in loads:
        made.start()
    for load, store in zip(loads, stores):
        load.wait()
        store.start()
    for made in stores:
        made.wait()


def per_device(*args):
    source, receiver, omegas, velocity, epsilon, delta, owner, reach, srows, scols = args
    hbm = pl.BlockSpec(memory_space=pl.ANY)
    out_shape = (
        jax.ShapeDtypeStruct(source.shape, F32),
        jax.ShapeDtypeStruct(receiver.shape, F32),
        jax.ShapeDtypeStruct((STEPS, ROWS, 1024), F32),
    )

    def block(n):
        return pltpu.VMEM((n * 8, LANES), F32)

    def plane(n):
        return pltpu.VMEM((4, n * 8, LANES), F32)

    def small(array):
        return pltpu.SMEM(array.shape, array.dtype)

    counts = [Stream.SEMS] * 4 + [Relay.SEMS] * 4 + [Picture.SEMS] * 4
    made = pl.pallas_call(
        kernel,
        out_shape=out_shape,
        in_specs=[hbm] * 10,
        out_specs=(hbm, hbm, hbm),
        scratch_shapes=[small(array) for array in (omegas, owner, reach, srows, scols)]
        + [
            pltpu.VMEM((2, 2, 1, ROWS, 1024), F32),
            pltpu.VMEM((3, 2, ROWS, 1024), F32),
            block(PLANE_UNITS),
            block(PLANE_UNITS),
            plane(TALL),
            plane(TALL),
            plane(ROWS),
        ]
        + [plane(TALL)] * 6
        + [
            block(40),
            block(IMAGE_UNITS),
            block(IMAGE_UNITS),
            pltpu.VMEM((STEPS, ROWS, 1024), F32),
            pltpu.SemaphoreType.DMA((10,)),
            pltpu.SemaphoreType.DMA((2,)),
            pltpu.SemaphoreType.DMA((2,)),
        ]
        + [pltpu.SemaphoreType.DMA((n,)) for n in counts]
        + Stream.scratch(128) * 2
        + Relay.scratch(64) * 2
        + Picture.scratch() * 2,
        compiler_params=pltpu.CompilerParams(
            collective_id=0, has_side_effects=True, vmem_limit_bytes=52 << 20
        ),
        name="migrate",
    )(omegas, owner, reach, srows, scols, source, receiver, velocity, epsilon, delta)
    return pl.pallas_call(
        hand_over,
        out_shape=out_shape,
        in_specs=[hbm] * 3,
        out_specs=(hbm, hbm, hbm),
        scratch_shapes=[pltpu.VMEM(o.shape, F32) for o in out_shape]
        + [pltpu.SemaphoreType.DMA((6,))],
        compiler_params=pltpu.CompilerParams(vmem_limit_bytes=52 << 20),
        name="hand_over",
    )(*made)


def solution(mesh):
    in_specs = (
        P(None, "freq", "tile", None),
        P(None, "freq", "tile", None),
        P("freq"),
        P("freq", "tile", None),
        P("freq", "tile", None),
        P("freq", "tile", None),
        P(),
        P(),
        P(),
        P(),
    )
    out_specs = (
        P(None, "freq", "tile", None),
        P(None, "freq", "tile", None),
        P(None, "tile", None),
    )
    return jax.shard_map(
        per_device, mesh=mesh, in_specs=in_specs, out_specs=out_specs, check_vma=False
    )
```

```python
import math

import jax
import jax.numpy as jnp
import numpy as np
from jax import lax
from jax.experimental import pallas as pl
from jax.experimental.pallas import tpu as pltpu
from jax.sharding import PartitionSpec as P

STEPS = 2
HMAX = 3
ROWS = 64
TALL = ROWS + 2 * HMAX
LANES = 128
GAIN = 16.0 / math.sqrt(128.0)
MESH = pl.DeviceIdType.MESH
F32 = jnp.float32


def _minimax(fn, high, degree, weight):
    count = 2000
    nodes = high / 2 + high / 2 * np.cos(np.pi * (np.arange(count) + 0.5) / count)
    target, scale = fn(nodes), weight(nodes)
    table = np.vander(nodes, degree + 1, increasing=True)
    bias = np.ones(count)
    best, least = None, np.inf
    for _ in range(60):
        coefs = np.linalg.lstsq(table * (bias * scale)[:, None], target * bias * scale, rcond=None)[0]
        error = np.abs((table @ coefs - target) * scale)
        if error.max() < least:
            best, least = coefs, error.max()
        bias = bias * (error / error.max() + 1e-3) ** 0.3
        bias = bias / bias.max()
    return tuple(float(np.float32(c)) for c in best)


REACH_SQ = 1.6 * 1.6
SIN = _minimax(lambda u: np.sin(np.sqrt(u)) / np.sqrt(u), REACH_SQ, 4, np.sqrt)
COS = _minimax(lambda u: np.cos(np.sqrt(u)), REACH_SQ, 4, np.ones_like)

GROUPS = sorted({a * a + b * b for a in range(4) for b in range(4)})
COUNTS = [
    sum(1 for a in range(-3, 4) for b in range(-3, 4) if a * a + b * b == r) for r in GROUPS
]
NEEDED = [
    max(max(a, b) for a in range(4) for b in range(4) if a * a + b * b == r) for r in GROUPS
]
TAPERS = [float(np.float32(math.exp(-r / 4.0))) for r in GROUPS]


def at(unit, count=1):
    return pl.ds(pl.multiple_of(unit * 8, 8), count * 8)


def horner(u, coefs):
    value = coefs[-1] * u + coefs[-2]
    for c in coefs[-3::-1]:
        value = value * u + c
    return value


def cis(x):
    u = x * x
    return horner(u, COS), x * horner(u, SIN)


def mul(a, b):
    return a[0] * b[0] - a[1] * b[1], a[0] * b[1] + a[1] * b[0]


def square(a):
    twice = a[1] + a[1]
    return 1.0 - a[1] * twice, a[0] * twice


def coords():
    f = lax.axis_index("freq")
    return f // 16, (f // 4) % 4, (f // 2) % 2, f % 2


def device(z, x, y, c):
    return {"freq": ((z * 4 + x) * 2 + y) * 2 + c}


def xy_peers():
    z, x, y, c = coords()
    out = []
    for k in (5, 4, 3, 7, 2, 6, 1):
        px, py = (x + k // 2) % 4, (y + k % 2) % 2
        out.append((device(z, px, py, c), px * 2 + py))
    return x * 2 + y, out


def z_peers():
    z, x, y, c = coords()
    return z, [(device((z + k) % 8, x, y, c), (z + k) % 8) for k in (4, 3, 5, 2, 6, 1, 7)]


def flat_peers():
    z, x, y, c = coords()
    out = []
    for k in (10, 11, 8, 9, 6, 7, 14, 15, 4, 5, 12, 13, 2, 3, 1):
        px, py, pc = (x + k // 4) % 4, (y + k // 2 % 2) % 2, (c + k % 2) % 2
        out.append((device(z, px, py, pc), px * 4 + py * 2 + pc))
    return x * 4 + y * 2 + c, out


def core_peer():
    z, x, y, c = coords()
    return device(z, x, y, 1 - c)


def all_peers():
    return [d for d, _ in z_peers()[1]] + [d for d, _ in flat_peers()[1]]


class Stream:
    SEMS = 30

    def __init__(self, src, res, base, units, order, bufs, sends, recvs):
        self.src, self.res, self.base, self.units = src, res, base, units
        self.core_in, self.half, self.in1, self.sum1, self.in2, self.out1 = bufs
        self.sends, self.recvs = sends, recvs
        self.groups = [xy_peers() if o == "xy" else z_peers() for o in order]
        self.core = coords()[3]
        self.started = []

    @staticmethod
    def scratch(units):
        def block(n):
            return pltpu.VMEM((n * 8, LANES), F32)

        return [
            block(units // 2),
            block(units // 2),
            block(7 * units // 16),
            block(units // 16),
            block(7 * units // 128),
            block(units // 16),
        ]

    def copy(self, slot, src, dst, to):
        made = pltpu.make_async_remote_copy(
            src_ref=src,
            dst_ref=dst,
            send_sem=self.sends.at[slot],
            recv_sem=self.recvs.at[slot],
            device_id=to,
            device_id_type=MESH,
        )
        made.start()
        self.started.append(made)
        return made

    def core_out(self):
        n = self.units // 2
        other = self.base + (1 - self.core) * n
        self.flying = [self.copy(0, self.src.at[at(other, n)], self.core_in, core_peer())]

    def land(self):
        for made in self.flying:
            made.wait_recv()

    def core_sum(self):
        n = self.units // 2
        mine = self.base + self.core * n

        def body(i, _):
            self.half[at(i * 4, 4)] = self.src[at(mine + i * 4, 4)] + self.core_in[at(i * 4, 4)]
            return 0

        lax.fori_loop(0, n // 4, body, 0)

    def scatter1(self):
        n = self.units // 16
        self.flying = [
            self.copy(1 + k, self.half.at[at(j * n, n)], self.in1.at[at(k * n, n)], to)
            for k, (to, j) in enumerate(self.groups[0][1])
        ]

    def sum1_(self):
        n = self.units // 16
        me = self.groups[0][0]

        def body(i, _):
            total = self.half[at(me * n + i)]
            for k in range(7):
                total = total + self.in1[at(k * n + i)]
            self.sum1[at(i)] = total
            return 0

        lax.fori_loop(0, n, body, 0)

    def scatter2(self):
        n = self.units // 128
        self.flying = [
            self.copy(8 + k, self.sum1.at[at(j * n, n)], self.in2.at[at(k * n, n)], to)
            for k, (to, j) in enumerate(self.groups[1][1])
        ]

    def sum2_(self):
        n = self.units // 128
        me = self.groups[1][0]
        for i in range(n):
            total = self.sum1[at(me * n + i)]
            for k in range(7):
                total = total + self.in2[at(k * n + i)]
            self.out1[at(me * n + i)] = total

    def gather2(self):
        n = self.units // 128
        me = self.groups[1][0]
        self.flying = [
            self.copy(15 + k, self.out1.at[at(me * n, n)], self.out1.at[at(me * n, n)], to)
            for k, (to, j) in enumerate(self.groups[1][1])
        ]

    def gather1(self):
        n = self.units // 16
        place = self.base + self.core * (self.units // 2) + self.groups[0][0] * n
        self.flying = [
            self.copy(22 + k, self.out1, self.res.at[at(place, n)], to)
            for k, (to, j) in enumerate(self.groups[0][1])
        ]

        def body(i, _):
            self.res[at(place + i)] = self.out1[at(i)]
            return 0

        lax.fori_loop(0, n, body, 0)

    def core_back(self):
        n = self.units // 2
        mine = self.base + self.core * n
        self.flying = [
            self.copy(29, self.res.at[at(mine, n)], self.res.at[at(mine, n)], core_peer())
        ]

    def finish(self):
        for made in self.started:
            made.wait_send()
        self.started = []


class Relay:
    SEMS = 23

    def __init__(self, src, res, base, units, bufs, sends, recvs):
        self.src, self.res, self.base, self.units = src, res, base, units
        self.core_in, self.half, self.shares, self.stack, self.total = bufs
        self.sends, self.recvs = sends, recvs
        self.z, self.ring = z_peers()
        self.me, self.group = xy_peers()
        self.core = coords()[3]
        self.started = []

    @staticmethod
    def scratch(units):
        def block(n):
            return pltpu.VMEM((n * 8, LANES), F32)

        share = units // 16
        return [block(units // 2), block(units // 2), block(7 * share), block(8 * share), block(share)]

    copy = Stream.copy
    land = Stream.land
    finish = Stream.finish
    core_out = Stream.core_out
    core_sum = Stream.core_sum

    def scatter1(self):
        n = self.units // 16
        self.flying = [
            self.copy(1 + k, self.half.at[at(j * n, n)], self.shares.at[at(k * n, n)], to)
            for k, (to, j) in enumerate(self.ring)
        ]

    def exchange(self):
        n = self.units // 16
        total = self.half[at(self.z * n, n)]
        for k in range(7):
            total = total + self.shares[at(k * n, n)]
        mine = at(self.me * n, n)
        self.stack[mine] = total
        self.flying = [
            self.copy(8 + k, self.stack.at[mine], self.stack.at[mine], to)
            for k, (to, j) in enumerate(self.group)
        ]

    def gather(self):
        n = self.units // 16
        place = self.base + self.core * (self.units // 2) + self.z * n
        total = self.stack[at(0, n)]
        for k in range(1, 8):
            total = total + self.stack[at(k * n, n)]
        self.total[...] = total
        self.res[at(place, n)] = total
        self.flying = [
            self.copy(15 + k, self.total, self.res.at[at(place, n)], to)
            for k, (to, j) in enumerate(self.ring)
        ]

    def core_back(self):
        n = self.units // 2
        mine = at(self.base + self.core * n, n)
        self.flying = [self.copy(22, self.res.at[mine], self.res.at[mine], core_peer())]


class Picture:
    SEMS = 37
    SHARE = ROWS // 16

    def __init__(self, src, res, base, bufs, sends, recvs):
        self.src, self.res, self.base = src, res, base
        self.shares, self.stack, self.total = bufs
        self.sends, self.recvs = sends, recvs
        self.me, self.group = flat_peers()
        self.z, self.ring = z_peers()
        self.started = []

    @staticmethod
    def scratch():
        n = Picture.SHARE * 8
        return [
            pltpu.VMEM((15 * n, LANES), F32),
            pltpu.VMEM((8 * n, LANES), F32),
            pltpu.VMEM((n, LANES), F32),
        ]

    copy = Stream.copy
    land = Stream.land
    finish = Stream.finish

    def scatter(self):
        n = self.SHARE
        self.flying = [
            self.copy(k, self.src.at[at(self.base + j * n, n)], self.shares.at[at(k * n, n)], to)
            for k, (to, j) in enumerate(self.group)
        ]

    def exchange(self):
        n = self.SHARE
        for i in range(n):
            total = self.src[at(self.base + self.me * n + i)]
            for k in range(15):
                total = total + self.shares[at(k * n + i)]
            self.stack[at(self.z * n + i)] = total
        mine = at(self.z * n, n)
        self.flying = [
            self.copy(15 + k, self.stack.at[mine], self.stack.at[mine], to)
            for k, (to, j) in enumerate(self.ring)
        ]

    def gather(self):
        n = self.SHARE
        place = self.base + self.me * n
        for i in range(n):
            total = self.stack[at(i)]
            for k in range(1, 8):
                total = total + self.stack[at(k * n + i)]
            total = total * GAIN
            self.total[at(i)] = total
            self.res[at(place + i)] = total
        self.flying = [
            self.copy(22 + k, self.total, self.res.at[at(place, n)], to)
            for k, (to, j) in enumerate(self.group)
        ]


def spread(here):
    lane = lax.broadcasted_iota(jnp.int32, (8, LANES), 1)
    block = lax.broadcasted_iota(jnp.int32, (8, LANES), 0)
    above = jnp.where(block < 7, pltpu.roll(here, 7, 0), 0.0)
    below = jnp.where(block > 0, pltpu.roll(here, 1, 0), 0.0)
    out = []
    for b in range(1, 4):
        plus = pltpu.roll(jnp.where(lane < b, above, here), LANES - b, 1)
        minus = pltpu.roll(jnp.where(lane >= LANES - b, below, here), b, 1)
        out.append(plus + minus)
    return out


def spread_rows(field, pairs, first, count):
    def body(i, _):
        for c in range(4):
            for pair, value in zip(pairs, spread(field[c, at(first + i)])):
                pair[c, at(first + i)] = value
        return 0

    lax.fori_loop(0, count, body, 0, unroll=4 if count % 4 == 0 else 1)


def weights_of(planes, step, x, omega):
    t, s = x // 8, x % 8

    def row(array):
        start = (step * 3 + array) * 512 + t * 64 + s
        both = [planes[pl.ds(start + i, 8, stride=8)] for i in range(2)]
        return jnp.concatenate(both, axis=0)

    turn = cis((0.5 * omega) * row(0))
    turn = square(turn)
    q, a = omega * row(1), omega * row(2)
    z = cis(q)
    u = a * a
    w1 = (1.0 + u * (-0.5 + u * (1.0 / 24.0)), a * (u * (1.0 / 6.0) - 1.0))
    w2 = square(w1)
    w4 = square(w2)
    w8 = square(w4)
    w16 = square(w8)
    w32 = square(w16)
    w64 = square(w32)
    w128 = square(w64)
    g = {}
    g[1] = mul(z, w1)
    g[2] = mul(square(g[1]), w2)
    g[4] = mul(square(g[2]), w8)
    g[8] = mul(square(g[4]), w32)
    g[5] = mul(mul(g[4], w8), g[1])
    g[9] = mul(mul(g[8], w16), g[1])
    w34 = mul(w32, w2)
    g[10] = mul(square(g[5]), mul(w34, w16))
    g[13] = mul(mul(g[9], g[4]), mul(w64, w8))
    g[18] = mul(square(g[9]), mul(w34, w128))
    return turn, g


def two_rows(field, pairs, planes, coef, step, x, omega):
    rows = [field] + list(pairs)

    def gathered(r, c):
        total = None
        for a in range(4):
            for b in range(4):
                if a * a + b * b != r:
                    continue
                for shift in sorted({a, -a}):
                    piece = rows[b][c, at(x + HMAX + shift, 2)]
                    total = piece if total is None else total + piece
        return total

    turn, g = weights_of(planes, step, x, omega)
    first = coef[at(step * 20, 2)]
    acc = [first * gathered(0, c) for c in range(4)]
    for index, r in enumerate(GROUPS):
        if r == 0:
            continue
        scale = coef[at(step * 20 + index * 2, 2)]
        wr, wi = g[r][0] * scale, g[r][1] * scale
        sr, si, rr, ri = [gathered(r, c) for c in range(4)]
        acc[0] = acc[0] + (wr * sr - wi * si)
        acc[1] = acc[1] + (wr * si + wi * sr)
        acc[2] = acc[2] + (wr * rr + wi * ri)
        acc[3] = acc[3] + (wr * ri - wi * rr)
    tr, ti = turn
    return (
        tr * acc[0] - ti * acc[1],
        tr * acc[1] + ti * acc[0],
        tr * acc[2] + ti * acc[3],
        tr * acc[3] - ti * acc[2],
    )


PLANE_UNITS = STEPS * 3 * ROWS
IMAGE_UNITS = STEPS * ROWS


def kernel(
    omegas_in, owner_in, reach_in, srows_in, scols_in, source, receiver, velocity, epsilon, delta,
    source_out, receiver_out, image_out,
    omegas, owner, reach, srows, scols,
    raw_fields, raw_model, cand, planes, field0, field1, field2, pair1, pair2, pair3, next1, next2,
    next3, coef, images, image_sum, load_sems, halo_sends, halo_recvs, *rest,
):
    sems, bufs = rest[:12], rest[12:]
    tile = lax.axis_index("tile")
    index = lax.axis_index("freq")
    neighbour = {"tile": 1 - tile}
    pairs, nexts = (pair1, pair2, pair3), (next1, next2, next3)

    barrier = pltpu.get_barrier_semaphore()
    greeted = all_peers() + [neighbour]
    for peer in greeted:
        pl.semaphore_signal(barrier, inc=1, device_id=peer, device_id_type=MESH)

    loads = []
    for i, array in enumerate((velocity, epsilon, delta)):
        loads.append(pltpu.make_async_copy(array, raw_model.at[i], load_sems.at[i]))
    for i, array in enumerate((source, receiver)):
        loads.append(pltpu.make_async_copy(array, raw_fields.at[i], load_sems.at[3 + i]))
    smalls = ((omegas_in, omegas), (owner_in, owner), (reach_in, reach), (srows_in, srows), (scols_in, scols))
    for i, (array, place) in enumerate(smalls):
        loads.append(pltpu.make_async_copy(array, place, load_sems.at[5 + i]))
    for made in loads:
        made.start()

    for made in loads[:3] + loads[5:]:
        made.wait()
    omega = omegas[0]
    picks = []
    for step in range(STEPS):
        for slot in range(2):
            hit = owner[step] == index * 2 + slot
            picks.append(jnp.full((8, LANES), jnp.where(hit, 1.0, 0.0), F32))

    def candidate(t, _):
        for k in range(8):
            place = (pl.ds(pl.multiple_of(t * 8, 8), 8), pl.ds(k * LANES, LANES))
            forms = []
            for slot in range(2):
                v = raw_model[(0, slot) + place]
                e = raw_model[(1, slot) + place]
                d = raw_model[(2, slot) + place]
                wide = 1.0 + 2.0 * d
                both = 1.0 / (v * wide)
                slowness = both * wide
                stretch = both * v
                curve = 5.0 * slowness * stretch
                forms.append((10.0 * slowness, curve, curve * ((e - d) * stretch * 0.125)))
            for step in range(STEPS):
                for n in range(3):
                    value = picks[step * 2] * forms[0][n] + picks[step * 2 + 1] * forms[1][n]
                    cand[at((step * 3 + n) * 64 + t * 8 + k)] = value
        return 0

    lax.fori_loop(0, 8, candidate, 0)
    pl.semaphore_wait(barrier, len(greeted))

    a0 = Stream(cand, planes, 0, 128, ("xy", "z"), bufs[0:6], sems[0], sems[1])
    a1 = Stream(cand, planes, 192, 128, ("xy", "z"), bufs[6:12], sems[2], sems[3])
    b0 = Relay(cand, planes, 128, 64, bufs[12:17], sems[4], sems[5])
    b1 = Relay(cand, planes, 320, 64, bufs[17:22], sems[6], sems[7])
    p0 = Picture(images, image_sum, 0, bufs[22:25], sems[8], sems[9])
    p1 = Picture(images, image_sum, ROWS, bufs[25:28], sems[10], sems[11])
    for s in (a0, b0, a1, b1):
        s.core_out()

    for made in loads[3:5]:
        made.wait()
    zero = jnp.zeros((8, LANES), F32)
    for field in (field0, field1) + pairs + nexts:
        for i in range(HMAX):
            for c in range(4):
                field[c, at(67 * tile + i)] = zero
    delay = jnp.full((8, LANES), omega * 0.05, F32)
    pulse = (16.0 * jnp.cos(delay), -16.0 * jnp.sin(delay))

    def arrange(t, _):
        for c in range(4):
            for k in range(8):
                place = (pl.ds(pl.multiple_of(t * 8, 8), 8), pl.ds(k * LANES, LANES))
                value = raw_fields[(c // 2, c % 2, 0) + place]
                if c < 2:
                    row = lax.broadcasted_iota(jnp.int32, (8, LANES), 0) + (tile * ROWS + t * 8)
                    col = lax.broadcasted_iota(jnp.int32, (8, LANES), 1) + k * LANES
                    for s in range(4):
                        hit = (row == srows[s]) & (col == scols[s])
                        value = value + jnp.where(hit, pulse[c], 0.0)
                field0[c, pl.ds((t * 8 + HMAX) * 8 + k, 8, stride=8)] = value
        return 0

    def weights():
        for step in range(STEPS):
            live = [jnp.where(reach[step] >= n, t, 0.0) for n, t in zip(NEEDED, TAPERS)]
            total = live[0] * COUNTS[0]
            for n, w in zip(COUNTS[1:], live[1:]):
                total = total + w * n
            inverse = 1.0 / jnp.full((8, LANES), total, F32)
            for i, w in enumerate(live):
                coef[at(step * 20 + i * 2)] = inverse * w
                coef[at(step * 20 + i * 2 + 1)] = inverse * w

    def halo(field, slot):
        made = pltpu.make_async_remote_copy(
            src_ref=field.at[:, at(64 - 61 * tile, HMAX)],
            dst_ref=field.at[:, at(67 * tile, HMAX)],
            send_sem=halo_sends.at[slot],
            recv_sem=halo_recvs.at[slot],
            device_id=neighbour,
            device_id_type=MESH,
        )
        made.start()
        return made

    for s in (a0, b0):
        s.land()
        s.core_sum()
        s.scatter1()
    lax.fori_loop(0, 8, arrange, 0)
    halo0 = halo(field0, 0)
    a0.land()
    a0.sum1_()
    a0.scatter2()
    b0.land()
    b0.exchange()
    for s in (a1, b1):
        s.land()
        s.core_sum()
        s.scatter1()
    weights()
    spread_rows(field0, pairs, HMAX, ROWS)
    halo0.wait()
    spread_rows(field0, pairs, 67 * (1 - tile), HMAX)
    a0.land()
    a0.sum2_()
    a0.gather2()
    b0.land()
    b0.gather()
    a1.land()
    a1.sum1_()
    a1.scatter2()
    b1.land()
    b1.exchange()
    a0.land()
    a0.gather1()
    b0.land()
    b0.core_back()
    a1.land()
    a1.sum2_()
    a1.gather2()
    b1.land()
    b1.gather()
    a0.land()
    a0.core_back()
    b0.land()
    a0.land()
    a1.land()
    a1.gather1()
    b1.land()
    b1.core_back()

    def first_step(i, _):
        x = (1 - tile) * (ROWS - 2) + (2 * tile - 1) * (i * 2)
        out = two_rows(field0, pairs, planes, coef, 0, x, omega)
        for c in range(4):
            field1[c, at(x + HMAX, 2)] = out[c]
            for h in range(2):
                for pair, value in zip(nexts, spread(out[c][h * 8 : h * 8 + 8])):
                    pair[c, at(x + HMAX + h)] = value
        images[at(x, 2)] = out[0] * out[2] + out[1] * out[3]
        return 0

    lax.fori_loop(0, 2, first_step, 0)
    halo1 = halo(field1, 1)
    lax.fori_loop(2, 20, first_step, 0)
    a1.land()
    a1.core_back()
    lax.fori_loop(20, ROWS // 2, first_step, 0)
    p0.scatter()
    halo1.wait()
    spread_rows(field1, nexts, 67 * (1 - tile), HMAX)
    a1.land()
    b1.land()

    def second_step(i, _):
        x = i * 2
        out = two_rows(field1, nexts, planes, coef, 1, x, omega)
        for c in range(4):
            field2[c, at(x, 2)] = out[c]
        images[at(ROWS + x, 2)] = out[0] * out[2] + out[1] * out[3]
        return 0

    lax.fori_loop(0, ROWS // 2, second_step, 0)
    p1.scatter()
    p0.land()
    p0.exchange()

    def restore(t, _):
        for c in range(4):
            for k in range(8):
                place = (pl.ds(pl.multiple_of(t * 8, 8), 8), pl.ds(k * LANES, LANES))
                out = (source_out, receiver_out)[c // 2]
                out[(c % 2, 0) + place] = field2[
                    c, pl.ds(t * 64 + k, 8, stride=8)
                ]
        return 0

    lax.fori_loop(0, 8, restore, 0)
    for s in (a0, b0, a1, b1):
        s.finish()
    p0.land()
    p0.gather()
    p1.land()
    p1.exchange()
    p1.land()
    p1.gather()
    for s in (p0, p1):
        s.finish()
    p0.land()
    p1.land()

    def picture(t, _):
        for step in range(STEPS):
            for k in range(8):
                place = (pl.ds(pl.multiple_of(t * 8, 8), 8), pl.ds(k * LANES, LANES))
                value = image_sum[pl.ds(step * 512 + t * 64 + k, 8, stride=8)]
                image_out[(step,) + place] = value
        return 0

    lax.fori_loop(0, 8, picture, 0)


def hand_over(*refs):
    between, sems = refs[6:9], refs[9]
    loads = [pltpu.make_async_copy(refs[i], between[i], sems.at[i]) for i in range(3)]
    stores = [pltpu.make_async_copy(between[i], refs[3 + i], sems.at[3 + i]) for i in range(3)]
    for made in loads:
        made.start()
    for load, store in zip(loads, stores):
        load.wait()
        store.start()
    for made in stores:
        made.wait()


def per_device(*args):
    source, receiver, omegas, velocity, epsilon, delta, owner, reach, srows, scols = args
    hbm = pl.BlockSpec(memory_space=pl.ANY)
    out_shape = (
        jax.ShapeDtypeStruct(source.shape, F32),
        jax.ShapeDtypeStruct(receiver.shape, F32),
        jax.ShapeDtypeStruct((STEPS, ROWS, 1024), F32),
    )

    def block(n):
        return pltpu.VMEM((n * 8, LANES), F32)

    def plane(n):
        return pltpu.VMEM((4, n * 8, LANES), F32)

    def small(array):
        return pltpu.SMEM(array.shape, array.dtype)

    counts = [Stream.SEMS] * 4 + [Relay.SEMS] * 4 + [Picture.SEMS] * 4
    made = pl.pallas_call(
        kernel,
        out_shape=out_shape,
        in_specs=[hbm] * 10,
        out_specs=tuple([pl.BlockSpec(memory_space=pltpu.VMEM)] * 3),
        scratch_shapes=[small(array) for array in (omegas, owner, reach, srows, scols)]
        + [
            pltpu.VMEM((2, 2, 1, ROWS, 1024), F32),
            pltpu.VMEM((3, 2, ROWS, 1024), F32),
            block(PLANE_UNITS),
            block(PLANE_UNITS),
            plane(TALL),
            plane(TALL),
            plane(ROWS),
        ]
        + [plane(TALL)] * 6
        + [
            block(40),
            block(IMAGE_UNITS),
            block(IMAGE_UNITS),
            pltpu.SemaphoreType.DMA((10,)),
            pltpu.SemaphoreType.DMA((2,)),
            pltpu.SemaphoreType.DMA((2,)),
        ]
        + [pltpu.SemaphoreType.DMA((n,)) for n in counts]
        + Stream.scratch(128) * 2
        + Relay.scratch(64) * 2
        + Picture.scratch() * 2,
        compiler_params=pltpu.CompilerParams(
            collective_id=0, has_side_effects=True, vmem_limit_bytes=52 << 20
        ),
        name="migrate",
    )(omegas, owner, reach, srows, scols, source, receiver, velocity, epsilon, delta)
    return pl.pallas_call(
        hand_over,
        out_shape=out_shape,
        in_specs=[hbm] * 3,
        out_specs=(hbm, hbm, hbm),
        scratch_shapes=[pltpu.VMEM(o.shape, F32) for o in out_shape]
        + [pltpu.SemaphoreType.DMA((6,))],
        compiler_params=pltpu.CompilerParams(vmem_limit_bytes=52 << 20),
        name="hand_over",
    )(*made)


def solution(mesh):
    in_specs = (
        P(None, "freq", "tile", None),
        P(None, "freq", "tile", None),
        P("freq"),
        P("freq", "tile", None),
        P("freq", "tile", None),
        P("freq", "tile", None),
        P(),
        P(),
        P(),
        P(),
    )
    out_specs = (
        P(None, "freq", "tile", None),
        P(None, "freq", "tile", None),
        P(None, "tile", None),
    )
    return jax.shard_map(
        per_device, mesh=mesh, in_specs=in_specs, out_specs=out_specs, check_vma=False
    )
```

```python
import math

import jax
import jax.numpy as jnp
import numpy as np
from jax import lax
from jax.experimental import pallas as pl
from jax.experimental.pallas import tpu as pltpu
from jax.sharding import PartitionSpec as P

STEPS = 2
HMAX = 3
ROWS = 64
TALL = ROWS + 2 * HMAX
LANES = 128
GAIN = 16.0 / math.sqrt(128.0)
MESH = pl.DeviceIdType.MESH
F32 = jnp.float32


def _minimax(fn, high, degree, weight):
    count = 2000
    nodes = high / 2 + high / 2 * np.cos(np.pi * (np.arange(count) + 0.5) / count)
    target, scale = fn(nodes), weight(nodes)
    table = np.vander(nodes, degree + 1, increasing=True)
    bias = np.ones(count)
    best, least = None, np.inf
    for _ in range(60):
        coefs = np.linalg.lstsq(table * (bias * scale)[:, None], target * bias * scale, rcond=None)[0]
        error = np.abs((table @ coefs - target) * scale)
        if error.max() < least:
            best, least = coefs, error.max()
        bias = bias * (error / error.max() + 1e-3) ** 0.3
        bias = bias / bias.max()
    return tuple(float(np.float32(c)) for c in best)


REACH_SQ = 1.6 * 1.6
SIN = _minimax(lambda u: np.sin(np.sqrt(u)) / np.sqrt(u), REACH_SQ, 4, np.sqrt)
COS = _minimax(lambda u: np.cos(np.sqrt(u)), REACH_SQ, 4, np.ones_like)

GROUPS = sorted({a * a + b * b for a in range(4) for b in range(4)})
COUNTS = [
    sum(1 for a in range(-3, 4) for b in range(-3, 4) if a * a + b * b == r) for r in GROUPS
]
NEEDED = [
    max(max(a, b) for a in range(4) for b in range(4) if a * a + b * b == r) for r in GROUPS
]
TAPERS = [float(np.float32(math.exp(-r / 4.0))) for r in GROUPS]


def at(unit, count=1):
    return pl.ds(pl.multiple_of(unit * 8, 8), count * 8)


def horner(u, coefs):
    value = coefs[-1] * u + coefs[-2]
    for c in coefs[-3::-1]:
        value = value * u + c
    return value


def cis(x):
    u = x * x
    return horner(u, COS), x * horner(u, SIN)


def mul(a, b):
    return a[0] * b[0] - a[1] * b[1], a[0] * b[1] + a[1] * b[0]


def square(a):
    twice = a[1] + a[1]
    return 1.0 - a[1] * twice, a[0] * twice


def coords():
    f = lax.axis_index("freq")
    return lax.div(f, 16), lax.rem(lax.div(f, 4), 4), lax.rem(lax.div(f, 2), 2), lax.rem(f, 2)


def device(z, x, y, c):
    return {"freq": ((z * 4 + x) * 2 + y) * 2 + c}


def xy_peers():
    z, x, y, c = coords()
    out = []
    for k in (5, 4, 3, 7, 2, 6, 1):
        px, py = lax.rem(x + k // 2, 4), lax.rem(y + k % 2, 2)
        out.append((device(z, px, py, c), px * 2 + py))
    return x * 2 + y, out


def z_peers():
    z, x, y, c = coords()
    return z, [(device(lax.rem(z + k, 8), x, y, c), lax.rem(z + k, 8)) for k in (4, 3, 5, 2, 6, 1, 7)]


def flat_peers():
    z, x, y, c = coords()
    out = []
    for k in (10, 11, 8, 9, 6, 7, 14, 15, 4, 5, 12, 13, 2, 3, 1):
        px, py, pc = lax.rem(x + k // 4, 4), lax.rem(y + k // 2 % 2, 2), lax.rem(c + k % 2, 2)
        out.append((device(z, px, py, pc), px * 4 + py * 2 + pc))
    return x * 4 + y * 2 + c, out


def core_peer():
    z, x, y, c = coords()
    return device(z, x, y, 1 - c)


def all_peers():
    return [d for d, _ in z_peers()[1]] + [d for d, _ in flat_peers()[1]]


class Stream:
    SEMS = 6

    def __init__(self, src, res, base, units, order, bufs, sends, recvs):
        self.src, self.res, self.base, self.units = src, res, base, units
        self.core_in, self.half, self.in1, self.sum1, self.in2, self.out1 = bufs
        self.sends, self.recvs = sends, recvs
        self.groups = [xy_peers() if o == "xy" else z_peers() for o in order]
        self.core = coords()[3]
        self.done = 0

    @staticmethod
    def scratch(units):
        def block(n):
            return pltpu.VMEM((n * 8, LANES), F32)

        return [
            block(units // 2),
            block(units // 2),
            block(7 * units // 16),
            block(units // 16),
            block(7 * units // 128),
            block(units // 16),
        ]

    def send(self, phase, parts):
        for src, dst, to in parts:
            pltpu.make_async_remote_copy(
                src_ref=src,
                dst_ref=dst,
                send_sem=self.sends.at[phase],
                recv_sem=self.recvs.at[phase],
                device_id=to,
                device_id_type=MESH,
            ).start()
        self.phase = phase

    def land(self):
        whole = self.whole(self.phase)
        pltpu.make_async_copy(whole, whole, self.recvs.at[self.phase]).wait()

    def finish(self):
        for phase in range(self.done, self.phase + 1):
            whole = self.whole(phase)
            pltpu.make_async_copy(whole, whole, self.sends.at[phase]).wait()
        self.done = self.phase + 1

    def core_out(self):
        n = self.units // 2
        other = self.base + (1 - self.core) * n
        self.send(0, [(self.src.at[at(other, n)], self.core_in, core_peer())])

    def core_sum(self):
        n = self.units // 2
        mine = self.base + self.core * n

        def body(i, _):
            self.half[at(i * 16, 16)] = self.src[at(mine + i * 16, 16)] + self.core_in[at(i * 16, 16)]
            return 0

        lax.fori_loop(0, n // 16, body, 0)

    def scatter1(self):
        n = self.units // 16
        self.send(1, [
            (self.half.at[at(j * n, n)], self.in1.at[at(k * n, n)], to)
            for k, (to, j) in enumerate(self.groups[0][1])
        ])

    def sum1_(self):
        n = self.units // 16
        me = self.groups[0][0]

        total = self.half[at(me * n, n)]
        for k in range(7):
            total = total + self.in1[at(k * n, n)]
        self.sum1[...] = total

    def scatter2(self):
        n = self.units // 128
        self.send(2, [
            (self.sum1.at[at(j * n, n)], self.in2.at[at(k * n, n)], to)
            for k, (to, j) in enumerate(self.groups[1][1])
        ])

    def sum2_(self):
        n = self.units // 128
        me = self.groups[1][0]
        for i in range(n):
            total = self.sum1[at(me * n + i)]
            for k in range(7):
                total = total + self.in2[at(k * n + i)]
            self.out1[at(me * n + i)] = total

    def gather2(self):
        n = self.units // 128
        me = self.groups[1][0]
        mine = at(me * n, n)
        self.send(3, [(self.out1.at[mine], self.out1.at[mine], to) for to, j in self.groups[1][1]])

    def gather1(self):
        n = self.units // 16
        place = self.base + self.core * (self.units // 2) + self.groups[0][0] * n
        self.send(4, [(self.out1, self.res.at[at(place, n)], to) for to, j in self.groups[0][1]])
        self.res[at(place, n)] = self.out1[...]

    def core_back(self):
        n = self.units // 2
        mine = self.base + self.core * n
        self.send(5, [(self.res.at[at(mine, n)], self.res.at[at(mine, n)], core_peer())])

    def whole(self, phase):
        first, second = self.units // 16, self.units // 128
        if phase == 0:
            return self.core_in
        if phase == 5:
            return self.res.at[at(self.base, self.units // 2)]
        return (self.in1, self.in2, self.out1.at[at(0, 7 * second)], self.res.at[at(self.base, 7 * first)])[phase - 1]


class Relay:
    SEMS = 5

    def __init__(self, src, res, base, units, bufs, sends, recvs):
        self.src, self.res, self.base, self.units = src, res, base, units
        self.core_in, self.half, self.shares, self.stack, self.total = bufs
        self.sends, self.recvs = sends, recvs
        self.z, self.ring = z_peers()
        self.me, self.group = xy_peers()
        self.core = coords()[3]
        self.done = 0

    @staticmethod
    def scratch(units):
        def block(n):
            return pltpu.VMEM((n * 8, LANES), F32)

        share = units // 16
        return [block(units // 2), block(units // 2), block(7 * share), block(8 * share), block(share)]

    send = Stream.send
    land = Stream.land
    finish = Stream.finish
    core_out = Stream.core_out
    core_sum = Stream.core_sum

    def scatter1(self):
        n = self.units // 16
        self.send(1, [
            (self.half.at[at(j * n, n)], self.shares.at[at(k * n, n)], to)
            for k, (to, j) in enumerate(self.ring)
        ])

    def exchange(self):
        n = self.units // 16
        total = self.half[at(self.z * n, n)]
        for k in range(7):
            total = total + self.shares[at(k * n, n)]
        mine = at(self.me * n, n)
        self.stack[mine] = total
        self.send(2, [(self.stack.at[mine], self.stack.at[mine], to) for to, j in self.group])

    def gather(self):
        n = self.units // 16
        place = self.base + self.core * (self.units // 2) + self.z * n
        total = self.stack[at(0, n)]
        for k in range(1, 8):
            total = total + self.stack[at(k * n, n)]
        self.total[...] = total
        self.res[at(place, n)] = total
        self.send(3, [(self.total, self.res.at[at(place, n)], to) for to, j in self.ring])

    def core_back(self):
        n = self.units // 2
        mine = at(self.base + self.core * n, n)
        self.send(4, [(self.res.at[mine], self.res.at[mine], core_peer())])

    def whole(self, phase):
        share = self.units // 16
        if phase == 0:
            return self.core_in
        if phase == 4:
            return self.res.at[at(self.base, self.units // 2)]
        return (self.shares, self.stack.at[at(0, 7 * share)], self.res.at[at(self.base, 7 * share)])[phase - 1]


class Picture:
    SEMS = 3
    SHARE = ROWS // 16

    def __init__(self, src, res, base, bufs, sends, recvs):
        self.src, self.res, self.base = src, res, base
        self.shares, self.stack, self.total = bufs
        self.sends, self.recvs = sends, recvs
        self.me, self.group = flat_peers()
        self.z, self.ring = z_peers()
        self.done = 0

    @staticmethod
    def scratch():
        n = Picture.SHARE * 8
        return [
            pltpu.VMEM((15 * n, LANES), F32),
            pltpu.VMEM((8 * n, LANES), F32),
            pltpu.VMEM((n, LANES), F32),
        ]

    send = Stream.send
    land = Stream.land
    finish = Stream.finish

    def scatter(self):
        n = self.SHARE
        self.send(0, [
            (self.src.at[at(self.base + j * n, n)], self.shares.at[at(k * n, n)], to)
            for k, (to, j) in enumerate(self.group)
        ])

    def exchange(self):
        n = self.SHARE
        for i in range(n):
            total = self.src[at(self.base + self.me * n + i)]
            for k in range(15):
                total = total + self.shares[at(k * n + i)]
            self.stack[at(self.z * n + i)] = total
        mine = at(self.z * n, n)
        self.send(1, [(self.stack.at[mine], self.stack.at[mine], to) for to, j in self.ring])

    def gather(self):
        n = self.SHARE
        place = self.base + self.me * n
        for i in range(n):
            total = self.stack[at(i)]
            for k in range(1, 8):
                total = total + self.stack[at(k * n + i)]
            total = total * GAIN
            self.total[at(i)] = total
            self.res[at(place + i)] = total
        self.send(2, [(self.total, self.res.at[at(place, n)], to) for to, j in self.group])

    def whole(self, phase):
        n = self.SHARE
        return (self.shares, self.stack.at[at(0, 7 * n)], self.res.at[at(self.base, 15 * n)])[phase]


def spread(here):
    lane = lax.broadcasted_iota(jnp.int32, (8, LANES), 1)
    block = lax.broadcasted_iota(jnp.int32, (8, LANES), 0)
    above = jnp.where(block < 7, pltpu.roll(here, 7, 0), 0.0)
    below = jnp.where(block > 0, pltpu.roll(here, 1, 0), 0.0)
    out = []
    for b in range(1, 4):
        plus = pltpu.roll(jnp.where(lane < b, above, here), LANES - b, 1)
        minus = pltpu.roll(jnp.where(lane >= LANES - b, below, here), b, 1)
        out.append(plus + minus)
    return out


def spread_rows(field, pairs, first, count):
    def body(i, _):
        for c in range(4):
            for pair, value in zip(pairs, spread(field[c, at(first + i)])):
                pair[c, at(first + i)] = value
        return 0

    lax.fori_loop(0, count, body, 0, unroll=4 if count % 4 == 0 else 1)


def weights_of(planes, step, x, omega):
    t, s = x // 8, x % 8

    def row(array):
        start = (step * 3 + array) * 512 + t * 64 + s
        both = [planes[pl.ds(start + i, 8, stride=8)] for i in range(2)]
        return jnp.concatenate(both, axis=0)

    turn = cis((0.5 * omega) * row(0))
    turn = square(turn)
    q, a = omega * row(1), omega * row(2)
    z = cis(q)
    u = a * a
    w1 = (1.0 + u * (-0.5 + u * (1.0 / 24.0)), a * (u * (1.0 / 6.0) - 1.0))
    w2 = square(w1)
    w4 = square(w2)
    w8 = square(w4)
    w16 = square(w8)
    w32 = square(w16)
    w64 = square(w32)
    w128 = square(w64)
    g = {}
    g[1] = mul(z, w1)
    g[2] = mul(square(g[1]), w2)
    g[4] = mul(square(g[2]), w8)
    g[8] = mul(square(g[4]), w32)
    g[5] = mul(mul(g[4], w8), g[1])
    g[9] = mul(mul(g[8], w16), g[1])
    w34 = mul(w32, w2)
    g[10] = mul(square(g[5]), mul(w34, w16))
    g[13] = mul(mul(g[9], g[4]), mul(w64, w8))
    g[18] = mul(square(g[9]), mul(w34, w128))
    return turn, g


def two_rows(field, pairs, planes, coef, step, x, omega):
    rows = [field] + list(pairs)

    def gathered(r, c):
        total = None
        for a in range(4):
            for b in range(4):
                if a * a + b * b != r:
                    continue
                for shift in sorted({a, -a}):
                    piece = rows[b][c, at(x + HMAX + shift, 2)]
                    total = piece if total is None else total + piece
        return total

    turn, g = weights_of(planes, step, x, omega)
    first = coef[at(step * 20, 2)]
    acc = [first * gathered(0, c) for c in range(4)]
    for index, r in enumerate(GROUPS):
        if r == 0:
            continue
        scale = coef[at(step * 20 + index * 2, 2)]
        wr, wi = g[r][0] * scale, g[r][1] * scale
        sr, si, rr, ri = [gathered(r, c) for c in range(4)]
        acc[0] = acc[0] + (wr * sr - wi * si)
        acc[1] = acc[1] + (wr * si + wi * sr)
        acc[2] = acc[2] + (wr * rr + wi * ri)
        acc[3] = acc[3] + (wr * ri - wi * rr)
    tr, ti = turn
    return (
        tr * acc[0] - ti * acc[1],
        tr * acc[1] + ti * acc[0],
        tr * acc[2] + ti * acc[3],
        tr * acc[3] - ti * acc[2],
    )


PLANE_UNITS = STEPS * 3 * ROWS
IMAGE_UNITS = STEPS * ROWS


def kernel(
    omegas_in, owner_in, reach_in, srows_in, scols_in, source, receiver, velocity, epsilon, delta,
    source_out, receiver_out, image_out,
    omegas, owner, reach, srows, scols,
    raw_fields, raw_model, cand, planes, field0, field1, field2, pair1, pair2, pair3, next1, next2,
    next3, coef, images, image_sum, load_sems, halo_sends, halo_recvs, *rest,
):
    sems, bufs = rest[:12], rest[12:]
    tile = lax.axis_index("tile")
    index = lax.axis_index("freq")
    neighbour = {"tile": 1 - tile}
    pairs, nexts = (pair1, pair2, pair3), (next1, next2, next3)

    barrier = pltpu.get_barrier_semaphore()
    greeted = all_peers() + [neighbour]
    for peer in greeted:
        pl.semaphore_signal(barrier, inc=1, device_id=peer, device_id_type=MESH)

    loads = []
    for i, array in enumerate((velocity, epsilon, delta)):
        loads.append(pltpu.make_async_copy(array, raw_model.at[i], load_sems.at[i]))
    for i, array in enumerate((source, receiver)):
        loads.append(pltpu.make_async_copy(array, raw_fields.at[i], load_sems.at[3 + i]))
    smalls = ((omegas_in, omegas), (owner_in, owner), (reach_in, reach), (srows_in, srows), (scols_in, scols))
    for i, (array, place) in enumerate(smalls):
        loads.append(pltpu.make_async_copy(array, place, load_sems.at[5 + i]))
    for made in loads:
        made.start()

    a0 = Stream(cand, planes, 0, 128, ("xy", "z"), bufs[0:6], sems[0], sems[1])
    a1 = Stream(cand, planes, 192, 128, ("xy", "z"), bufs[6:12], sems[2], sems[3])
    b0 = Relay(cand, planes, 128, 64, bufs[12:17], sems[4], sems[5])
    b1 = Relay(cand, planes, 320, 64, bufs[17:22], sems[6], sems[7])
    p0 = Picture(images, image_sum, 0, bufs[22:25], sems[8], sems[9])
    p1 = Picture(images, image_sum, ROWS, bufs[25:28], sems[10], sems[11])

    for made in loads[:3] + loads[5:]:
        made.wait()
    omega = omegas[0]
    picks = []
    for step in range(STEPS):
        for slot in range(2):
            hit = owner[step] == index * 2 + slot
            picks.append(jnp.full((8, LANES), jnp.where(hit, 1.0, 0.0), F32))

    def candidate(t, _):
        for k in range(8):
            place = (pl.ds(pl.multiple_of(t * 8, 8), 8), pl.ds(k * LANES, LANES))
            forms = []
            for slot in range(2):
                v = raw_model[(0, slot) + place]
                e = raw_model[(1, slot) + place]
                d = raw_model[(2, slot) + place]
                wide = 1.0 + 2.0 * d
                both = 1.0 / (v * wide)
                slowness = both * wide
                stretch = both * v
                curve = 5.0 * slowness * stretch
                forms.append((10.0 * slowness, curve, curve * ((e - d) * stretch * 0.125)))
            for step in range(STEPS):
                for n in range(3):
                    value = picks[step * 2] * forms[0][n] + picks[step * 2 + 1] * forms[1][n]
                    cand[at((step * 3 + n) * 64 + t * 8 + k)] = value
        return 0

    lax.fori_loop(0, 8, candidate, 0)
    pl.semaphore_wait(barrier, len(greeted))

    for s in (a0, b0, a1, b1):
        s.core_out()

    for made in loads[3:5]:
        made.wait()
    zero = jnp.zeros((8, LANES), F32)
    for field in (field0, field1) + pairs + nexts:
        for i in range(HMAX):
            for c in range(4):
                field[c, at(67 * tile + i)] = zero
    delay = jnp.full((8, LANES), omega * 0.05, F32)
    pulse = (16.0 * jnp.cos(delay), -16.0 * jnp.sin(delay))

    def arrange(t, _):
        for c in range(4):
            for k in range(8):
                place = (pl.ds(pl.multiple_of(t * 8, 8), 8), pl.ds(k * LANES, LANES))
                value = raw_fields[(c // 2, c % 2, 0) + place]
                if c < 2:
                    row = lax.broadcasted_iota(jnp.int32, (8, LANES), 0) + (tile * ROWS + t * 8)
                    col = lax.broadcasted_iota(jnp.int32, (8, LANES), 1) + k * LANES
                    for s in range(4):
                        hit = (row == srows[s]) & (col == scols[s])
                        value = value + jnp.where(hit, pulse[c], 0.0)
                field0[c, pl.ds((t * 8 + HMAX) * 8 + k, 8, stride=8)] = value
        return 0

    def weights():
        for step in range(STEPS):
            live = [jnp.where(reach[step] >= n, t, 0.0) for n, t in zip(NEEDED, TAPERS)]
            total = live[0] * COUNTS[0]
            for n, w in zip(COUNTS[1:], live[1:]):
                total = total + w * n
            inverse = 1.0 / jnp.full((8, LANES), total, F32)
            for i, w in enumerate(live):
                coef[at(step * 20 + i * 2)] = inverse * w
                coef[at(step * 20 + i * 2 + 1)] = inverse * w

    def halo(field, slot):
        made = pltpu.make_async_remote_copy(
            src_ref=field.at[:, at(64 - 61 * tile, HMAX)],
            dst_ref=field.at[:, at(67 * tile, HMAX)],
            send_sem=halo_sends.at[slot],
            recv_sem=halo_recvs.at[slot],
            device_id=neighbour,
            device_id_type=MESH,
        )
        made.start()
        return made

    for s in (a0, b0):
        s.land()
        s.core_sum()
        s.scatter1()
    lax.fori_loop(0, 8, arrange, 0)
    halo0 = halo(field0, 0)
    a0.land()
    a0.sum1_()
    a0.scatter2()
    b0.land()
    b0.exchange()
    for s in (a1, b1):
        s.land()
        s.core_sum()
        s.scatter1()
    weights()
    spread_rows(field0, pairs, HMAX, ROWS)
    halo0.wait()
    spread_rows(field0, pairs, 67 * (1 - tile), HMAX)
    a0.land()
    a0.sum2_()
    a0.gather2()
    b0.land()
    b0.gather()
    a1.land()
    a1.sum1_()
    a1.scatter2()
    b1.land()
    b1.exchange()
    a0.land()
    a0.gather1()
    b0.land()
    b0.core_back()
    a1.land()
    a1.sum2_()
    a1.gather2()
    b1.land()
    b1.gather()
    a0.land()
    a0.core_back()
    b0.land()
    a0.land()
    a1.land()
    a1.gather1()
    b1.land()
    b1.core_back()

    def first_step(i, _):
        x = (1 - tile) * (ROWS - 2) + (2 * tile - 1) * (i * 2)
        out = two_rows(field0, pairs, planes, coef, 0, x, omega)
        for c in range(4):
            field1[c, at(x + HMAX, 2)] = out[c]
            for h in range(2):
                for pair, value in zip(nexts, spread(out[c][h * 8 : h * 8 + 8])):
                    pair[c, at(x + HMAX + h)] = value
        images[at(x, 2)] = out[0] * out[2] + out[1] * out[3]
        return 0

    lax.fori_loop(0, 2, first_step, 0)
    halo1 = halo(field1, 1)
    lax.fori_loop(2, 20, first_step, 0)
    a1.land()
    a1.core_back()
    lax.fori_loop(20, ROWS // 2, first_step, 0)
    p0.scatter()
    a1.land()
    b1.land()

    def second_step(i, _):
        x = tile * (ROWS - 2) + (1 - 2 * tile) * (i * 2)
        out = two_rows(field1, nexts, planes, coef, 1, x, omega)
        for c in range(4):
            field2[c, at(x, 2)] = out[c]
        images[at(ROWS + x, 2)] = out[0] * out[2] + out[1] * out[3]
        return 0

    lax.fori_loop(0, 30, second_step, 0)
    halo1.wait()
    spread_rows(field1, nexts, 67 * (1 - tile), HMAX)
    lax.fori_loop(30, ROWS // 2, second_step, 0)
    p1.scatter()
    p0.land()
    p0.exchange()

    def restore(t, _):
        for c in range(4):
            for k in range(8):
                place = (pl.ds(pl.multiple_of(t * 8, 8), 8), pl.ds(k * LANES, LANES))
                out = (source_out, receiver_out)[c // 2]
                out[(c % 2, 0) + place] = field2[
                    c, pl.ds(t * 64 + k, 8, stride=8)
                ]
        return 0

    lax.fori_loop(0, 8, restore, 0)
    for s in (a0, b0, a1, b1):
        s.finish()
    p0.land()
    p0.gather()
    p1.land()
    p1.exchange()
    p1.land()
    p1.gather()
    for s in (p0, p1):
        s.finish()
    p0.land()
    p1.land()

    def picture(t, _):
        for step in range(STEPS):
            for k in range(8):
                place = (pl.ds(pl.multiple_of(t * 8, 8), 8), pl.ds(k * LANES, LANES))
                value = image_sum[pl.ds(step * 512 + t * 64 + k, 8, stride=8)]
                image_out[(step,) + place] = value
        return 0

    lax.fori_loop(0, 8, picture, 0)


def hand_over(*refs):
    between, sems = refs[6:9], refs[9]
    loads = [pltpu.make_async_copy(refs[i], between[i], sems.at[i]) for i in range(3)]
    stores = [pltpu.make_async_copy(between[i], refs[3 + i], sems.at[3 + i]) for i in range(3)]
    for made in loads:
        made.start()
    for load, store in zip(loads, stores):
        load.wait()
        store.start()
    for made in stores:
        made.wait()


def per_device(*args):
    source, receiver, omegas, velocity, epsilon, delta, owner, reach, srows, scols = args
    hbm = pl.BlockSpec(memory_space=pl.ANY)
    out_shape = (
        jax.ShapeDtypeStruct(source.shape, F32),
        jax.ShapeDtypeStruct(receiver.shape, F32),
        jax.ShapeDtypeStruct((STEPS, ROWS, 1024), F32),
    )

    def block(n):
        return pltpu.VMEM((n * 8, LANES), F32)

    def plane(n):
        return pltpu.VMEM((4, n * 8, LANES), F32)

    def small(array):
        return pltpu.SMEM(array.shape, array.dtype)

    counts = [Stream.SEMS] * 4 + [Relay.SEMS] * 4 + [Picture.SEMS] * 4
    made = pl.pallas_call(
        kernel,
        out_shape=out_shape,
        in_specs=[hbm] * 10,
        out_specs=tuple([pl.BlockSpec(memory_space=pltpu.VMEM)] * 3),
        scratch_shapes=[small(array) for array in (omegas, owner, reach, srows, scols)]
        + [
            pltpu.VMEM((2, 2, 1, ROWS, 1024), F32),
            pltpu.VMEM((3, 2, ROWS, 1024), F32),
            block(PLANE_UNITS),
            block(PLANE_UNITS),
            plane(TALL),
            plane(TALL),
            plane(ROWS),
        ]
        + [plane(TALL)] * 6
        + [
            block(40),
            block(IMAGE_UNITS),
            block(IMAGE_UNITS),
            pltpu.SemaphoreType.DMA((10,)),
            pltpu.SemaphoreType.DMA((2,)),
            pltpu.SemaphoreType.DMA((2,)),
        ]
        + [pltpu.SemaphoreType.DMA((n,)) for n in counts]
        + Stream.scratch(128) * 2
        + Relay.scratch(64) * 2
        + Picture.scratch() * 2,
        compiler_params=pltpu.CompilerParams(
            collective_id=0, has_side_effects=True, vmem_limit_bytes=52 << 20
        ),
        name="migrate",
    )(omegas, owner, reach, srows, scols, source, receiver, velocity, epsilon, delta)
    return pl.pallas_call(
        hand_over,
        out_shape=out_shape,
        in_specs=[hbm] * 3,
        out_specs=(hbm, hbm, hbm),
        scratch_shapes=[pltpu.VMEM(o.shape, F32) for o in out_shape]
        + [pltpu.SemaphoreType.DMA((6,))],
        compiler_params=pltpu.CompilerParams(vmem_limit_bytes=52 << 20),
        name="hand_over",
    )(*made)


def solution(mesh):
    in_specs = (
        P(None, "freq", "tile", None),
        P(None, "freq", "tile", None),
        P("freq"),
        P("freq", "tile", None),
        P("freq", "tile", None),
        P("freq", "tile", None),
        P(),
        P(),
        P(),
        P(),
    )
    out_specs = (
        P(None, "freq", "tile", None),
        P(None, "freq", "tile", None),
        P(None, "tile", None),
    )
    return jax.shard_map(
        per_device, mesh=mesh, in_specs=in_specs, out_specs=out_specs, check_vma=False
    )
```

```python
import math

import jax
import jax.numpy as jnp
import numpy as np
from jax import lax
from jax.experimental import pallas as pl
from jax.experimental.pallas import tpu as pltpu
from jax.sharding import PartitionSpec as P

STEPS = 2
HMAX = 3
ROWS = 64
TALL = ROWS + 2 * HMAX
LANES = 128
GAIN = 16.0 / math.sqrt(128.0)
MESH = pl.DeviceIdType.MESH
F32 = jnp.float32


def _minimax(fn, high, degree, weight):
    count = 2000
    nodes = high / 2 + high / 2 * np.cos(np.pi * (np.arange(count) + 0.5) / count)
    target, scale = fn(nodes), weight(nodes)
    table = np.vander(nodes, degree + 1, increasing=True)
    bias = np.ones(count)
    best, least = None, np.inf
    for _ in range(60):
        coefs = np.linalg.lstsq(table * (bias * scale)[:, None], target * bias * scale, rcond=None)[0]
        error = np.abs((table @ coefs - target) * scale)
        if error.max() < least:
            best, least = coefs, error.max()
        bias = bias * (error / error.max() + 1e-3) ** 0.3
        bias = bias / bias.max()
    return tuple(float(np.float32(c)) for c in best)


REACH_SQ = 1.6 * 1.6
SIN = _minimax(lambda u: np.sin(np.sqrt(u)) / np.sqrt(u), REACH_SQ, 4, np.sqrt)
COS = _minimax(lambda u: np.cos(np.sqrt(u)), REACH_SQ, 4, np.ones_like)

GROUPS = sorted({a * a + b * b for a in range(4) for b in range(4)})
COUNTS = [
    sum(1 for a in range(-3, 4) for b in range(-3, 4) if a * a + b * b == r) for r in GROUPS
]
NEEDED = [
    max(max(a, b) for a in range(4) for b in range(4) if a * a + b * b == r) for r in GROUPS
]
TAPERS = [float(np.float32(math.exp(-r / 4.0))) for r in GROUPS]


def at(unit, count=1):
    return pl.ds(pl.multiple_of(unit * 8, 8), count * 8)


def horner(u, coefs):
    value = coefs[-1] * u + coefs[-2]
    for c in coefs[-3::-1]:
        value = value * u + c
    return value


def cis(x):
    u = x * x
    return horner(u, COS), x * horner(u, SIN)


def mul(a, b):
    return a[0] * b[0] - a[1] * b[1], a[0] * b[1] + a[1] * b[0]


def square(a):
    twice = a[1] + a[1]
    return 1.0 - a[1] * twice, a[0] * twice


def coords():
    f = lax.axis_index("freq")
    return lax.div(f, 16), lax.rem(lax.div(f, 4), 4), lax.rem(lax.div(f, 2), 2), lax.rem(f, 2)


def device(z, x, y, c):
    return {"freq": ((z * 4 + x) * 2 + y) * 2 + c}


def xy_peers():
    z, x, y, c = coords()
    out = []
    for k in (5, 4, 3, 7, 2, 6, 1):
        px, py = lax.rem(x + k // 2, 4), lax.rem(y + k % 2, 2)
        out.append((device(z, px, py, c), px * 2 + py))
    return x * 2 + y, out


def z_peers():
    z, x, y, c = coords()
    return z, [(device(lax.rem(z + k, 8), x, y, c), lax.rem(z + k, 8)) for k in (4, 3, 5, 2, 6, 1, 7)]


def x_peers():
    z, x, y, c = coords()
    return x, [(device(z, lax.rem(x + k, 4), y, c), lax.rem(x + k, 4)) for k in (2, 1, 3)]


def flat_peers():
    z, x, y, c = coords()
    out = []
    for k in (10, 11, 8, 9, 6, 7, 14, 15, 4, 5, 12, 13, 2, 3, 1):
        px, py, pc = lax.rem(x + k // 4, 4), lax.rem(y + k // 2 % 2, 2), lax.rem(c + k % 2, 2)
        out.append((device(z, px, py, pc), px * 4 + py * 2 + pc))
    return x * 4 + y * 2 + c, out


def core_peer():
    z, x, y, c = coords()
    return device(z, x, y, 1 - c)


def all_peers():
    return [d for d, _ in z_peers()[1]] + [d for d, _ in flat_peers()[1]]


class Stream:
    SEMS = 6

    def __init__(self, src, res, base, units, order, bufs, sends, recvs):
        self.src, self.res, self.base, self.units = src, res, base, units
        self.core_in, self.half, self.in1, self.sum1, self.in2, self.out1 = bufs
        self.sends, self.recvs = sends, recvs
        self.groups = [xy_peers() if o == "xy" else z_peers() for o in order]
        self.core = coords()[3]
        self.done = 0

    @staticmethod
    def scratch(units):
        def block(n):
            return pltpu.VMEM((n * 8, LANES), F32)

        return [
            block(units // 2),
            block(units // 2),
            block(7 * units // 16),
            block(units // 16),
            block(7 * units // 128),
            block(units // 16),
        ]

    def send(self, phase, parts):
        for src, dst, to in parts:
            pltpu.make_async_remote_copy(
                src_ref=src,
                dst_ref=dst,
                send_sem=self.sends.at[phase],
                recv_sem=self.recvs.at[phase],
                device_id=to,
                device_id_type=MESH,
            ).start()
        self.phase = phase

    def land(self):
        whole = self.whole(self.phase)
        pltpu.make_async_copy(whole, whole, self.recvs.at[self.phase]).wait()

    def finish(self):
        for phase in range(self.done, self.phase + 1):
            whole = self.whole(phase)
            pltpu.make_async_copy(whole, whole, self.sends.at[phase]).wait()
        self.done = self.phase + 1

    def core_out(self):
        n = self.units // 2
        other = self.base + (1 - self.core) * n
        self.send(0, [(self.src.at[at(other, n)], self.core_in, core_peer())])

    def core_sum(self):
        n = self.units // 2
        mine = self.base + self.core * n

        def body(i, _):
            self.half[at(i * 16, 16)] = self.src[at(mine + i * 16, 16)] + self.core_in[at(i * 16, 16)]
            return 0

        lax.fori_loop(0, n // 16, body, 0)

    def scatter1(self):
        n = self.units // 16
        self.send(1, [
            (self.half.at[at(j * n, n)], self.in1.at[at(k * n, n)], to)
            for k, (to, j) in enumerate(self.groups[0][1])
        ])

    def sum1_(self):
        n = self.units // 16
        me = self.groups[0][0]

        total = self.half[at(me * n, n)]
        for k in range(7):
            total = total + self.in1[at(k * n, n)]
        self.sum1[...] = total

    def scatter2(self):
        n = self.units // 128
        self.send(2, [
            (self.sum1.at[at(j * n, n)], self.in2.at[at(k * n, n)], to)
            for k, (to, j) in enumerate(self.groups[1][1])
        ])

    def sum2_(self):
        n = self.units // 128
        me = self.groups[1][0]
        for i in range(n):
            total = self.sum1[at(me * n + i)]
            for k in range(7):
                total = total + self.in2[at(k * n + i)]
            self.out1[at(me * n + i)] = total

    def gather2(self):
        n = self.units // 128
        me = self.groups[1][0]
        mine = at(me * n, n)
        self.send(3, [(self.out1.at[mine], self.out1.at[mine], to) for to, j in self.groups[1][1]])

    def gather1(self):
        n = self.units // 16
        place = self.base + self.core * (self.units // 2) + self.groups[0][0] * n
        self.send(4, [(self.out1, self.res.at[at(place, n)], to) for to, j in self.groups[0][1]])
        self.res[at(place, n)] = self.out1[...]

    def core_back(self):
        n = self.units // 2
        mine = self.base + self.core * n
        self.send(5, [(self.res.at[at(mine, n)], self.res.at[at(mine, n)], core_peer())])

    def whole(self, phase):
        first, second = self.units // 16, self.units // 128
        if phase == 0:
            return self.core_in
        if phase == 5:
            return self.res.at[at(self.base, self.units // 2)]
        return (self.in1, self.in2, self.out1.at[at(0, 7 * second)], self.res.at[at(self.base, 7 * first)])[phase - 1]


class Relay:
    SEMS = 6

    def __init__(self, src, res, base, units, bufs, sends, recvs):
        self.src, self.res, self.base, self.units = src, res, base, units
        self.core_in, self.half, self.shares, self.stack, self.total = bufs
        self.sends, self.recvs = sends, recvs
        self.z, self.ring = z_peers()
        self.me, self.group = xy_peers()
        self.x, self.line = x_peers()
        self.core = coords()[3]
        self.done = 0

    @staticmethod
    def scratch(units):
        def block(n):
            return pltpu.VMEM((n * 8, LANES), F32)

        share = units // 16
        return [block(units // 2), block(units // 2), block(7 * share), block(2 * share), block(share)]

    send = Stream.send
    land = Stream.land
    finish = Stream.finish
    core_out = Stream.core_out
    core_sum = Stream.core_sum

    def scatter1(self):
        n = self.units // 16
        self.send(1, [
            (self.half.at[at(j * n, n)], self.shares.at[at(k * n, n)], to)
            for k, (to, j) in enumerate(self.ring)
        ])

    def scatter2(self):
        n, quarter = self.units // 16, self.units // 64
        total = self.half[at(self.z * n, n)]
        for k in range(7):
            total = total + self.shares[at(k * n, n)]
        self.half[at(self.z * n, n)] = total
        mine = at(self.me * quarter, quarter)
        self.stack[mine] = self.half[at(self.z * n + self.x * quarter, quarter)]
        self.send(2, [
            (self.half.at[at(self.z * n + lax.div(j, 2) * quarter, quarter)], self.stack.at[mine], to)
            for to, j in self.group
        ])

    def gather2(self):
        quarter = self.units // 64
        total = self.stack[at(0, quarter)]
        for k in range(1, 8):
            total = total + self.stack[at(k * quarter, quarter)]
        mine = at(self.x * quarter, quarter)
        self.total[mine] = total
        self.send(3, [(self.total.at[mine], self.total.at[mine], to) for to, j in self.line])

    def gather1(self):
        n = self.units // 16
        place = self.base + self.core * (self.units // 2) + self.z * n
        self.send(4, [(self.total, self.res.at[at(place, n)], to) for to, j in self.ring])
        self.res[at(place, n)] = self.total[...]

    def core_back(self):
        n = self.units // 2
        mine = at(self.base + self.core * n, n)
        self.send(5, [(self.res.at[mine], self.res.at[mine], core_peer())])

    def whole(self, phase):
        share, quarter = self.units // 16, self.units // 64
        if phase == 0:
            return self.core_in
        if phase == 5:
            return self.res.at[at(self.base, self.units // 2)]
        return (
            self.shares,
            self.stack.at[at(0, 7 * quarter)],
            self.total.at[at(0, 3 * quarter)],
            self.res.at[at(self.base, 7 * share)],
        )[phase - 1]


class Picture:
    SEMS = 3
    SHARE = ROWS // 16

    def __init__(self, src, res, base, bufs, sends, recvs):
        self.src, self.res, self.base = src, res, base
        self.shares, self.stack, self.total = bufs
        self.sends, self.recvs = sends, recvs
        self.me, self.group = flat_peers()
        self.z, self.ring = z_peers()
        self.done = 0

    @staticmethod
    def scratch():
        n = Picture.SHARE * 8
        return [
            pltpu.VMEM((15 * n, LANES), F32),
            pltpu.VMEM((8 * n, LANES), F32),
            pltpu.VMEM((n, LANES), F32),
        ]

    send = Stream.send
    land = Stream.land
    finish = Stream.finish

    def scatter(self):
        n = self.SHARE
        self.send(0, [
            (self.src.at[at(self.base + j * n, n)], self.shares.at[at(k * n, n)], to)
            for k, (to, j) in enumerate(self.group)
        ])

    def exchange(self):
        n = self.SHARE
        for i in range(n):
            total = self.src[at(self.base + self.me * n + i)]
            for k in range(15):
                total = total + self.shares[at(k * n + i)]
            self.stack[at(self.z * n + i)] = total
        mine = at(self.z * n, n)
        self.send(1, [(self.stack.at[mine], self.stack.at[mine], to) for to, j in self.ring])

    def gather(self):
        n = self.SHARE
        place = self.base + self.me * n
        for i in range(n):
            total = self.stack[at(i)]
            for k in range(1, 8):
                total = total + self.stack[at(k * n + i)]
            total = total * GAIN
            self.total[at(i)] = total
            self.res[at(place + i)] = total
        self.send(2, [(self.total, self.res.at[at(place, n)], to) for to, j in self.group])

    def whole(self, phase):
        n = self.SHARE
        return (self.shares, self.stack.at[at(0, 7 * n)], self.res.at[at(self.base, 15 * n)])[phase]


def spread(here):
    lane = lax.broadcasted_iota(jnp.int32, (8, LANES), 1)
    block = lax.broadcasted_iota(jnp.int32, (8, LANES), 0)
    above = jnp.where(block < 7, pltpu.roll(here, 7, 0), 0.0)
    below = jnp.where(block > 0, pltpu.roll(here, 1, 0), 0.0)
    out = []
    for b in range(1, 4):
        plus = pltpu.roll(jnp.where(lane < b, above, here), LANES - b, 1)
        minus = pltpu.roll(jnp.where(lane >= LANES - b, below, here), b, 1)
        out.append(plus + minus)
    return out


def spread_rows(field, pairs, first, count):
    def body(i, _):
        for c in range(4):
            for pair, value in zip(pairs, spread(field[c, at(first + i)])):
                pair[c, at(first + i)] = value
        return 0

    lax.fori_loop(0, count, body, 0, unroll=4 if count % 4 == 0 else 1)


def plane_unit(step, array, t):
    if array == 2:
        return step * 192 + 128 + t * 8
    return step * 192 + lax.div(t, 4) * 64 + array * 32 + lax.rem(t, 4) * 8


def weights_of(planes, step, x, omega):
    t, s = lax.div(x, 8), lax.rem(x, 8)

    def row(array):
        start = plane_unit(step, array, t) * 8 + s
        both = [planes[pl.ds(start + i, 8, stride=8)] for i in range(2)]
        return jnp.concatenate(both, axis=0)

    turn = cis((0.5 * omega) * row(0))
    turn = square(turn)
    q, a = omega * row(1), omega * row(2)
    z = cis(q)
    u = a * a
    w1 = (1.0 + u * (-0.5 + u * (1.0 / 24.0)), a * (u * (1.0 / 6.0) - 1.0))
    w2 = square(w1)
    w4 = square(w2)
    w8 = square(w4)
    w16 = square(w8)
    w32 = square(w16)
    w64 = square(w32)
    w128 = square(w64)
    g = {}
    g[1] = mul(z, w1)
    g[2] = mul(square(g[1]), w2)
    g[4] = mul(square(g[2]), w8)
    g[8] = mul(square(g[4]), w32)
    g[5] = mul(mul(g[4], w8), g[1])
    g[9] = mul(mul(g[8], w16), g[1])
    w34 = mul(w32, w2)
    g[10] = mul(square(g[5]), mul(w34, w16))
    g[13] = mul(mul(g[9], g[4]), mul(w64, w8))
    g[18] = mul(square(g[9]), mul(w34, w128))
    return turn, g


def two_rows(field, pairs, planes, coef, step, x, omega):
    rows = [field] + list(pairs)

    def gathered(r, c):
        total = None
        for a in range(4):
            for b in range(4):
                if a * a + b * b != r:
                    continue
                for shift in sorted({a, -a}):
                    piece = rows[b][c, at(x + HMAX + shift, 2)]
                    total = piece if total is None else total + piece
        return total

    turn, g = weights_of(planes, step, x, omega)
    first = coef[at(step * 20, 2)]
    acc = [first * gathered(0, c) for c in range(4)]
    for index, r in enumerate(GROUPS):
        if r == 0:
            continue
        scale = coef[at(step * 20 + index * 2, 2)]
        wr, wi = g[r][0] * scale, g[r][1] * scale
        sr, si, rr, ri = [gathered(r, c) for c in range(4)]
        acc[0] = acc[0] + (wr * sr - wi * si)
        acc[1] = acc[1] + (wr * si + wi * sr)
        acc[2] = acc[2] + (wr * rr + wi * ri)
        acc[3] = acc[3] + (wr * ri - wi * rr)
    tr, ti = turn
    return (
        tr * acc[0] - ti * acc[1],
        tr * acc[1] + ti * acc[0],
        tr * acc[2] + ti * acc[3],
        tr * acc[3] - ti * acc[2],
    )


PLANE_UNITS = STEPS * 3 * ROWS
IMAGE_UNITS = STEPS * ROWS


def kernel(
    omegas_in, numbers_in, source, receiver, velocity, epsilon, delta,
    source_out, receiver_out, image_out,
    omegas, numbers,
    raw_fields, raw_model, cand, planes, field0, field1, field2, pair1, pair2, pair3, next1, next2,
    next3, coef, images, image_sum, load_sems, halo_sends, halo_recvs, *rest,
):
    sems, bufs = rest[:12], rest[12:]
    tile = lax.axis_index("tile")
    index = lax.axis_index("freq")
    neighbour = {"tile": 1 - tile}
    pairs, nexts = (pair1, pair2, pair3), (next1, next2, next3)

    barrier = pltpu.get_barrier_semaphore()
    greeted = all_peers() + [neighbour]
    for peer in greeted:
        pl.semaphore_signal(barrier, inc=1, device_id=peer, device_id_type=MESH)

    loads = []
    for i, array in enumerate((velocity, epsilon, delta)):
        loads.append(pltpu.make_async_copy(array, raw_model.at[i], load_sems.at[i]))
    for i, array in enumerate((source, receiver)):
        loads.append(pltpu.make_async_copy(array, raw_fields.at[i], load_sems.at[3 + i]))
    smalls = ((omegas_in, omegas), (numbers_in, numbers))
    for i, (array, place) in enumerate(smalls):
        loads.append(pltpu.make_async_copy(array, place, load_sems.at[5 + i]))
    for made in loads:
        made.start()

    a0 = Stream(cand, planes, 0, 128, ("xy", "z"), bufs[0:6], sems[0], sems[1])
    a1 = Stream(cand, planes, 192, 128, ("xy", "z"), bufs[6:12], sems[2], sems[3])
    b0 = Relay(cand, planes, 128, 64, bufs[12:17], sems[4], sems[5])
    b1 = Relay(cand, planes, 320, 64, bufs[17:22], sems[6], sems[7])
    p0 = Picture(images, image_sum, 0, bufs[22:25], sems[8], sems[9])
    p1 = Picture(images, image_sum, ROWS, bufs[25:28], sems[10], sems[11])

    for made in loads[:3] + loads[5:]:
        made.wait()
    omega = omegas[0]
    owner, reach = [numbers[i] for i in (0, 1)], [numbers[i] for i in (2, 3)]
    srows, scols = [numbers[4 + i] for i in range(4)], [numbers[8 + i] for i in range(4)]
    picks = []
    for step in range(STEPS):
        for slot in range(2):
            hit = owner[step] == index * 2 + slot
            picks.append(jnp.full((8, LANES), jnp.where(hit, 1.0, 0.0), F32))

    def candidate(t, _):
        for k in range(8):
            place = (pl.ds(pl.multiple_of(t * 8, 8), 8), pl.ds(k * LANES, LANES))
            forms = []
            for slot in range(2):
                v = raw_model[(0, slot) + place]
                e = raw_model[(1, slot) + place]
                d = raw_model[(2, slot) + place]
                wide = 1.0 + 2.0 * d
                both = 1.0 / (v * wide)
                slowness = both * wide
                stretch = both * v
                curve = 5.0 * slowness * stretch
                forms.append((10.0 * slowness, curve, curve * ((e - d) * stretch * 0.125)))
            for step in range(STEPS):
                for n in range(3):
                    value = picks[step * 2] * forms[0][n] + picks[step * 2 + 1] * forms[1][n]
                    cand[at(plane_unit(step, n, t) + k)] = value
        return 0

    lax.fori_loop(0, 8, candidate, 0)
    pl.semaphore_wait(barrier, len(greeted))

    for s in (a0, b0, a1, b1):
        s.core_out()

    for made in loads[3:5]:
        made.wait()
    zero = jnp.zeros((8, LANES), F32)
    for field in (field0, field1) + pairs + nexts:
        for i in range(HMAX):
            for c in range(4):
                field[c, at(67 * tile + i)] = zero
    delay = jnp.full((8, LANES), omega * 0.05, F32)
    pulse = (16.0 * jnp.cos(delay), -16.0 * jnp.sin(delay))

    def arrange(t, _):
        for c in range(4):
            for k in range(8):
                place = (pl.ds(pl.multiple_of(t * 8, 8), 8), pl.ds(k * LANES, LANES))
                value = raw_fields[(c // 2, c % 2, 0) + place]
                if c < 2:
                    row = lax.broadcasted_iota(jnp.int32, (8, LANES), 0) + (tile * ROWS + t * 8)
                    col = lax.broadcasted_iota(jnp.int32, (8, LANES), 1) + k * LANES
                    for s in range(4):
                        hit = (row == srows[s]) & (col == scols[s])
                        value = value + jnp.where(hit, pulse[c], 0.0)
                field0[c, pl.ds((t * 8 + HMAX) * 8 + k, 8, stride=8)] = value
        return 0

    def weights():
        for step in range(STEPS):
            live = [jnp.where(reach[step] >= n, t, 0.0) for n, t in zip(NEEDED, TAPERS)]
            total = live[0] * COUNTS[0]
            for n, w in zip(COUNTS[1:], live[1:]):
                total = total + w * n
            inverse = 1.0 / jnp.full((8, LANES), total, F32)
            for i, w in enumerate(live):
                coef[at(step * 20 + i * 2)] = inverse * w
                coef[at(step * 20 + i * 2 + 1)] = inverse * w

    def halo(field, slot):
        made = pltpu.make_async_remote_copy(
            src_ref=field.at[:, at(64 - 61 * tile, HMAX)],
            dst_ref=field.at[:, at(67 * tile, HMAX)],
            send_sem=halo_sends.at[slot],
            recv_sem=halo_recvs.at[slot],
            device_id=neighbour,
            device_id_type=MESH,
        )
        made.start()
        return made

    for s in (a0, b0):
        s.land()
        s.core_sum()
        s.scatter1()
    lax.fori_loop(0, 8, arrange, 0)
    halo0 = halo(field0, 0)
    for s in (a1, b1):
        s.land()
        s.core_sum()
        s.scatter1()
    a0.land()
    a0.sum1_()
    a0.scatter2()
    b0.land()
    b0.scatter2()
    weights()
    spread_rows(field0, pairs, HMAX, ROWS)
    a1.land()
    a1.sum1_()
    a1.scatter2()
    b1.land()
    b1.scatter2()
    halo0.wait()
    spread_rows(field0, pairs, 67 * (1 - tile), HMAX)
    a0.land()
    a0.sum2_()
    a0.gather2()
    b0.land()
    b0.gather2()
    a1.land()
    a1.sum2_()
    a1.gather2()
    b1.land()
    b1.gather2()
    for s in (a0, b0):
        s.land()
        s.gather1()
    for s in (a1, b1):
        s.land()
        s.gather1()
    for s in (a0, b0):
        s.land()
        s.core_back()

    core = coords()[3]

    def first_row(i):
        part = core + lax.div(i, 16) * (1 - 2 * core)
        return part * 32 + (1 - tile) * 30 + (2 * tile - 1) * (lax.rem(i, 16) * 2)

    def spread_done(i):
        place = first_row(i) + HMAX
        for c in range(4):
            for h in range(2):
                for pair, value in zip(nexts, spread(field1[c, at(place + h)])):
                    pair[c, at(place + h)] = value

    def first_pair(i, behind):
        x = first_row(i)
        out = two_rows(field0, pairs, planes, coef, 0, x, omega)
        if behind:
            spread_done(i - 1)
        for c in range(4):
            field1[c, at(x + HMAX, 2)] = out[c]
        images[at(x, 2)] = out[0] * out[2] + out[1] * out[3]

    def first_step(i, _):
        first_pair(i, True)
        return 0

    first_pair(0, False)
    lax.fori_loop(1, 16, first_step, 0)
    for s in (a0, b0):
        s.land()
    for s in (a1, b1):
        s.land()
        s.core_back()
    lax.fori_loop(16, 18, first_step, 0)
    halo1 = halo(field1, 1)
    lax.fori_loop(18, ROWS // 2, first_step, 0)
    p0.scatter()
    spread_done(ROWS // 2 - 1)
    a1.land()
    b1.land()

    def second_step(i, _):
        x = tile * (ROWS - 2) + (1 - 2 * tile) * (i * 2)
        out = two_rows(field1, nexts, planes, coef, 1, x, omega)
        for c in range(4):
            field2[c, at(x, 2)] = out[c]
        images[at(ROWS + x, 2)] = out[0] * out[2] + out[1] * out[3]
        return 0

    lax.fori_loop(0, 30, second_step, 0)
    halo1.wait()
    spread_rows(field1, nexts, 67 * (1 - tile), HMAX)
    lax.fori_loop(30, ROWS // 2, second_step, 0)
    p1.scatter()
    p0.land()
    p0.exchange()

    def restore(t, _):
        for c in range(4):
            for k in range(8):
                place = (pl.ds(pl.multiple_of(t * 8, 8), 8), pl.ds(k * LANES, LANES))
                out = (source_out, receiver_out)[c // 2]
                out[(c % 2, 0) + place] = field2[
                    c, pl.ds(t * 64 + k, 8, stride=8)
                ]
        return 0

    def picture(step):
        def body(t, _):
            for k in range(8):
                place = (pl.ds(pl.multiple_of(t * 8, 8), 8), pl.ds(k * LANES, LANES))
                image_out[(step,) + place] = image_sum[pl.ds(step * 512 + t * 64 + k, 8, stride=8)]
            return 0

        return body

    lax.fori_loop(0, 8, restore, 0)
    for s in (a0, b0, a1, b1):
        s.finish()
    p1.land()
    p1.exchange()
    p0.land()
    p0.gather()
    p1.land()
    p1.gather()
    p0.finish()
    p0.land()
    lax.fori_loop(0, 8, picture(0), 0)
    p1.finish()
    p1.land()
    lax.fori_loop(0, 8, picture(1), 0)


def hand_over(*refs):
    between, sems = refs[6:9], refs[9]
    loads = [pltpu.make_async_copy(refs[i], between[i], sems.at[i]) for i in range(3)]
    stores = [pltpu.make_async_copy(between[i], refs[3 + i], sems.at[3 + i]) for i in range(3)]
    for made in loads:
        made.start()
    for load, store in zip(loads, stores):
        load.wait()
        store.start()
    for made in stores:
        made.wait()


def per_device(*args):
    source, receiver, omegas, velocity, epsilon, delta, owner, reach, srows, scols = args
    hbm = pl.BlockSpec(memory_space=pl.ANY)
    out_shape = (
        jax.ShapeDtypeStruct(source.shape, F32),
        jax.ShapeDtypeStruct(receiver.shape, F32),
        jax.ShapeDtypeStruct((STEPS, ROWS, 1024), F32),
    )

    def block(n):
        return pltpu.VMEM((n * 8, LANES), F32)

    def plane(n):
        return pltpu.VMEM((4, n * 8, LANES), F32)

    def small(array):
        return pltpu.SMEM(array.shape, array.dtype)

    numbers = jnp.concatenate([owner[:2], reach, srows, scols])
    counts = [Stream.SEMS] * 4 + [Relay.SEMS] * 4 + [Picture.SEMS] * 4
    made = pl.pallas_call(
        kernel,
        out_shape=out_shape,
        in_specs=[hbm] * 7,
        out_specs=tuple([pl.BlockSpec(memory_space=pltpu.VMEM)] * 3),
        scratch_shapes=[small(array) for array in (omegas, numbers)]
        + [
            pltpu.VMEM((2, 2, 1, ROWS, 1024), F32),
            pltpu.VMEM((3, 2, ROWS, 1024), F32),
            block(PLANE_UNITS),
            block(PLANE_UNITS),
            plane(TALL),
            plane(TALL),
            plane(ROWS),
        ]
        + [plane(TALL)] * 6
        + [
            block(40),
            block(IMAGE_UNITS),
            block(IMAGE_UNITS),
            pltpu.SemaphoreType.DMA((10,)),
            pltpu.SemaphoreType.DMA((2,)),
            pltpu.SemaphoreType.DMA((2,)),
        ]
        + [pltpu.SemaphoreType.DMA((n,)) for n in counts]
        + Stream.scratch(128) * 2
        + Relay.scratch(64) * 2
        + Picture.scratch() * 2,
        compiler_params=pltpu.CompilerParams(
            collective_id=0, has_side_effects=True, vmem_limit_bytes=52 << 20
        ),
        name="migrate",
    )(omegas, numbers, source, receiver, velocity, epsilon, delta)
    return pl.pallas_call(
        hand_over,
        out_shape=out_shape,
        in_specs=[hbm] * 3,
        out_specs=(hbm, hbm, hbm),
        scratch_shapes=[pltpu.VMEM(o.shape, F32) for o in out_shape]
        + [pltpu.SemaphoreType.DMA((6,))],
        compiler_params=pltpu.CompilerParams(vmem_limit_bytes=52 << 20),
        name="hand_over",
    )(*made)


def solution(mesh):
    in_specs = (
        P(None, "freq", "tile", None),
        P(None, "freq", "tile", None),
        P("freq"),
        P("freq", "tile", None),
        P("freq", "tile", None),
        P("freq", "tile", None),
        P(),
        P(),
        P(),
        P(),
    )
    out_specs = (
        P(None, "freq", "tile", None),
        P(None, "freq", "tile", None),
        P(None, "tile", None),
    )
    return jax.shard_map(
        per_device, mesh=mesh, in_specs=in_specs, out_specs=out_specs, check_vma=False
    )
```

```python
import math

import jax
import jax.numpy as jnp
import numpy as np
from jax import lax
from jax.experimental import pallas as pl
from jax.experimental.pallas import tpu as pltpu
from jax.sharding import PartitionSpec as P

STEPS = 2
HMAX = 3
ROWS = 64
TALL = ROWS + 2 * HMAX
LANES = 128
GAIN = 16.0 / math.sqrt(128.0)
MESH = pl.DeviceIdType.MESH
F32 = jnp.float32


def _minimax(fn, high, degree, weight):
    count = 2000
    nodes = high / 2 + high / 2 * np.cos(np.pi * (np.arange(count) + 0.5) / count)
    target, scale = fn(nodes), weight(nodes)
    table = np.vander(nodes, degree + 1, increasing=True)
    bias = np.ones(count)
    best, least = None, np.inf
    for _ in range(60):
        coefs = np.linalg.lstsq(table * (bias * scale)[:, None], target * bias * scale, rcond=None)[0]
        error = np.abs((table @ coefs - target) * scale)
        if error.max() < least:
            best, least = coefs, error.max()
        bias = bias * (error / error.max() + 1e-3) ** 0.3
        bias = bias / bias.max()
    return tuple(float(np.float32(c)) for c in best)


REACH_SQ = 1.6 * 1.6
SIN = _minimax(lambda u: np.sin(np.sqrt(u)) / np.sqrt(u), REACH_SQ, 4, np.sqrt)
COS = _minimax(lambda u: np.cos(np.sqrt(u)), REACH_SQ, 4, np.ones_like)

GROUPS = sorted({a * a + b * b for a in range(4) for b in range(4)})
COUNTS = [
    sum(1 for a in range(-3, 4) for b in range(-3, 4) if a * a + b * b == r) for r in GROUPS
]
NEEDED = [
    max(max(a, b) for a in range(4) for b in range(4) if a * a + b * b == r) for r in GROUPS
]
TAPERS = [float(np.float32(math.exp(-r / 4.0))) for r in GROUPS]


def at(unit, count=1):
    return pl.ds(pl.multiple_of(unit * 8, 8), count * 8)


def horner(u, coefs):
    value = coefs[-1] * u + coefs[-2]
    for c in coefs[-3::-1]:
        value = value * u + c
    return value


def cis(x):
    u = x * x
    return horner(u, COS), x * horner(u, SIN)


def mul(a, b):
    return a[0] * b[0] - a[1] * b[1], a[0] * b[1] + a[1] * b[0]


def square(a):
    twice = a[1] + a[1]
    return 1.0 - a[1] * twice, a[0] * twice


def coords():
    f = lax.axis_index("freq")
    return lax.div(f, 16), lax.rem(lax.div(f, 4), 4), lax.rem(lax.div(f, 2), 2), lax.rem(f, 2)


def device(z, x, y, c):
    return {"freq": ((z * 4 + x) * 2 + y) * 2 + c}


def xy_peers():
    z, x, y, c = coords()
    out = []
    for k in (5, 4, 3, 7, 2, 6, 1):
        px, py = lax.rem(x + k // 2, 4), lax.rem(y + k % 2, 2)
        out.append((device(z, px, py, c), px * 2 + py))
    return x * 2 + y, out


def z_peers():
    z, x, y, c = coords()
    return z, [(device(lax.rem(z + k, 8), x, y, c), lax.rem(z + k, 8)) for k in (4, 3, 5, 2, 6, 1, 7)]


def x_peers():
    z, x, y, c = coords()
    return x, [(device(z, lax.rem(x + k, 4), y, c), lax.rem(x + k, 4)) for k in (2, 1, 3)]


def flat_peers():
    z, x, y, c = coords()
    out = []
    for k in (10, 11, 8, 9, 6, 7, 14, 15, 4, 5, 12, 13, 2, 3, 1):
        px, py, pc = lax.rem(x + k // 4, 4), lax.rem(y + k // 2 % 2, 2), lax.rem(c + k % 2, 2)
        out.append((device(z, px, py, pc), px * 4 + py * 2 + pc))
    return x * 4 + y * 2 + c, out


def core_peer():
    z, x, y, c = coords()
    return device(z, x, y, 1 - c)


def all_peers():
    return [d for d, _ in z_peers()[1]] + [d for d, _ in flat_peers()[1]]


class Stream:
    SEMS = 6

    def __init__(self, src, res, base, units, order, bufs, sends, recvs):
        self.src, self.res, self.base, self.units = src, res, base, units
        self.core_in, self.half, self.in1, self.sum1, self.in2, self.out1 = bufs
        self.sends, self.recvs = sends, recvs
        self.groups = [xy_peers() if o == "xy" else z_peers() for o in order]
        self.core = coords()[3]
        self.done = 0

    @staticmethod
    def scratch(units):
        def block(n):
            return pltpu.VMEM((n * 8, LANES), F32)

        return [
            block(units // 2),
            block(units // 2),
            block(7 * units // 16),
            block(units // 16),
            block(7 * units // 128),
            block(units // 16),
        ]

    def send(self, phase, parts):
        for src, dst, to in parts:
            pltpu.make_async_remote_copy(
                src_ref=src,
                dst_ref=dst,
                send_sem=self.sends.at[phase],
                recv_sem=self.recvs.at[phase],
                device_id=to,
                device_id_type=MESH,
            ).start()
        self.phase = phase

    def land(self):
        whole = self.whole(self.phase)
        pltpu.make_async_copy(whole, whole, self.recvs.at[self.phase]).wait()

    def finish(self):
        for phase in range(self.done, self.phase + 1):
            whole = self.whole(phase)
            pltpu.make_async_copy(whole, whole, self.sends.at[phase]).wait()
        self.done = self.phase + 1

    def core_out(self):
        n = self.units // 2
        other = self.base + (1 - self.core) * n
        self.send(0, [(self.src.at[at(other, n)], self.core_in, core_peer())])

    def core_sum(self):
        n = self.units // 2
        mine = self.base + self.core * n

        def body(i, _):
            self.half[at(i * 16, 16)] = self.src[at(mine + i * 16, 16)] + self.core_in[at(i * 16, 16)]
            return 0

        lax.fori_loop(0, n // 16, body, 0)

    def scatter1(self):
        n = self.units // 16
        self.send(1, [
            (self.half.at[at(j * n, n)], self.in1.at[at(k * n, n)], to)
            for k, (to, j) in enumerate(self.groups[0][1])
        ])

    def sum1_(self):
        n = self.units // 16
        me = self.groups[0][0]

        total = self.half[at(me * n, n)]
        for k in range(7):
            total = total + self.in1[at(k * n, n)]
        self.sum1[...] = total

    def scatter2(self):
        n = self.units // 128
        self.send(2, [
            (self.sum1.at[at(j * n, n)], self.in2.at[at(k * n, n)], to)
            for k, (to, j) in enumerate(self.groups[1][1])
        ])

    def sum2_(self):
        n = self.units // 128
        me = self.groups[1][0]
        for i in range(n):
            total = self.sum1[at(me * n + i)]
            for k in range(7):
                total = total + self.in2[at(k * n + i)]
            self.out1[at(me * n + i)] = total

    def gather2(self):
        n = self.units // 128
        me = self.groups[1][0]
        mine = at(me * n, n)
        self.send(3, [(self.out1.at[mine], self.out1.at[mine], to) for to, j in self.groups[1][1]])

    def gather1(self):
        n = self.units // 16
        place = self.base + self.core * (self.units // 2) + self.groups[0][0] * n
        self.send(4, [(self.out1, self.res.at[at(place, n)], to) for to, j in self.groups[0][1]])
        self.res[at(place, n)] = self.out1[...]

    def core_back(self):
        n = self.units // 2
        mine = self.base + self.core * n
        self.send(5, [(self.res.at[at(mine, n)], self.res.at[at(mine, n)], core_peer())])

    def whole(self, phase):
        first, second = self.units // 16, self.units // 128
        if phase == 0:
            return self.core_in
        if phase == 5:
            return self.res.at[at(self.base, self.units // 2)]
        return (self.in1, self.in2, self.out1.at[at(0, 7 * second)], self.res.at[at(self.base, 7 * first)])[phase - 1]


class Relay:
    SEMS = 6

    def __init__(self, src, res, base, units, bufs, sends, recvs):
        self.src, self.res, self.base, self.units = src, res, base, units
        self.core_in, self.half, self.shares, self.stack, self.total = bufs
        self.sends, self.recvs = sends, recvs
        self.z, self.ring = z_peers()
        self.me, self.group = xy_peers()
        self.x, self.line = x_peers()
        self.core = coords()[3]
        self.done = 0

    @staticmethod
    def scratch(units):
        def block(n):
            return pltpu.VMEM((n * 8, LANES), F32)

        share = units // 16
        return [block(units // 2), block(units // 2), block(7 * share), block(2 * share), block(share)]

    send = Stream.send
    land = Stream.land
    finish = Stream.finish
    core_out = Stream.core_out
    core_sum = Stream.core_sum

    def scatter1(self):
        n = self.units // 16
        self.send(1, [
            (self.half.at[at(j * n, n)], self.shares.at[at(k * n, n)], to)
            for k, (to, j) in enumerate(self.ring)
        ])

    def scatter2(self):
        n, quarter = self.units // 16, self.units // 64
        total = self.half[at(self.z * n, n)]
        for k in range(7):
            total = total + self.shares[at(k * n, n)]
        self.half[at(self.z * n, n)] = total
        mine = at(self.me * quarter, quarter)
        self.stack[mine] = self.half[at(self.z * n + self.x * quarter, quarter)]
        self.send(2, [
            (self.half.at[at(self.z * n + lax.div(j, 2) * quarter, quarter)], self.stack.at[mine], to)
            for to, j in self.group
        ])

    def gather2(self):
        quarter = self.units // 64
        total = self.stack[at(0, quarter)]
        for k in range(1, 8):
            total = total + self.stack[at(k * quarter, quarter)]
        mine = at(self.x * quarter, quarter)
        self.total[mine] = total
        self.send(3, [(self.total.at[mine], self.total.at[mine], to) for to, j in self.line])

    def gather1(self):
        n = self.units // 16
        place = self.base + self.core * (self.units // 2) + self.z * n
        self.send(4, [(self.total, self.res.at[at(place, n)], to) for to, j in self.ring])
        self.res[at(place, n)] = self.total[...]

    def core_back(self):
        n = self.units // 2
        mine = at(self.base + self.core * n, n)
        self.send(5, [(self.res.at[mine], self.res.at[mine], core_peer())])

    def whole(self, phase):
        share, quarter = self.units // 16, self.units // 64
        if phase == 0:
            return self.core_in
        if phase == 5:
            return self.res.at[at(self.base, self.units // 2)]
        return (
            self.shares,
            self.stack.at[at(0, 7 * quarter)],
            self.total.at[at(0, 3 * quarter)],
            self.res.at[at(self.base, 7 * share)],
        )[phase - 1]


class Picture:
    SEMS = 3
    SHARE = ROWS // 16

    def __init__(self, src, res, base, bufs, sends, recvs):
        self.src, self.res, self.base = src, res, base
        self.shares, self.stack, self.total = bufs
        self.sends, self.recvs = sends, recvs
        self.me, self.group = flat_peers()
        self.z, self.ring = z_peers()
        self.done = 0

    @staticmethod
    def scratch():
        n = Picture.SHARE * 8
        return [
            pltpu.VMEM((15 * n, LANES), F32),
            pltpu.VMEM((8 * n, LANES), F32),
            pltpu.VMEM((n, LANES), F32),
        ]

    send = Stream.send
    land = Stream.land
    finish = Stream.finish

    def scatter(self):
        n = self.SHARE
        self.send(0, [
            (self.src.at[at(self.base + j * n, n)], self.shares.at[at(k * n, n)], to)
            for k, (to, j) in enumerate(self.group)
        ])

    def exchange(self):
        n = self.SHARE
        for i in range(n):
            total = self.src[at(self.base + self.me * n + i)]
            for k in range(15):
                total = total + self.shares[at(k * n + i)]
            self.stack[at(self.z * n + i)] = total
        mine = at(self.z * n, n)
        self.send(1, [(self.stack.at[mine], self.stack.at[mine], to) for to, j in self.ring])

    def gather(self):
        n = self.SHARE
        place = self.base + self.me * n
        for i in range(n):
            total = self.stack[at(i)]
            for k in range(1, 8):
                total = total + self.stack[at(k * n + i)]
            total = total * GAIN
            self.total[at(i)] = total
            self.res[at(place + i)] = total
        self.send(2, [(self.total, self.res.at[at(place, n)], to) for to, j in self.group])

    def whole(self, phase):
        n = self.SHARE
        return (self.shares, self.stack.at[at(0, 7 * n)], self.res.at[at(self.base, 15 * n)])[phase]


def spread(here):
    lane = lax.broadcasted_iota(jnp.int32, (8, LANES), 1)
    block = lax.broadcasted_iota(jnp.int32, (8, LANES), 0)
    above = jnp.where(block < 7, pltpu.roll(here, 7, 0), 0.0)
    below = jnp.where(block > 0, pltpu.roll(here, 1, 0), 0.0)
    out = []
    for b in range(1, 4):
        plus = pltpu.roll(jnp.where(lane < b, above, here), LANES - b, 1)
        minus = pltpu.roll(jnp.where(lane >= LANES - b, below, here), b, 1)
        out.append(plus + minus)
    return out


def spread_rows(field, pairs, first, count):
    def body(i, _):
        for c in range(4):
            for pair, value in zip(pairs, spread(field[c, at(first + i)])):
                pair[c, at(first + i)] = value
        return 0

    lax.fori_loop(0, count, body, 0, unroll=4 if count % 4 == 0 else count)


def plane_unit(step, array, t):
    if array == 2:
        return step * 192 + 128 + t * 8
    return step * 192 + lax.div(t, 4) * 64 + array * 32 + lax.rem(t, 4) * 8


def weights_of(planes, step, x, omega):
    t, s = lax.div(x, 8), lax.rem(x, 8)

    def row(array):
        start = plane_unit(step, array, t) * 8 + s
        both = [planes[pl.ds(start + i, 8, stride=8)] for i in range(2)]
        return jnp.concatenate(both, axis=0)

    turn = cis((0.5 * omega) * row(0))
    turn = square(turn)
    q, a = omega * row(1), omega * row(2)
    z = cis(q)
    u = a * a
    w1 = (1.0 + u * (-0.5 + u * (1.0 / 24.0)), a * (u * (1.0 / 6.0) - 1.0))
    w2 = square(w1)
    w4 = square(w2)
    w8 = square(w4)
    w16 = square(w8)
    w32 = square(w16)
    w64 = square(w32)
    w128 = square(w64)
    g = {}
    g[1] = mul(z, w1)
    g[2] = mul(square(g[1]), w2)
    g[4] = mul(square(g[2]), w8)
    g[8] = mul(square(g[4]), w32)
    g[5] = mul(mul(g[4], w8), g[1])
    g[9] = mul(mul(g[8], w16), g[1])
    w34 = mul(w32, w2)
    g[10] = mul(square(g[5]), mul(w34, w16))
    g[13] = mul(mul(g[9], g[4]), mul(w64, w8))
    g[18] = mul(square(g[9]), mul(w34, w128))
    return turn, g


def gathered(field, pairs, x, r, c):
    rows = [field] + list(pairs)
    total = None
    for a in range(4):
        for b in range(4):
            if a * a + b * b != r:
                continue
            for shift in sorted({a, -a}):
                piece = rows[b][c, at(x + HMAX + shift, 2)]
                total = piece if total is None else total + piece
    return total


def two_rows(sums, planes, coef, step, x, omega):
    turn, g = weights_of(planes, step, x, omega)
    first = coef[at(step * 20, 2)]
    acc = [first * sums(0, c) for c in range(4)]
    for index, r in enumerate(GROUPS):
        if r == 0:
            continue
        scale = coef[at(step * 20 + index * 2, 2)]
        wr, wi = g[r][0] * scale, g[r][1] * scale
        sr, si, rr, ri = [sums(r, c) for c in range(4)]
        acc[0] = acc[0] + (wr * sr - wi * si)
        acc[1] = acc[1] + (wr * si + wi * sr)
        acc[2] = acc[2] + (wr * rr + wi * ri)
        acc[3] = acc[3] + (wr * ri - wi * rr)
    tr, ti = turn
    return (
        tr * acc[0] - ti * acc[1],
        tr * acc[1] + ti * acc[0],
        tr * acc[2] + ti * acc[3],
        tr * acc[3] - ti * acc[2],
    )


PLANE_UNITS = STEPS * 3 * ROWS
IMAGE_UNITS = STEPS * ROWS


def kernel(
    omegas_in, numbers_in, source, receiver, velocity, epsilon, delta,
    source_out, receiver_out, image_out,
    omegas, numbers,
    raw_fields, raw_model, cand, planes, field0, field1, field2, pair1, pair2, pair3, next1, next2,
    next3, kept, coef, images, image_sum, load_sems, halo_sends, halo_recvs, *rest,
):
    sems, bufs = rest[:12], rest[12:]
    tile = lax.axis_index("tile")
    index = lax.axis_index("freq")
    neighbour = {"tile": 1 - tile}
    pairs, nexts = (pair1, pair2, pair3), (next1, next2, next3)

    barrier = pltpu.get_barrier_semaphore()
    greeted = all_peers() + [neighbour]
    for peer in greeted:
        pl.semaphore_signal(barrier, inc=1, device_id=peer, device_id_type=MESH)

    loads = []
    for i, array in enumerate((velocity, epsilon, delta)):
        loads.append(pltpu.make_async_copy(array, raw_model.at[i], load_sems.at[i]))
    for i, array in enumerate((source, receiver)):
        loads.append(pltpu.make_async_copy(array, raw_fields.at[i], load_sems.at[3 + i]))
    smalls = ((omegas_in, omegas), (numbers_in, numbers))
    for i, (array, place) in enumerate(smalls):
        loads.append(pltpu.make_async_copy(array, place, load_sems.at[5 + i]))
    for made in loads:
        made.start()

    a0 = Stream(cand, planes, 0, 128, ("xy", "z"), bufs[0:6], sems[0], sems[1])
    a1 = Stream(cand, planes, 192, 128, ("xy", "z"), bufs[6:12], sems[2], sems[3])
    b0 = Relay(cand, planes, 128, 64, bufs[12:17], sems[4], sems[5])
    b1 = Relay(cand, planes, 320, 64, bufs[17:22], sems[6], sems[7])
    p0 = Picture(images, image_sum, 0, bufs[22:25], sems[8], sems[9])
    p1 = Picture(images, image_sum, ROWS, bufs[25:28], sems[10], sems[11])

    for made in loads[:3] + loads[5:]:
        made.wait()
    omega = omegas[0]
    owner, reach = [numbers[i] for i in (0, 1)], [numbers[i] for i in (2, 3)]
    srows, scols = [numbers[4 + i] for i in range(4)], [numbers[8 + i] for i in range(4)]
    picks = []
    for step in range(STEPS):
        for slot in range(2):
            hit = owner[step] == index * 2 + slot
            picks.append(jnp.full((8, LANES), jnp.where(hit, 1.0, 0.0), F32))

    def candidate(t, _):
        for k in range(8):
            place = (pl.ds(pl.multiple_of(t * 8, 8), 8), pl.ds(k * LANES, LANES))
            forms = []
            for slot in range(2):
                v = raw_model[(0, slot) + place]
                e = raw_model[(1, slot) + place]
                d = raw_model[(2, slot) + place]
                wide = 1.0 + 2.0 * d
                both = 1.0 / (v * wide)
                slowness = both * wide
                stretch = both * v
                curve = 5.0 * slowness * stretch
                forms.append((10.0 * slowness, curve, curve * ((e - d) * stretch * 0.125)))
            for step in range(STEPS):
                for n in range(3):
                    value = picks[step * 2] * forms[0][n] + picks[step * 2 + 1] * forms[1][n]
                    cand[at(plane_unit(step, n, t) + k)] = value
        return 0

    lax.fori_loop(0, 8, candidate, 0)
    pl.semaphore_wait(barrier, len(greeted))

    for s in (a0, b0, a1, b1):
        s.core_out()

    for made in loads[3:5]:
        made.wait()
    zero = jnp.zeros((8, LANES), F32)
    for field in (field0, field1) + pairs + nexts:
        for i in range(HMAX):
            for c in range(4):
                field[c, at(67 * tile + i)] = zero
    delay = jnp.full((8, LANES), omega * 0.05, F32)
    pulse = (16.0 * jnp.cos(delay), -16.0 * jnp.sin(delay))

    def arrange(t, _):
        for c in range(4):
            for k in range(8):
                place = (pl.ds(pl.multiple_of(t * 8, 8), 8), pl.ds(k * LANES, LANES))
                value = raw_fields[(c // 2, c % 2, 0) + place]
                if c < 2:
                    row = lax.broadcasted_iota(jnp.int32, (8, LANES), 0) + (tile * ROWS + t * 8)
                    col = lax.broadcasted_iota(jnp.int32, (8, LANES), 1) + k * LANES
                    for s in range(4):
                        hit = (row == srows[s]) & (col == scols[s])
                        value = value + jnp.where(hit, pulse[c], 0.0)
                field0[c, pl.ds((t * 8 + HMAX) * 8 + k, 8, stride=8)] = value
        return 0

    def weights():
        for step in range(STEPS):
            live = [jnp.where(reach[step] >= n, t, 0.0) for n, t in zip(NEEDED, TAPERS)]
            total = live[0] * COUNTS[0]
            for n, w in zip(COUNTS[1:], live[1:]):
                total = total + w * n
            inverse = 1.0 / jnp.full((8, LANES), total, F32)
            for i, w in enumerate(live):
                coef[at(step * 20 + i * 2)] = inverse * w
                coef[at(step * 20 + i * 2 + 1)] = inverse * w

    def halo(field, slot):
        made = pltpu.make_async_remote_copy(
            src_ref=field.at[:, at(64 - 61 * tile, HMAX)],
            dst_ref=field.at[:, at(67 * tile, HMAX)],
            send_sem=halo_sends.at[slot],
            recv_sem=halo_recvs.at[slot],
            device_id=neighbour,
            device_id_type=MESH,
        )
        made.start()
        return made

    for s in (a0, b0):
        s.land()
        s.core_sum()
        s.scatter1()
    lax.fori_loop(0, 8, arrange, 0)
    halo0 = halo(field0, 0)
    for s in (a1, b1):
        s.land()
        s.core_sum()
        s.scatter1()
    a0.land()
    a0.sum1_()
    a0.scatter2()
    b0.land()
    b0.scatter2()
    weights()
    spread_rows(field0, pairs, HMAX, ROWS)
    a1.land()
    a1.sum1_()
    a1.scatter2()
    b1.land()
    b1.scatter2()
    halo0.wait()
    spread_rows(field0, pairs, 67 * (1 - tile), HMAX)
    a0.land()
    a0.sum2_()
    a0.gather2()
    b0.land()
    b0.gather2()
    a1.land()
    a1.sum2_()
    a1.gather2()
    b1.land()
    b1.gather2()
    for s in (a0, b0):
        s.land()
        s.gather1()
    for s in (a1, b1):
        s.land()
        s.gather1()

    def keep(i, _):
        for index, r in enumerate(GROUPS):
            for c in range(4):
                kept[index * 4 + c, at(i * 2, 2)] = gathered(field0, pairs, i * 2, r, c)
        return 0

    lax.fori_loop(0, ROWS // 2, keep, 0)
    for s in (a0, b0):
        s.land()
        s.core_back()

    core = coords()[3]

    def first_row(i):
        part = core + lax.div(i, 16) * (1 - 2 * core)
        return part * 32 + (1 - tile) * 30 + (2 * tile - 1) * (lax.rem(i, 16) * 2)

    def spread_done(i):
        place = first_row(i) + HMAX
        for c in range(4):
            for h in range(2):
                for pair, value in zip(nexts, spread(field1[c, at(place + h)])):
                    pair[c, at(place + h)] = value

    def first_pair(i, behind):
        x = first_row(i)
        out = two_rows(lambda r, c: kept[GROUPS.index(r) * 4 + c, at(x, 2)], planes, coef, 0, x, omega)
        if behind:
            spread_done(i - 1)
        for c in range(4):
            field1[c, at(x + HMAX, 2)] = out[c]
        images[at(x, 2)] = out[0] * out[2] + out[1] * out[3]

    def first_step(i, _):
        first_pair(i, True)
        return 0

    first_pair(0, False)
    lax.fori_loop(1, 16, first_step, 0)
    for s in (a0, b0):
        s.land()
    for s in (a1, b1):
        s.land()
        s.core_back()
    lax.fori_loop(16, 18, first_step, 0)
    halo1 = halo(field1, 1)
    lax.fori_loop(18, ROWS // 2, first_step, 0)
    p0.scatter()
    spread_done(ROWS // 2 - 1)
    a1.land()
    b1.land()

    def second_step(i, _):
        x = tile * (ROWS - 2) + (1 - 2 * tile) * (i * 2)
        out = two_rows(lambda r, c: gathered(field1, nexts, x, r, c), planes, coef, 1, x, omega)
        for c in range(4):
            field2[c, at(x, 2)] = out[c]
        images[at(ROWS + x, 2)] = out[0] * out[2] + out[1] * out[3]
        return 0

    lax.fori_loop(0, 30, second_step, 0)
    halo1.wait()
    spread_rows(field1, nexts, 67 * (1 - tile), HMAX)
    lax.fori_loop(30, ROWS // 2, second_step, 0)
    p1.scatter()
    p0.land()
    p0.exchange()

    def restore(t, _):
        for c in range(4):
            for k in range(8):
                place = (pl.ds(pl.multiple_of(t * 8, 8), 8), pl.ds(k * LANES, LANES))
                out = (source_out, receiver_out)[c // 2]
                out[(c % 2, 0) + place] = field2[
                    c, pl.ds(t * 64 + k, 8, stride=8)
                ]
        return 0

    def picture(step):
        def body(t, _):
            for k in range(8):
                place = (pl.ds(pl.multiple_of(t * 8, 8), 8), pl.ds(k * LANES, LANES))
                image_out[(step,) + place] = image_sum[pl.ds(step * 512 + t * 64 + k, 8, stride=8)]
            return 0

        return body

    lax.fori_loop(0, 8, restore, 0)
    for s in (a0, b0, a1, b1):
        s.finish()
    p1.land()
    p1.exchange()
    p0.land()
    p0.gather()
    p1.land()
    p1.gather()
    p0.finish()
    p0.land()
    lax.fori_loop(0, 8, picture(0), 0)
    p1.finish()
    p1.land()
    lax.fori_loop(0, 8, picture(1), 0)


def hand_over(*refs):
    sems = refs[6]
    stores = [
        pltpu.make_async_copy(refs[i].at[h], refs[3 + i].at[h], sems.at[i * 2 + h])
        for i in range(3)
        for h in range(2)
    ]
    for made in stores:
        made.start()
    for made in stores:
        made.wait()


def per_device(*args):
    source, receiver, omegas, velocity, epsilon, delta, owner, reach, srows, scols = args
    hbm = pl.BlockSpec(memory_space=pl.ANY)
    out_shape = (
        jax.ShapeDtypeStruct(source.shape, F32),
        jax.ShapeDtypeStruct(receiver.shape, F32),
        jax.ShapeDtypeStruct((STEPS, ROWS, 1024), F32),
    )

    def block(n):
        return pltpu.VMEM((n * 8, LANES), F32)

    def plane(n):
        return pltpu.VMEM((4, n * 8, LANES), F32)

    def small(array):
        return pltpu.SMEM(array.shape, array.dtype)

    numbers = jnp.concatenate([owner[:2], reach, srows, scols])
    counts = [Stream.SEMS] * 4 + [Relay.SEMS] * 4 + [Picture.SEMS] * 4
    made = pl.pallas_call(
        kernel,
        out_shape=out_shape,
        in_specs=[hbm] * 7,
        out_specs=tuple([pl.BlockSpec(memory_space=pltpu.VMEM)] * 3),
        scratch_shapes=[small(array) for array in (omegas, numbers)]
        + [
            pltpu.VMEM((2, 2, 1, ROWS, 1024), F32),
            pltpu.VMEM((3, 2, ROWS, 1024), F32),
            block(PLANE_UNITS),
            block(PLANE_UNITS),
            plane(TALL),
            plane(TALL),
            plane(ROWS),
        ]
        + [plane(TALL)] * 6
        + [
            pltpu.VMEM((4 * len(GROUPS), ROWS * 8, LANES), F32),
            block(40),
            block(IMAGE_UNITS),
            block(IMAGE_UNITS),
            pltpu.SemaphoreType.DMA((10,)),
            pltpu.SemaphoreType.DMA((2,)),
            pltpu.SemaphoreType.DMA((2,)),
        ]
        + [pltpu.SemaphoreType.DMA((n,)) for n in counts]
        + Stream.scratch(128) * 2
        + Relay.scratch(64) * 2
        + Picture.scratch() * 2,
        compiler_params=pltpu.CompilerParams(
            collective_id=0, has_side_effects=True, vmem_limit_bytes=52 << 20
        ),
        name="migrate",
    )(omegas, numbers, source, receiver, velocity, epsilon, delta)
    return pl.pallas_call(
        hand_over,
        out_shape=out_shape,
        in_specs=[pl.BlockSpec(memory_space=pltpu.VMEM)] * 3,
        out_specs=(hbm, hbm, hbm),
        scratch_shapes=[pltpu.SemaphoreType.DMA((6,))],
        compiler_params=pltpu.CompilerParams(vmem_limit_bytes=52 << 20),
        name="hand_over",
    )(*made)


def solution(mesh):
    in_specs = (
        P(None, "freq", "tile", None),
        P(None, "freq", "tile", None),
        P("freq"),
        P("freq", "tile", None),
        P("freq", "tile", None),
        P("freq", "tile", None),
        P(),
        P(),
        P(),
        P(),
    )
    out_specs = (
        P(None, "freq", "tile", None),
        P(None, "freq", "tile", None),
        P(None, "tile", None),
    )
    return jax.shard_map(
        per_device, mesh=mesh, in_specs=in_specs, out_specs=out_specs, check_vma=False
    )
```

```python
import math

import jax
import jax.numpy as jnp
import numpy as np
from jax import lax
from jax.experimental import pallas as pl
from jax.experimental.pallas import tpu as pltpu
from jax.sharding import PartitionSpec as P

STEPS = 2
HMAX = 3
ROWS = 64
TALL = ROWS + 2 * HMAX
LANES = 128
GAIN = 16.0 / math.sqrt(128.0)
MESH = pl.DeviceIdType.MESH
F32 = jnp.float32


def _minimax(fn, high, degree, weight):
    count = 2000
    nodes = high / 2 + high / 2 * np.cos(np.pi * (np.arange(count) + 0.5) / count)
    target, scale = fn(nodes), weight(nodes)
    table = np.vander(nodes, degree + 1, increasing=True)
    bias = np.ones(count)
    best, least = None, np.inf
    for _ in range(60):
        coefs = np.linalg.lstsq(table * (bias * scale)[:, None], target * bias * scale, rcond=None)[0]
        error = np.abs((table @ coefs - target) * scale)
        if error.max() < least:
            best, least = coefs, error.max()
        bias = bias * (error / error.max() + 1e-3) ** 0.3
        bias = bias / bias.max()
    return tuple(float(np.float32(c)) for c in best)


REACH_SQ = 1.6 * 1.6
SIN = _minimax(lambda u: np.sin(np.sqrt(u)) / np.sqrt(u), REACH_SQ, 4, np.sqrt)
COS = _minimax(lambda u: np.cos(np.sqrt(u)), REACH_SQ, 4, np.ones_like)

GROUPS = sorted({a * a + b * b for a in range(4) for b in range(4)})
COUNTS = [
    sum(1 for a in range(-3, 4) for b in range(-3, 4) if a * a + b * b == r) for r in GROUPS
]
NEEDED = [
    max(max(a, b) for a in range(4) for b in range(4) if a * a + b * b == r) for r in GROUPS
]
TAPERS = [float(np.float32(math.exp(-r / 4.0))) for r in GROUPS]


def at(unit, count=1):
    return pl.ds(pl.multiple_of(unit * 8, 8), count * 8)


def horner(u, coefs):
    value = coefs[-1] * u + coefs[-2]
    for c in coefs[-3::-1]:
        value = value * u + c
    return value


def cis(x):
    u = x * x
    return horner(u, COS), x * horner(u, SIN)


def mul(a, b):
    return a[0] * b[0] - a[1] * b[1], a[0] * b[1] + a[1] * b[0]


def square(a):
    twice = a[1] + a[1]
    return 1.0 - a[1] * twice, a[0] * twice


def coords():
    f = lax.axis_index("freq")
    return lax.div(f, 16), lax.rem(lax.div(f, 4), 4), lax.rem(lax.div(f, 2), 2), lax.rem(f, 2)


def device(z, x, y, c):
    return {"freq": ((z * 4 + x) * 2 + y) * 2 + c}


def xy_peers():
    z, x, y, c = coords()
    out = []
    for k in (5, 4, 3, 7, 2, 6, 1):
        px, py = lax.rem(x + k // 2, 4), lax.rem(y + k % 2, 2)
        out.append((device(z, px, py, c), px * 2 + py))
    return x * 2 + y, out


def z_peers():
    z, x, y, c = coords()
    return z, [(device(lax.rem(z + k, 8), x, y, c), lax.rem(z + k, 8)) for k in (4, 3, 5, 2, 6, 1, 7)]


def x_peers():
    z, x, y, c = coords()
    return x, [(device(z, lax.rem(x + k, 4), y, c), lax.rem(x + k, 4)) for k in (2, 1, 3)]


def flat_peers():
    z, x, y, c = coords()
    out = []
    for k in (10, 11, 8, 9, 6, 7, 14, 15, 4, 5, 12, 13, 2, 3, 1):
        px, py, pc = lax.rem(x + k // 4, 4), lax.rem(y + k // 2 % 2, 2), lax.rem(c + k % 2, 2)
        out.append((device(z, px, py, pc), px * 4 + py * 2 + pc))
    return x * 4 + y * 2 + c, out


def core_peer():
    z, x, y, c = coords()
    return device(z, x, y, 1 - c)


def all_peers():
    return [d for d, _ in z_peers()[1]] + [d for d, _ in flat_peers()[1]]


class Stream:
    SEMS = 6

    def __init__(self, src, res, base, units, order, bufs, sends, recvs):
        self.src, self.res, self.base, self.units = src, res, base, units
        self.core_in, self.half, self.in1, self.sum1, self.in2, self.out1 = bufs
        self.sends, self.recvs = sends, recvs
        self.groups = [xy_peers() if o == "xy" else z_peers() for o in order]
        self.core = coords()[3]
        self.done = 0

    @staticmethod
    def scratch(units):
        def block(n):
            return pltpu.VMEM((n * 8, LANES), F32)

        return [
            block(units // 2),
            block(units // 2),
            block(7 * units // 16),
            block(units // 16),
            block(7 * units // 128),
            block(units // 16),
        ]

    def send(self, phase, parts):
        for src, dst, to in parts:
            pltpu.make_async_remote_copy(
                src_ref=src,
                dst_ref=dst,
                send_sem=self.sends.at[phase],
                recv_sem=self.recvs.at[phase],
                device_id=to,
                device_id_type=MESH,
            ).start()
        self.phase = phase

    def land(self):
        whole = self.whole(self.phase)
        pltpu.make_async_copy(whole, whole, self.recvs.at[self.phase]).wait()

    def finish(self):
        for phase in range(self.done, self.phase + 1):
            whole = self.whole(phase)
            pltpu.make_async_copy(whole, whole, self.sends.at[phase]).wait()
        self.done = self.phase + 1

    def core_out(self):
        n = self.units // 2
        other = self.base + (1 - self.core) * n
        self.send(0, [(self.src.at[at(other, n)], self.core_in, core_peer())])

    def core_sum(self):
        n = self.units // 2
        mine = self.base + self.core * n

        def body(i, _):
            self.half[at(i * 16, 16)] = self.src[at(mine + i * 16, 16)] + self.core_in[at(i * 16, 16)]
            return 0

        lax.fori_loop(0, n // 16, body, 0)

    def scatter1(self):
        n = self.units // 16
        self.send(1, [
            (self.half.at[at(j * n, n)], self.in1.at[at(k * n, n)], to)
            for k, (to, j) in enumerate(self.groups[0][1])
        ])

    def sum1_(self):
        n = self.units // 16
        me = self.groups[0][0]

        total = self.half[at(me * n, n)]
        for k in range(7):
            total = total + self.in1[at(k * n, n)]
        self.sum1[...] = total

    def scatter2(self):
        n = self.units // 128
        self.send(2, [
            (self.sum1.at[at(j * n, n)], self.in2.at[at(k * n, n)], to)
            for k, (to, j) in enumerate(self.groups[1][1])
        ])

    def sum2_(self):
        n = self.units // 128
        me = self.groups[1][0]
        for i in range(n):
            total = self.sum1[at(me * n + i)]
            for k in range(7):
                total = total + self.in2[at(k * n + i)]
            self.out1[at(me * n + i)] = total

    def gather2(self):
        n = self.units // 128
        me = self.groups[1][0]
        mine = at(me * n, n)
        self.send(3, [(self.out1.at[mine], self.out1.at[mine], to) for to, j in self.groups[1][1]])

    def gather1(self):
        n = self.units // 16
        place = self.base + self.core * (self.units // 2) + self.groups[0][0] * n
        self.send(4, [(self.out1, self.res.at[at(place, n)], to) for to, j in self.groups[0][1]])
        self.res[at(place, n)] = self.out1[...]

    def core_back(self):
        n = self.units // 2
        mine = self.base + self.core * n
        self.send(5, [(self.res.at[at(mine, n)], self.res.at[at(mine, n)], core_peer())])

    def whole(self, phase):
        first, second = self.units // 16, self.units // 128
        if phase == 0:
            return self.core_in
        if phase == 5:
            return self.res.at[at(self.base, self.units // 2)]
        return (self.in1, self.in2, self.out1.at[at(0, 7 * second)], self.res.at[at(self.base, 7 * first)])[phase - 1]


class Relay:
    SEMS = 6

    def __init__(self, src, res, base, units, bufs, sends, recvs):
        self.src, self.res, self.base, self.units = src, res, base, units
        self.core_in, self.half, self.shares, self.stack, self.total = bufs
        self.sends, self.recvs = sends, recvs
        self.z, self.ring = z_peers()
        self.me, self.group = xy_peers()
        self.x, self.line = x_peers()
        self.core = coords()[3]
        self.done = 0

    @staticmethod
    def scratch(units):
        def block(n):
            return pltpu.VMEM((n * 8, LANES), F32)

        share = units // 16
        return [block(units // 2), block(units // 2), block(7 * share), block(2 * share), block(share)]

    send = Stream.send
    land = Stream.land
    finish = Stream.finish
    core_out = Stream.core_out
    core_sum = Stream.core_sum

    def scatter1(self):
        n = self.units // 16
        self.send(1, [
            (self.half.at[at(j * n, n)], self.shares.at[at(k * n, n)], to)
            for k, (to, j) in enumerate(self.ring)
        ])

    def scatter2(self):
        n, quarter = self.units // 16, self.units // 64
        total = self.half[at(self.z * n, n)]
        for k in range(7):
            total = total + self.shares[at(k * n, n)]
        self.half[at(self.z * n, n)] = total
        mine = at(self.me * quarter, quarter)
        self.stack[mine] = self.half[at(self.z * n + self.x * quarter, quarter)]
        self.send(2, [
            (self.half.at[at(self.z * n + lax.div(j, 2) * quarter, quarter)], self.stack.at[mine], to)
            for to, j in self.group
        ])

    def gather2(self):
        quarter = self.units // 64
        total = self.stack[at(0, quarter)]
        for k in range(1, 8):
            total = total + self.stack[at(k * quarter, quarter)]
        mine = at(self.x * quarter, quarter)
        self.total[mine] = total
        self.send(3, [(self.total.at[mine], self.total.at[mine], to) for to, j in self.line])

    def gather1(self):
        n = self.units // 16
        place = self.base + self.core * (self.units // 2) + self.z * n
        self.send(4, [(self.total, self.res.at[at(place, n)], to) for to, j in self.ring])
        self.res[at(place, n)] = self.total[...]

    def core_back(self):
        n = self.units // 2
        mine = at(self.base + self.core * n, n)
        self.send(5, [(self.res.at[mine], self.res.at[mine], core_peer())])

    def whole(self, phase):
        share, quarter = self.units // 16, self.units // 64
        if phase == 0:
            return self.core_in
        if phase == 5:
            return self.res.at[at(self.base, self.units // 2)]
        return (
            self.shares,
            self.stack.at[at(0, 7 * quarter)],
            self.total.at[at(0, 3 * quarter)],
            self.res.at[at(self.base, 7 * share)],
        )[phase - 1]


class Picture:
    SEMS = 3
    SHARE = ROWS // 16

    def __init__(self, src, res, base, bufs, sends, recvs):
        self.src, self.res, self.base = src, res, base
        self.shares, self.stack, self.total = bufs
        self.sends, self.recvs = sends, recvs
        self.me, self.group = flat_peers()
        self.z, self.ring = z_peers()
        self.done = 0

    @staticmethod
    def scratch():
        n = Picture.SHARE * 8
        return [
            pltpu.VMEM((15 * n, LANES), F32),
            pltpu.VMEM((8 * n, LANES), F32),
            pltpu.VMEM((n, LANES), F32),
        ]

    send = Stream.send
    land = Stream.land
    finish = Stream.finish

    def scatter(self):
        n = self.SHARE
        self.send(0, [
            (self.src.at[at(self.base + j * n, n)], self.shares.at[at(k * n, n)], to)
            for k, (to, j) in enumerate(self.group)
        ])

    def exchange(self):
        n = self.SHARE
        for i in range(n):
            total = self.src[at(self.base + self.me * n + i)]
            for k in range(15):
                total = total + self.shares[at(k * n + i)]
            self.stack[at(self.z * n + i)] = total
        mine = at(self.z * n, n)
        self.send(1, [(self.stack.at[mine], self.stack.at[mine], to) for to, j in self.ring])

    def gather(self):
        n = self.SHARE
        place = self.base + self.me * n
        for i in range(n):
            total = self.stack[at(i)]
            for k in range(1, 8):
                total = total + self.stack[at(k * n + i)]
            total = total * GAIN
            self.total[at(i)] = total
            self.res[at(place + i)] = total
        self.send(2, [(self.total, self.res.at[at(place, n)], to) for to, j in self.group])

    def whole(self, phase):
        n = self.SHARE
        return (self.shares, self.stack.at[at(0, 7 * n)], self.res.at[at(self.base, 15 * n)])[phase]


def spread(here):
    lane = lax.broadcasted_iota(jnp.int32, (8, LANES), 1)
    block = lax.broadcasted_iota(jnp.int32, (8, LANES), 0)
    above = jnp.where(block < 7, pltpu.roll(here, 7, 0), 0.0)
    below = jnp.where(block > 0, pltpu.roll(here, 1, 0), 0.0)
    out = []
    for b in range(1, 4):
        plus = pltpu.roll(jnp.where(lane < b, above, here), LANES - b, 1)
        minus = pltpu.roll(jnp.where(lane >= LANES - b, below, here), b, 1)
        out.append(plus + minus)
    return out


def spread_rows(field, pairs, first, count):
    def body(i, _):
        for c in range(4):
            for pair, value in zip(pairs, spread(field[c, at(first + i)])):
                pair[c, at(first + i)] = value
        return 0

    lax.fori_loop(0, count, body, 0, unroll=4 if count % 4 == 0 else count)


def plane_unit(step, array, t):
    if array == 2:
        return step * 192 + 128 + t * 8
    return step * 192 + lax.div(t, 4) * 64 + array * 32 + lax.rem(t, 4) * 8


def weights_of(planes, step, x, omega):
    t, s = lax.div(x, 8), lax.rem(x, 8)

    def row(array):
        start = plane_unit(step, array, t) * 8 + s
        both = [planes[pl.ds(start + i, 8, stride=8)] for i in range(2)]
        return jnp.concatenate(both, axis=0)

    turn = cis((0.5 * omega) * row(0))
    turn = square(turn)
    q, a = omega * row(1), omega * row(2)
    z = cis(q)
    u = a * a
    w1 = (1.0 + u * (-0.5 + u * (1.0 / 24.0)), a * (u * (1.0 / 6.0) - 1.0))
    w2 = square(w1)
    w4 = square(w2)
    w8 = square(w4)
    w16 = square(w8)
    w32 = square(w16)
    w64 = square(w32)
    w128 = square(w64)
    g = {}
    g[1] = mul(z, w1)
    g[2] = mul(square(g[1]), w2)
    g[4] = mul(square(g[2]), w8)
    g[8] = mul(square(g[4]), w32)
    g[5] = mul(mul(g[4], w8), g[1])
    g[9] = mul(mul(g[8], w16), g[1])
    w34 = mul(w32, w2)
    g[10] = mul(square(g[5]), mul(w34, w16))
    g[13] = mul(mul(g[9], g[4]), mul(w64, w8))
    g[18] = mul(square(g[9]), mul(w34, w128))
    return turn, g


def gathered(field, pairs, x, r, c):
    rows = [field] + list(pairs)
    total = None
    for a in range(4):
        for b in range(4):
            if a * a + b * b != r:
                continue
            for shift in sorted({a, -a}):
                piece = rows[b][c, at(x + HMAX + shift, 2)]
                total = piece if total is None else total + piece
    return total


def two_rows(sums, planes, coef, step, x, omega):
    turn, g = weights_of(planes, step, x, omega)
    first = coef[at(step * 20, 2)]
    acc = [first * sums(0, c) for c in range(4)]
    for index, r in enumerate(GROUPS):
        if r == 0:
            continue
        scale = coef[at(step * 20 + index * 2, 2)]
        wr, wi = g[r][0] * scale, g[r][1] * scale
        sr, si, rr, ri = [sums(r, c) for c in range(4)]
        acc[0] = acc[0] + (wr * sr - wi * si)
        acc[1] = acc[1] + (wr * si + wi * sr)
        acc[2] = acc[2] + (wr * rr + wi * ri)
        acc[3] = acc[3] + (wr * ri - wi * rr)
    tr, ti = turn
    return (
        tr * acc[0] - ti * acc[1],
        tr * acc[1] + ti * acc[0],
        tr * acc[2] + ti * acc[3],
        tr * acc[3] - ti * acc[2],
    )


PLANE_UNITS = STEPS * 3 * ROWS
IMAGE_UNITS = STEPS * ROWS


def kernel(
    omegas_in, numbers_in, source, receiver, velocity, epsilon, delta,
    source_out, receiver_out, image_out,
    omegas, numbers,
    raw_fields, raw_model, cand, planes, field0, field1, field2, pair1, pair2, pair3, next1, next2,
    next3, kept, coef, images, image_sum, load_sems, halo_sends, halo_recvs, *rest,
):
    sems, bufs = rest[:12], rest[12:]
    tile = lax.axis_index("tile")
    index = lax.axis_index("freq")
    neighbour = {"tile": 1 - tile}
    pairs, nexts = (pair1, pair2, pair3), (next1, next2, next3)

    barrier = pltpu.get_barrier_semaphore()
    greeted = all_peers() + [neighbour]
    for peer in greeted:
        pl.semaphore_signal(barrier, inc=1, device_id=peer, device_id_type=MESH)

    loads = []
    for i, array in enumerate((velocity, epsilon, delta)):
        loads.append(pltpu.make_async_copy(array, raw_model.at[i], load_sems.at[i]))
    for i, array in enumerate((source, receiver)):
        loads.append(pltpu.make_async_copy(array, raw_fields.at[i], load_sems.at[3 + i]))
    smalls = ((omegas_in, omegas), (numbers_in, numbers))
    for i, (array, place) in enumerate(smalls):
        loads.append(pltpu.make_async_copy(array, place, load_sems.at[5 + i]))
    for made in loads:
        made.start()

    a0 = Stream(cand, planes, 0, 128, ("xy", "z"), bufs[0:6], sems[0], sems[1])
    a1 = Stream(cand, planes, 192, 128, ("xy", "z"), bufs[6:12], sems[2], sems[3])
    b0 = Relay(cand, planes, 128, 64, bufs[12:17], sems[4], sems[5])
    b1 = Relay(cand, planes, 320, 64, bufs[17:22], sems[6], sems[7])
    p0 = Picture(images, image_sum, 0, bufs[22:25], sems[8], sems[9])
    p1 = Picture(images, image_sum, ROWS, bufs[25:28], sems[10], sems[11])

    for made in loads[:3] + loads[5:]:
        made.wait()
    omega = omegas[0]
    owner, reach = [numbers[i] for i in (0, 1)], [numbers[i] for i in (2, 3)]
    srows, scols = [numbers[4 + i] for i in range(4)], [numbers[8 + i] for i in range(4)]
    picks = []
    for step in range(STEPS):
        for slot in range(2):
            hit = owner[step] == index * 2 + slot
            picks.append(jnp.full((8, LANES), jnp.where(hit, 1.0, 0.0), F32))

    def candidate(t, _):
        for k in range(8):
            place = (pl.ds(pl.multiple_of(t * 8, 8), 8), pl.ds(k * LANES, LANES))
            forms = []
            for slot in range(2):
                v = raw_model[(0, slot) + place]
                e = raw_model[(1, slot) + place]
                d = raw_model[(2, slot) + place]
                wide = 1.0 + 2.0 * d
                both = 1.0 / (v * wide)
                slowness = both * wide
                stretch = both * v
                curve = 5.0 * slowness * stretch
                forms.append((10.0 * slowness, curve, curve * ((e - d) * stretch * 0.125)))
            for step in range(STEPS):
                for n in range(3):
                    value = picks[step * 2] * forms[0][n] + picks[step * 2 + 1] * forms[1][n]
                    cand[at(plane_unit(step, n, t) + k)] = value
        return 0

    lax.fori_loop(0, 8, candidate, 0)
    pl.semaphore_wait(barrier, len(greeted))

    for s in (a0, b0, a1, b1):
        s.core_out()

    for made in loads[3:5]:
        made.wait()
    zero = jnp.zeros((8, LANES), F32)
    for field in (field0, field1) + pairs + nexts:
        for i in range(HMAX):
            for c in range(4):
                field[c, at(67 * tile + i)] = zero
    delay = jnp.full((8, LANES), omega * 0.05, F32)
    pulse = (16.0 * jnp.cos(delay), -16.0 * jnp.sin(delay))

    def arrange(t, _):
        for c in range(4):
            for k in range(8):
                place = (pl.ds(pl.multiple_of(t * 8, 8), 8), pl.ds(k * LANES, LANES))
                value = raw_fields[(c // 2, c % 2, 0) + place]
                if c < 2:
                    row = lax.broadcasted_iota(jnp.int32, (8, LANES), 0) + (tile * ROWS + t * 8)
                    col = lax.broadcasted_iota(jnp.int32, (8, LANES), 1) + k * LANES
                    for s in range(4):
                        hit = (row == srows[s]) & (col == scols[s])
                        value = value + jnp.where(hit, pulse[c], 0.0)
                field0[c, pl.ds((t * 8 + HMAX) * 8 + k, 8, stride=8)] = value
        return 0

    def weights():
        for step in range(STEPS):
            live = [jnp.where(reach[step] >= n, t, 0.0) for n, t in zip(NEEDED, TAPERS)]
            total = live[0] * COUNTS[0]
            for n, w in zip(COUNTS[1:], live[1:]):
                total = total + w * n
            inverse = 1.0 / jnp.full((8, LANES), total, F32)
            for i, w in enumerate(live):
                coef[at(step * 20 + i * 2)] = inverse * w
                coef[at(step * 20 + i * 2 + 1)] = inverse * w

    def halo(field, slot):
        made = pltpu.make_async_remote_copy(
            src_ref=field.at[:, at(64 - 61 * tile, HMAX)],
            dst_ref=field.at[:, at(67 * tile, HMAX)],
            send_sem=halo_sends.at[slot],
            recv_sem=halo_recvs.at[slot],
            device_id=neighbour,
            device_id_type=MESH,
        )
        made.start()
        return made

    for s in (a0, b0):
        s.land()
        s.core_sum()
        s.scatter1()
    lax.fori_loop(0, 8, arrange, 0)
    halo0 = halo(field0, 0)
    for s in (a1, b1):
        s.land()
        s.core_sum()
        s.scatter1()
    a0.land()
    a0.sum1_()
    a0.scatter2()
    b0.land()
    b0.scatter2()
    weights()
    spread_rows(field0, pairs, HMAX, ROWS)
    a1.land()
    a1.sum1_()
    a1.scatter2()
    b1.land()
    b1.scatter2()
    halo0.wait()
    spread_rows(field0, pairs, 67 * (1 - tile), HMAX)
    a0.land()
    a0.sum2_()
    a0.gather2()
    b0.land()
    b0.gather2()
    a1.land()
    a1.sum2_()
    a1.gather2()
    b1.land()
    b1.gather2()
    for s in (a0, b0):
        s.land()
        s.gather1()
    for s in (a1, b1):
        s.land()
        s.gather1()

    def keep(i, _):
        for index, r in enumerate(GROUPS):
            for c in range(4):
                kept[index * 4 + c, at(i * 2, 2)] = gathered(field0, pairs, i * 2, r, c)
        return 0

    lax.fori_loop(0, ROWS // 2, keep, 0)
    for s in (a0, b0):
        s.land()
        s.core_back()

    core = coords()[3]

    def first_row(i):
        part = core + lax.div(i, 16) * (1 - 2 * core)
        return part * 32 + (1 - tile) * 30 + (2 * tile - 1) * (lax.rem(i, 16) * 2)

    def spread_done(i):
        place = first_row(i) + HMAX
        for c in range(4):
            for h in range(2):
                for pair, value in zip(nexts, spread(field1[c, at(place + h)])):
                    pair[c, at(place + h)] = value

    def first_pair(i, behind):
        x = first_row(i)
        out = two_rows(lambda r, c: kept[GROUPS.index(r) * 4 + c, at(x, 2)], planes, coef, 0, x, omega)
        if behind:
            spread_done(i - 1)
        for c in range(4):
            field1[c, at(x + HMAX, 2)] = out[c]
        images[at(x, 2)] = out[0] * out[2] + out[1] * out[3]

    def first_step(i, _):
        first_pair(i, True)
        return 0

    first_pair(0, False)
    lax.fori_loop(1, 16, first_step, 0)
    for s in (a0, b0):
        s.land()
    for s in (a1, b1):
        s.land()
        s.core_back()
    lax.fori_loop(16, 18, first_step, 0)
    halo1 = halo(field1, 1)
    lax.fori_loop(18, ROWS // 2, first_step, 0)
    p0.scatter()
    spread_done(ROWS // 2 - 1)
    a1.land()
    b1.land()

    def second_step(i, _):
        x = tile * (ROWS - 2) + (1 - 2 * tile) * (i * 2)
        out = two_rows(lambda r, c: gathered(field1, nexts, x, r, c), planes, coef, 1, x, omega)
        for c in range(4):
            field2[c, at(x, 2)] = out[c]
        images[at(ROWS + x, 2)] = out[0] * out[2] + out[1] * out[3]
        return 0

    lax.fori_loop(0, 30, second_step, 0)
    halo1.wait()
    spread_rows(field1, nexts, 67 * (1 - tile), HMAX)
    lax.fori_loop(30, ROWS // 2, second_step, 0)
    p1.scatter()
    p0.land()
    p0.exchange()

    def restore(t, _):
        for c in range(4):
            for k in range(8):
                place = (pl.ds(pl.multiple_of(t * 8, 8), 8), pl.ds(k * LANES, LANES))
                out = (source_out, receiver_out)[c // 2]
                out[(c % 2, 0) + place] = field2[
                    c, pl.ds(t * 64 + k, 8, stride=8)
                ]
        return 0

    def picture(step):
        def body(t, _):
            for k in range(8):
                place = (pl.ds(pl.multiple_of(t * 8, 8), 8), pl.ds(k * LANES, LANES))
                image_out[(step,) + place] = image_sum[pl.ds(step * 512 + t * 64 + k, 8, stride=8)]
            return 0

        return body

    lax.fori_loop(0, 8, restore, 0)
    for s in (a0, b0, a1, b1):
        s.finish()
    p1.land()
    p1.exchange()
    p0.land()
    p0.gather()
    p1.land()
    p1.gather()
    p0.finish()
    p0.land()
    lax.fori_loop(0, 8, picture(0), 0)
    p1.finish()
    p1.land()
    lax.fori_loop(0, 8, picture(1), 0)


def hand_over(*refs):
    sems = refs[6]
    stores = [
        pltpu.make_async_copy(refs[i].at[h], refs[3 + i].at[h], sems.at[i * 2 + h])
        for i in range(3)
        for h in range(2)
    ]
    for made in stores:
        made.start()
    for made in stores:
        made.wait()


def per_device(*args):
    source, receiver, omegas, velocity, epsilon, delta, owner, reach, srows, scols = args
    hbm = pl.BlockSpec(memory_space=pl.ANY)
    out_shape = (
        jax.ShapeDtypeStruct(source.shape, F32),
        jax.ShapeDtypeStruct(receiver.shape, F32),
        jax.ShapeDtypeStruct((STEPS, ROWS, 1024), F32),
    )

    def block(n):
        return pltpu.VMEM((n * 8, LANES), F32)

    def plane(n):
        return pltpu.VMEM((4, n * 8, LANES), F32)

    def small(array):
        return pltpu.SMEM(array.shape, array.dtype)

    numbers = jnp.concatenate([owner[:2], reach, srows, scols])
    counts = [Stream.SEMS] * 4 + [Relay.SEMS] * 4 + [Picture.SEMS] * 4
    made = pl.pallas_call(
        kernel,
        out_shape=out_shape,
        in_specs=[hbm] * 7,
        out_specs=tuple([pl.BlockSpec(memory_space=pltpu.VMEM)] * 3),
        scratch_shapes=[small(array) for array in (omegas, numbers)]
        + [
            pltpu.VMEM((2, 2, 1, ROWS, 1024), F32),
            pltpu.VMEM((3, 2, ROWS, 1024), F32),
            block(PLANE_UNITS),
            block(PLANE_UNITS + 1),
            plane(TALL),
            plane(TALL),
            plane(ROWS + 1),
        ]
        + [plane(TALL)] * 6
        + [
            pltpu.VMEM((4 * len(GROUPS), ROWS * 8, LANES), F32),
            block(40),
            block(IMAGE_UNITS),
            block(IMAGE_UNITS + 1),
            pltpu.SemaphoreType.DMA((10,)),
            pltpu.SemaphoreType.DMA((2,)),
            pltpu.SemaphoreType.DMA((2,)),
        ]
        + [pltpu.SemaphoreType.DMA((n,)) for n in counts]
        + Stream.scratch(128) * 2
        + Relay.scratch(64) * 2
        + Picture.scratch() * 2,
        compiler_params=pltpu.CompilerParams(
            collective_id=0, has_side_effects=True, vmem_limit_bytes=52 << 20
        ),
        name="migrate",
    )(omegas, numbers, source, receiver, velocity, epsilon, delta)
    return pl.pallas_call(
        hand_over,
        out_shape=out_shape,
        in_specs=[pl.BlockSpec(memory_space=pltpu.VMEM)] * 3,
        out_specs=(hbm, hbm, hbm),
        scratch_shapes=[pltpu.SemaphoreType.DMA((6,))],
        compiler_params=pltpu.CompilerParams(vmem_limit_bytes=52 << 20),
        name="hand_over",
    )(*made)


def solution(mesh):
    in_specs = (
        P(None, "freq", "tile", None),
        P(None, "freq", "tile", None),
        P("freq"),
        P("freq", "tile", None),
        P("freq", "tile", None),
        P("freq", "tile", None),
        P(),
        P(),
        P(),
        P(),
    )
    out_specs = (
        P(None, "freq", "tile", None),
        P(None, "freq", "tile", None),
        P(None, "tile", None),
    )
    return jax.shard_map(
        per_device, mesh=mesh, in_specs=in_specs, out_specs=out_specs, check_vma=False
    )
```
